32 devices in a mesh: groups: 2 (over y), dp: 4 (over z), feat: 2 (over x), test: 2 (over core).
Axes of the slice: x: 2, y: 2, z: 4, core: 2. Of those that a mesh axis runs over, the one named last changes fastest.
Arguments:
- train_inputs: bfloat16 [128, 96, 4096], P(('groups', 'dp', 'test'), None, 'feat'), parts along dimension 0, may hold values from -6 to 6
- train_grads: bfloat16 [128, 96, 14336], P(('groups', 'dp', 'test'), None, 'feat'), parts along dimension 0, may hold values from -6 to 6
- proj_in: bfloat16 [4096, 64], P('feat'), as said below
- proj_out: bfloat16 [14336, 64], P('feat'), as said below
- lengths: int32 [128], P(('groups', 'dp', 'test')), parts along dimension 0, may hold values from 24 to 96
- loss_mask: int32 [128, 96], P(('groups', 'dp', 'test')), parts along dimension 0, may hold values 0 or 1
- test_feats: bfloat16 [2048, 64, 64], P(('groups', 'dp', 'test'), 'feat'), parts along dimension 0, may hold values from -0.29882812 to 0.29882812
Outputs:
- scores: float32 [128, 8, 128], P(('groups', 'dp', 'test'), None, 'feat'), parts along dimension 0
The draws below stay inside these ranges and needn't reach their ends.
There are 2 independent parts, one for each index of `groups`. The reference program is written for one: setup_inputs(seed, part) draws one part's arguments, and reference() takes and returns one part's arrays. A program takes and returns all parts, laid end to end along the dimension named above; an argument that names none is the same for every part. Nothing has to cross between parts.
Inputs may be any that keep to these rules, and one draw needn't show every extreme that they name: `proj_in`: entries of order 4096 ** -0.5. `proj_out`: entries of order 14336 ** -0.5.
All inputs are finite; a program needn't handle non-finite values. No bound on the sum of `loss_mask` on one device may be relied on, other than what follows from the above.
Results may differ from the reference program's by a relative error of at most 0.0095.
Values may be sent and summed in bfloat16 or wider, within the bound.
No kernel may reach another device: no remote copies, remote signals or barrier semaphores. Data moves between devices by JAX's collectives and lax.ppermute only.
A program may use at most 64 MiB of HBM per device.

```python
import jax
import jax.numpy as jnp
from jax import lax

DIN = 4096
DOUT = 14336
RX = 64
RG = 64
LEN = 96
TE_DEV = 128
N_Q = 8
TRAIN = 64
TESTS = 1024


def row_scale(low):
    fraction = jnp.arange(TRAIN, dtype=jnp.float32) / max(TRAIN - 1, 1)
    return (low + fraction)[:, None, None]


def mixed_columns(own_values, shared, scale_key, fan_in, rank):
    scales = jnp.exp(jax.random.uniform(scale_key, (rank,), jnp.float32, jnp.log(0.5), jnp.log(3.0)))
    repeated = jnp.tile(shared, (1, rank // 8))
    return ((own_values + 0.8 * repeated) * scales[None, :] * (1.64 * fan_in) ** (-0.5)).astype(jnp.bfloat16)


def draw_train_inputs(key, part):
    key = jax.random.fold_in(key, 11)
    values = jax.random.truncated_normal(key, -4.0, 4.0, (TRAIN, LEN, DIN), jnp.float32) * row_scale(0.5)
    return values.astype(jnp.bfloat16)


def draw_train_grads(key, part):
    key = jax.random.fold_in(key, 12)
    values = jax.random.truncated_normal(key, -4.0, 4.0, (TRAIN, LEN, DOUT), jnp.float32) * row_scale(0.5)
    return values.astype(jnp.bfloat16)


def draw_proj_in(key, part):
    key = jax.random.fold_in(key, 21)
    own_key, common_key, scale_key = jax.random.split(key, 3)
    own_values = jax.random.truncated_normal(own_key, -4.0, 4.0, (DIN, RX), jnp.float32)
    shared = jax.random.truncated_normal(common_key, -4.0, 4.0, (DIN, 8), jnp.float32)
    return mixed_columns(own_values, shared, scale_key, DIN, RX)


def draw_proj_out(key, part):
    key = jax.random.fold_in(key, 22)
    own_key, common_key, scale_key = jax.random.split(key, 3)
    own_values = jax.random.truncated_normal(own_key, -4.0, 4.0, (DOUT, RG), jnp.float32)
    shared = jax.random.truncated_normal(common_key, -4.0, 4.0, (DOUT, 8), jnp.float32)
    return mixed_columns(own_values, shared, scale_key, DOUT, RG)


def touch_ends(values, key, smallest, top_value):
    dims = values.shape
    place = [jax.random.randint(jax.random.fold_in(key, axis), (), 0, dims[axis]) for axis in range(len(dims))]
    values = values.at[tuple(place)].set(smallest)
    longest = dims.index(max(dims))
    place[longest] = (place[longest] + 1) % dims[longest]
    return values.at[tuple(place)].set(top_value)


def shard_levels(rng, extent, shards, smallest, largest):
    gain, own = 1.0, jax.random.fold_in(rng, 6)
    for axis_at, blocks in shards:
        draws = jnp.exp(jax.random.uniform(jax.random.fold_in(own, axis_at), (blocks,), jnp.float32, smallest / len(shards), largest / len(shards)))
        gain = gain * jnp.repeat(draws, extent[axis_at] // blocks).reshape([-1 if axis == axis_at else 1 for axis in range(len(extent))])
    return gain


def gaussian(stream_key, extent, scale, reach, cuts=(), kind=jnp.bfloat16):
    values = scale * jax.random.normal(stream_key, extent, jnp.float32)
    if cuts:
        values = values * shard_levels(stream_key, extent, cuts, -0.22, 0.18)
    return jnp.clip(values, -reach, reach).astype(kind)


def setup_inputs(seed: int = 0, part: int = 0) -> dict:
    seeds = jax.random.split(jax.random.key(seed), 8)
    part_keys = jax.random.split(jax.random.fold_in(seeds[7], part), 8)
    train_inputs = draw_train_inputs(jax.random.fold_in(jax.random.fold_in(seeds[7], part), 71), part)
    train_grads = draw_train_grads(jax.random.fold_in(jax.random.fold_in(seeds[7], part), 71), part)
    proj_in = draw_proj_in(jax.random.fold_in(seeds[7], 71), part)
    proj_out = draw_proj_out(jax.random.fold_in(seeds[7], 71), part)
    lengths = touch_ends(jax.random.randint(part_keys[4], (TRAIN,), LEN // 4, LEN + 1), jax.random.fold_in(part_keys[4], 1), LEN // 4, LEN).astype(jnp.int32)
    loss_mask = touch_ends((jax.random.randint(part_keys[5], (TRAIN, LEN), 0, 4) < 3).astype(jnp.int32), jax.random.fold_in(part_keys[5], 1), 0, 1)
    test_feats = gaussian(part_keys[6], (TESTS, RG, RX), 0.05, 0.29882812, ((0, 8), (1, 2)))
    return {"train_inputs": train_inputs, "train_grads": train_grads, "proj_in": proj_in, "proj_out": proj_out, "lengths": lengths, "loss_mask": loss_mask, "test_feats": test_feats}


def damped_inverse(factor):
    order_size = factor.shape[0]
    identity = jnp.eye(order_size, dtype=jnp.float32)
    damped = factor + (0.1 * jnp.trace(factor) / order_size + 1e-06) * identity
    lower_factor = jnp.linalg.cholesky(damped)
    inverse_lower = lax.linalg.triangular_solve(lower_factor, identity, left_side=True, lower=True)
    return jnp.dot(inverse_lower.T, inverse_lower, precision=lax.Precision.HIGHEST)

def reference(train_inputs, train_grads, proj_in, proj_out, lengths, loss_mask, test_feats):
    tokens = TRAIN * LEN
    in_flat = jnp.dot(train_inputs.reshape(tokens, DIN).astype(jnp.float32), proj_in.astype(jnp.float32), preferred_element_type=jnp.float32).astype(jnp.bfloat16)
    grad_flat = jnp.dot(train_grads.reshape(tokens, DOUT).astype(jnp.float32), proj_out.astype(jnp.float32), preferred_element_type=jnp.float32).astype(jnp.bfloat16)
    positions = jnp.arange(LEN, dtype=jnp.int32)
    live_mask = ((loss_mask > 0) & (positions[None, :] < lengths[:, None])).astype(jnp.bfloat16)
    masked_in = (in_flat.reshape(TRAIN, LEN, RX) * live_mask[:, :, None]).reshape(tokens, RX)
    masked_grad = (grad_flat.reshape(TRAIN, LEN, RG) * live_mask[:, :, None]).reshape(tokens, RG)
    sums = jnp.einsum('etg,etx->egx', masked_grad.reshape(TRAIN, LEN, RG).astype(jnp.float32), in_flat.reshape(TRAIN, LEN, RX).astype(jnp.float32), precision=lax.Precision.HIGHEST)
    features = (sums / lengths.astype(jnp.float32)[:, None, None]).astype(jnp.bfloat16)
    in_factor = jnp.dot(masked_in.T.astype(jnp.float32), in_flat.astype(jnp.float32), preferred_element_type=jnp.float32) / float(tokens)
    grad_factor = jnp.dot(masked_grad.T.astype(jnp.float32), grad_flat.astype(jnp.float32), preferred_element_type=jnp.float32) / float(tokens)
    in_inverse = damped_inverse(in_factor)
    grad_inverse = damped_inverse(grad_factor)
    left_solved = jnp.einsum('gk,ekx->egx', grad_inverse, test_feats.astype(jnp.float32), precision=lax.Precision.HIGHEST)
    solved = jnp.einsum('egx,xy->egy', left_solved, in_inverse, precision=lax.Precision.HIGHEST).astype(jnp.bfloat16)
    scores = jnp.dot(features.reshape(TRAIN, RG * RX).astype(jnp.float32), solved.reshape(TESTS, RG * RX).T.astype(jnp.float32), preferred_element_type=jnp.float32)
    return scores.reshape(TRAIN, N_Q, TE_DEV)
```

```python
import functools

import jax
import jax.numpy as jnp
from jax import lax
from jax.experimental import pallas as pl
from jax.experimental.pallas import tpu as pltpu
from jax.sharding import PartitionSpec as P

f32 = jnp.float32
bf16 = jnp.bfloat16
VMEM_BYTES = 48 * 1024 * 1024


def xor_permute(values, axis, mask):
    size = lax.axis_size(axis)
    return lax.ppermute(values, axis, [(i, i ^ mask) for i in range(size)])


def chunk_of(width):
    for size in (1024, 512, 256, 128):
        if width % size == 0:
            return size
    return width


def project_body(start, rows, x_chunk, g_chunk, x_hbm, g_hbm, pin_hbm, pout_hbm, own_ref, sent_ref, x_buf, g_buf, pin_buf, pout_buf, sems):
    x_steps = x_buf.shape[0]
    g_steps = g_buf.shape[0]

    def copies(step):
        if step < x_steps:
            src, dst, wsrc, wdst, at, size = x_hbm, x_buf, pin_hbm, pin_buf, step, x_chunk
        else:
            src, dst, wsrc, wdst, at, size = g_hbm, g_buf, pout_hbm, pout_buf, step - x_steps, g_chunk
        return (
            pltpu.make_async_copy(wsrc.at[pl.ds(at * size, size), :], wdst.at[at], sems.at[0, step]),
            pltpu.make_async_copy(src.at[pl.ds(start, rows), pl.ds(at * size, size)], dst.at[at], sems.at[1, step]),
        )

    steps = x_steps + g_steps
    for step in range(steps):
        for copy in copies(step):
            copy.start()
    totals = []
    for first, last, buf, weights in ((0, x_steps, x_buf, pin_buf), (x_steps, steps, g_buf, pout_buf)):
        total = None
        for step in range(first, last):
            for copy in copies(step):
                copy.wait()
            term = jnp.dot(buf[step - first], weights[step - first], preferred_element_type=f32)
            total = term if total is None else total + term
        totals.append(total)
    both = jnp.concatenate(totals, axis=1)
    own_ref[...] = both
    sent_ref[...] = both.astype(bf16)


def project(x, g, pin, pout, start, rows):
    in_width, out_width = x.shape[1], g.shape[1]
    x_chunk, g_chunk = chunk_of(in_width), chunk_of(out_width)
    x_steps, g_steps = in_width // x_chunk, out_width // g_chunk
    rank = pin.shape[1]
    any_spec = pl.BlockSpec(memory_space=pl.ANY)
    return pl.pallas_call(
        functools.partial(project_body, start, rows, x_chunk, g_chunk),
        out_shape=(
            jax.ShapeDtypeStruct((rows, 2 * rank), f32),
            jax.ShapeDtypeStruct((rows, 2 * rank), bf16),
        ),
        in_specs=[any_spec] * 4,
        scratch_shapes=[
            pltpu.VMEM((x_steps, rows, x_chunk), bf16),
            pltpu.VMEM((g_steps, rows, g_chunk), bf16),
            pltpu.VMEM((x_steps, x_chunk, rank), bf16),
            pltpu.VMEM((g_steps, g_chunk, rank), bf16),
            pltpu.SemaphoreType.DMA((2, x_steps + g_steps)),
        ],
        compiler_params=pltpu.CompilerParams(vmem_limit_bytes=VMEM_BYTES),
        cost_estimate=pl.CostEstimate(
            flops=2 * rows * (in_width + out_width) * rank,
            bytes_accessed=2 * (rows + rank) * (in_width + out_width),
            transcendentals=0,
        ),
        name="project",
    )(x, g, pin, pout)


def gram_body(first, count, received, lengths_ref, mask_ref, own_ref, *refs):
    received_refs = refs[:received]
    gram_ref, feats_ref = refs[received:]
    seq_len = mask_ref.shape[1]
    rank = gram_ref.shape[0]
    positions = lax.broadcasted_iota(jnp.int32, (1, seq_len), 1)
    total = None
    feats = []
    for local in range(count):
        rows = pl.ds(local * seq_len, seq_len)
        summed = own_ref[rows, :]
        for ref in received_refs:
            summed = summed + ref[rows, :].astype(f32)
        rounded = summed.astype(bf16)
        length = lengths_ref[first + local]
        live = (mask_ref[first + local : first + local + 1, :] > 0) & (positions < length)
        turned = jnp.where(live, rounded.astype(f32).T, 0.0).astype(bf16)
        products = jnp.dot(turned, rounded, preferred_element_type=f32)
        total = products if total is None else total + products
        feats.append(products[rank:, :] / length.astype(f32))
    lane = lax.broadcasted_iota(jnp.int32, (rank, 2 * rank), 1)
    gram_ref[...] = jnp.where(lane < rank, total[:rank, :], total[rank:, :])
    half = count // 2
    for pair in range(half):
        other = pltpu.roll(feats[half + pair], rank, 1)
        feats_ref[pair] = jnp.where(lane < rank, feats[pair], other).astype(bf16)


def gram(lengths, mask, own, received, first, count):
    rank = own.shape[1] // 2
    vmem = pl.BlockSpec(memory_space=pltpu.VMEM)
    return pl.pallas_call(
        functools.partial(gram_body, first, count, len(received)),
        out_shape=(
            jax.ShapeDtypeStruct((rank, 2 * rank), f32),
            jax.ShapeDtypeStruct((count // 2, rank, 2 * rank), bf16),
        ),
        in_specs=[pl.BlockSpec(memory_space=pltpu.SMEM), vmem, vmem] + [vmem] * len(received),
        name="gram",
    )(lengths, mask, own, *received)


def flatten_body(tests_ref, out_ref, wide):
    count, rows, width = tests_ref.shape
    wide[...] = tests_ref[...].reshape(count * rows, width).astype(f32)
    for pair in range(rows // 2):
        low = wide[pl.ds(2 * pair, count, stride=rows), :]
        high = wide[pl.ds(2 * pair + 1, count, stride=rows), :]
        out_ref[:, 2 * width * pair : 2 * width * (pair + 1)] = jnp.concatenate([low, high], axis=1).astype(bf16)


def flatten(tests):
    count, rows, width = tests.shape
    vmem = pl.BlockSpec(memory_space=pltpu.VMEM)
    return pl.pallas_call(
        flatten_body,
        out_shape=jax.ShapeDtypeStruct((count, rows * width), bf16),
        in_specs=[vmem],
        out_specs=vmem,
        scratch_shapes=[pltpu.VMEM((count * rows, width), f32)],
        name="flatten",
    )(tests)


def both_inverses(total_tokens, packed):
    rank = packed.shape[0]
    lane = lax.broadcasted_iota(jnp.int32, (rank, 2 * rank), 1)
    sub = lax.broadcasted_iota(jnp.int32, (rank, 2 * rank), 0)
    left = lane < rank
    column = jnp.where(left, lane, lane - rank)
    diagonal = column == sub
    packed = packed / total_tokens
    on_diagonal = jnp.sum(jnp.where(diagonal, packed, 0.0), axis=0, keepdims=True)
    trace_in = jnp.sum(jnp.where(left[:1], on_diagonal, 0.0), axis=1, keepdims=True)
    trace_grad = jnp.sum(jnp.where(left[:1], 0.0, on_diagonal), axis=1, keepdims=True)
    damping = 0.1 * jnp.where(left[:1], trace_in, trace_grad) / rank + 1e-06
    packed = packed + jnp.where(diagonal, damping, 0.0)
    for k in range(rank):
        pivot_column = jnp.where(left, packed[:, k : k + 1], packed[:, rank + k : rank + k + 1])
        row = packed[k : k + 1, :]
        inverse = 1.0 / pivot_column[k : k + 1, :]
        at_pivot = column[:1] == k
        row = jnp.where(at_pivot, inverse, row * inverse)
        packed = jnp.where(sub == k, row, jnp.where(at_pivot, 0.0, packed) - pivot_column * row)
    return packed


def split(values):
    high = values.astype(bf16)
    return high, (values - high.astype(f32)).astype(bf16)


def product(left, right):
    left_high, left_low = split(left)
    right_high, right_low = split(right)
    dot = functools.partial(jnp.dot, preferred_element_type=f32)
    return dot(left_high, right_high) + dot(left_high, right_low) + dot(left_low, right_high)


def scores_body(total_tokens, blocks, chunks, gram_a_ref, gram_b_ref, tests_ref, *refs):
    feats_refs, (out_ref, inverse_buf, turned_buf, line_buf) = refs[:-4], refs[-4:]
    feat = lax.axis_index("feat")
    test = lax.axis_index("test")
    dp = lax.axis_index("dp")
    feat_count = lax.axis_size("feat")
    test_count = lax.axis_size("test")
    rank = gram_a_ref.shape[0]
    own_rows = rank // feat_count
    inverses = both_inverses(total_tokens, gram_a_ref[...] + gram_b_ref[...])
    inverse_buf[...] = pltpu.roll(inverses, rank, 1)
    grad_rows = inverse_buf[pl.ds(pl.multiple_of(feat * own_rows, 8), own_rows), :][:, :rank]
    in_inverse = inverses[:, :rank]
    zero = jnp.zeros_like(in_inverse)
    in_pair = jnp.concatenate(
        [jnp.concatenate([in_inverse, zero], axis=1), jnp.concatenate([zero, in_inverse], axis=1)], axis=0
    )
    grad_high, grad_low = split(grad_rows)
    in_high, in_low = split(in_pair)
    pairs = [ref[i] for ref in feats_refs for i in range(ref.shape[0])]
    count = len(pairs)
    for at in range(count):
        solved = jnp.dot(grad_high, pairs[at], preferred_element_type=f32) + jnp.dot(
            grad_low, pairs[at], preferred_element_type=f32
        )
        high, low = split(solved)
        turned_buf[at * own_rows : (at + 1) * own_rows, :] = (
            jnp.dot(high, in_high, preferred_element_type=f32)
            + jnp.dot(high, in_low, preferred_element_type=f32)
            + jnp.dot(low, in_high, preferred_element_type=f32)
        )
    lane = lax.broadcasted_iota(jnp.int32, (count, 2 * rank), 1)
    for g in range(0, own_rows, 2):
        low = turned_buf[pl.ds(g, count, stride=own_rows), :]
        high = turned_buf[pl.ds(g + 1, count, stride=own_rows), :]
        first = jnp.where(lane < rank, low, pltpu.roll(high, rank, 1))
        second = jnp.where(lane < rank, pltpu.roll(low, rank, 1), high)
        line_buf[:, g * rank : (g + 2) * rank] = jnp.concatenate([first, second], axis=0).astype(bf16)
    lines = line_buf[...]
    test_block = tests_ref.shape[0] // feat_count
    half = count // len(blocks)
    run = half // chunks
    for target in range(feat_count):
        part = lax.dot_general(
            lines,
            tests_ref[target * test_block : (target + 1) * test_block, :],
            (((1,), (1,)), ((), ())),
            preferred_element_type=f32,
        )
        for at, (dp_mask, test_mask) in enumerate(blocks):
            place = ((dp ^ dp_mask) * feat_count + target) * test_count + (test ^ test_mask)
            for chunk in range(chunks):
                begin = at * half + chunk * run
                for second in range(2):
                    to = (2 * chunk + second) * run
                    out_ref[place, to : to + run, :] = part[second * count + begin : second * count + begin + run, :]


def partial_scores(total_tokens, blocks, chunks, gram_a, gram_b, tests, feats, examples):
    rank = gram_a.shape[0]
    feat_count = lax.axis_size("feat")
    own_rows = rank // feat_count
    count = sum(f.shape[0] for f in feats)
    vmem = pl.BlockSpec(memory_space=pltpu.VMEM)
    return pl.pallas_call(
        functools.partial(scores_body, total_tokens, blocks, chunks),
        out_shape=jax.ShapeDtypeStruct((len(blocks) * feat_count, examples, tests.shape[0] // feat_count), f32),
        in_specs=[vmem] * (3 + len(feats)),
        out_specs=vmem,
        scratch_shapes=[
            pltpu.VMEM((rank, 2 * rank), f32),
            pltpu.VMEM((count * own_rows, 2 * rank), f32),
            pltpu.VMEM((2 * count, own_rows * rank), bf16),
        ],
        compiler_params=pltpu.CompilerParams(vmem_limit_bytes=VMEM_BYTES),
        name="scores",
    )(gram_a, gram_b, tests, *feats)


def masks_of(size):
    masks, mask = [], 1
    while mask < size:
        masks.append(mask)
        mask *= 2
    return masks


def on_device(train_inputs, train_grads, proj_in, proj_out, lengths, loss_mask, test_feats):
    examples, seq_len, in_width = train_inputs.shape
    out_width = train_grads.shape[2]
    tokens = examples * seq_len
    feat_count = lax.axis_size("feat")
    dp_count = lax.axis_size("dp")
    test_count = lax.axis_size("test")
    x = train_inputs.reshape(tokens, in_width)
    g = train_grads.reshape(tokens, out_width)
    part = examples // 2
    owns, gots = [], []
    for first in (0, part):
        own, sent = project(x, g, proj_in, proj_out, first * seq_len, part * seq_len)
        owns.append(own)
        gots.append([xor_permute(sent, "feat", mask) for mask in range(1, feat_count)])
    tests = flatten(test_feats)
    grams, feats = [], []
    for at, first in enumerate((0, part)):
        share, features = gram(lengths, loss_mask, owns[at], gots[at], first, part)
        grams.append(share)
        feats.append(features)
    factor = grams[0] + grams[1]
    features = jnp.concatenate(feats, axis=0)
    steps = [("test", m) for m in masks_of(test_count)] + [("dp", m) for m in masks_of(dp_count)]
    for at, (axis, mask) in enumerate(steps):
        other = xor_permute(factor, axis, mask)
        if at < len(steps) - 1:
            factor = factor + other
    blocks = [(0, 0)]
    for axis, mask in reversed(steps):
        features = jnp.concatenate([features, xor_permute(features, axis, mask)], axis=0)
        blocks = blocks + [(d ^ mask, t) if axis == "dp" else (d, t ^ mask) for d, t in blocks]
    total_tokens = float(tokens * dp_count * test_count)
    shares = partial_scores(total_tokens, blocks, 2, factor, other, tests, [features], examples)
    arrived = lax.all_to_all(shares, ("dp", "feat", "test"), split_axis=0, concat_axis=0)
    arrived = arrived.reshape((dp_count, feat_count, test_count) + arrived.shape[1:])
    scores = jnp.sum(arrived, axis=1)
    return scores.reshape((dp_count * test_count,) + scores.shape[2:]).transpose(1, 0, 2)


def solution(mesh):
    return jax.shard_map(
        on_device,
        mesh=mesh,
        in_specs=(
            P(("groups", "dp", "test"), None, "feat"),
            P(("groups", "dp", "test"), None, "feat"),
            P("feat", None),
            P("feat", None),
            P(("groups", "dp", "test")),
            P(("groups", "dp", "test"), None),
            P(("groups", "dp", "test"), "feat", None),
        ),
        out_specs=P(("groups", "dp", "test"), None, "feat"),
        check_vma=False,
    )
```

```python
import functools

import jax
import jax.numpy as jnp
from jax import lax
from jax.experimental import pallas as pl
from jax.experimental.pallas import tpu as pltpu
from jax.sharding import PartitionSpec as P

f32 = jnp.float32
bf16 = jnp.bfloat16
MIB = 1024 * 1024
NT = (((1,), (1,)), ((), ()))
VMEM = pl.BlockSpec(memory_space=pltpu.VMEM)
SMEM = pl.BlockSpec(memory_space=pltpu.SMEM)
ANY = pl.BlockSpec(memory_space=pl.ANY)


def xor_permute(values, axis, mask):
    size = lax.axis_size(axis)
    return lax.ppermute(values, axis, [(i, i ^ mask) for i in range(size)])


def masks_of(size):
    masks, mask = [], 1
    while mask < size:
        masks.append(mask)
        mask *= 2
    return masks


def project_body(rows, x_hbm, g_hbm, pin_hbm, pout_hbm, own_ref, sent_ref, x_buf, g_buf, pin_buf, pout_buf, sems):
    steps = x_hbm.shape[0] // rows
    rank = pin_hbm.shape[0]
    pin_copy = pltpu.make_async_copy(pin_hbm, pin_buf, sems.at[0])
    x_copy = pltpu.make_async_copy(x_hbm, x_buf, sems.at[1])
    pout_copy = pltpu.make_async_copy(pout_hbm, pout_buf, sems.at[2])

    def g_copy(step):
        begin = step * rows if isinstance(step, int) else pl.multiple_of(step * rows, rows)
        block = pl.ds(begin, rows)
        return pltpu.make_async_copy(g_hbm.at[block, :], g_buf.at[block, :], sems.at[3 + step])

    pin_copy.start()
    x_copy.start()
    pout_copy.start()
    for step in range(steps):
        g_copy(step).start()
    pin_copy.wait()
    x_copy.wait()
    own_ref[:, :rank] = lax.dot_general(x_buf[...], pin_buf[...], NT, preferred_element_type=f32)
    pout_copy.wait()

    @pl.loop(0, steps)
    def _(step):
        g_copy(step).wait()
        block = pl.ds(pl.multiple_of(step * rows, rows), rows)
        right = lax.dot_general(g_buf[block, :], pout_buf[...], NT, preferred_element_type=f32)
        both = jnp.concatenate([own_ref[block, :rank], right], axis=1)
        own_ref[block, :] = both
        sent_ref[block, :] = both.astype(bf16)


def project(x, g, pin, pout, rows):
    tokens, in_width = x.shape
    out_width = g.shape[1]
    rank = pin.shape[0]
    return pl.pallas_call(
        functools.partial(project_body, rows),
        out_shape=(
            jax.ShapeDtypeStruct((tokens, 2 * rank), f32),
            jax.ShapeDtypeStruct((tokens, 2 * rank), bf16),
        ),
        in_specs=[ANY] * 4,
        out_specs=(VMEM, VMEM),
        scratch_shapes=[
            pltpu.VMEM(x.shape, bf16),
            pltpu.VMEM(g.shape, bf16),
            pltpu.VMEM(pin.shape, bf16),
            pltpu.VMEM(pout.shape, bf16),
            pltpu.SemaphoreType.DMA((3 + tokens // rows,)),
        ],
        compiler_params=pltpu.CompilerParams(vmem_limit_bytes=60 * MIB),
        cost_estimate=pl.CostEstimate(
            flops=2 * tokens * (in_width + out_width) * rank,
            bytes_accessed=2 * (tokens + rank) * (in_width + out_width),
            transcendentals=0,
        ),
        name="project",
    )(x, g, pin, pout)


def factors_body(received, lengths_ref, mask_ref, own_ref, *refs):
    received_refs = refs[:received]
    factor_ref, rounded_ref, turned_ref = refs[received:]
    examples, seq_len = mask_ref.shape
    rank = factor_ref.shape[0]
    positions = lax.broadcasted_iota(jnp.int32, (1, seq_len), 1)
    total = None
    for example in range(examples):
        rows = pl.ds(example * seq_len, seq_len)
        summed = own_ref[rows, :]
        for ref in received_refs:
            summed = summed + ref[rows, :].astype(f32)
        rounded = summed.astype(bf16)
        rounded_ref[rows, :] = rounded
        live = (mask_ref[example : example + 1, :] > 0) & (positions < lengths_ref[example])
        turned = jnp.where(live, rounded.astype(f32).T, 0.0).astype(bf16)
        turned_ref[example] = turned
        products = jnp.dot(turned, rounded, preferred_element_type=f32)
        total = products if total is None else total + products
    lane = lax.broadcasted_iota(jnp.int32, (rank, 2 * rank), 1)
    factor_ref[...] = jnp.where(lane < rank, total[:rank, :], total[rank:, :])


def factors(lengths, mask, own, received):
    tokens, width = own.shape
    examples, seq_len = mask.shape
    return pl.pallas_call(
        functools.partial(factors_body, len(received)),
        out_shape=(
            jax.ShapeDtypeStruct((width // 2, width), f32),
            jax.ShapeDtypeStruct((tokens, width), bf16),
            jax.ShapeDtypeStruct((examples, width, seq_len), bf16),
        ),
        in_specs=[SMEM, VMEM, VMEM] + [VMEM] * len(received),
        out_specs=(VMEM, VMEM, VMEM),
        compiler_params=pltpu.CompilerParams(vmem_limit_bytes=4 * MIB),
        name="factors",
    )(lengths, mask, own, *received)


def features_body(lengths_ref, rounded_ref, turned_ref, feats_ref):
    half, rank, _ = feats_ref.shape
    examples, _, seq_len = turned_ref.shape
    lane = lax.broadcasted_iota(jnp.int32, (rank, 2 * rank), 1)

    def features(example):
        products = jnp.dot(
            turned_ref[example, rank:, :], rounded_ref[pl.ds(example * seq_len, seq_len), :], preferred_element_type=f32
        )
        return products / lengths_ref[example].astype(f32)

    for pair in range(half):
        other = pltpu.roll(features(half + pair), rank, 1)
        feats_ref[pair] = jnp.where(lane < rank, features(pair), other).astype(bf16)


def features_of(lengths, rounded, turned):
    examples, width, seq_len = turned.shape
    return pl.pallas_call(
        features_body,
        out_shape=jax.ShapeDtypeStruct((examples // 2, width // 2, width), bf16),
        in_specs=[SMEM, VMEM, VMEM],
        out_specs=VMEM,
        compiler_params=pltpu.CompilerParams(vmem_limit_bytes=4 * MIB),
        cost_estimate=pl.CostEstimate(flops=2 * examples * seq_len * width * width, bytes_accessed=8 * MIB, transcendentals=0),
        name="features",
    )(lengths, rounded, turned)


def split(values):
    high = values.astype(bf16)
    return high, (values - high.astype(f32)).astype(bf16)


def inverses_body(total_tokens, factor_a_ref, factor_b_ref, grad_ref, in_ref, inverse_buf):
    rank = factor_a_ref.shape[0]
    own_rows = grad_ref.shape[1]
    lane = lax.broadcasted_iota(jnp.int32, (rank, 2 * rank), 1)
    sub = lax.broadcasted_iota(jnp.int32, (rank, 2 * rank), 0)
    left = lane < rank
    column = jnp.where(left, lane, lane - rank)
    diagonal = column == sub
    packed = (factor_a_ref[...] + factor_b_ref[...]) / total_tokens
    on_diagonal = jnp.sum(jnp.where(diagonal, packed, 0.0), axis=0, keepdims=True)
    trace_in = jnp.sum(jnp.where(left[:1], on_diagonal, 0.0), axis=1, keepdims=True)
    trace_grad = jnp.sum(jnp.where(left[:1], 0.0, on_diagonal), axis=1, keepdims=True)
    damping = 0.1 * jnp.where(left[:1], trace_in, trace_grad) / rank + 1e-06
    packed = packed + jnp.where(diagonal, damping, 0.0)
    for k in range(rank):
        pivot_column = jnp.where(left, packed[:, k : k + 1], packed[:, rank + k : rank + k + 1])
        row = packed[k : k + 1, :]
        inverse = 1.0 / pivot_column[k : k + 1, :]
        at_pivot = column[:1] == k
        row = jnp.where(at_pivot, inverse, row * inverse)
        packed = jnp.where(sub == k, row, jnp.where(at_pivot, 0.0, packed) - pivot_column * row)
    inverse_buf[...] = pltpu.roll(packed, rank, 1)
    first_row = pl.multiple_of(lax.axis_index("feat") * own_rows, 8)
    grad_ref[0], grad_ref[1] = split(inverse_buf[pl.ds(first_row, own_rows), :][:, :rank])
    twice = pltpu.roll(packed, rank, 1)
    in_ref[0, :rank, :], in_ref[1, :rank, :] = split(jnp.where(left, packed, 0.0))
    in_ref[0, rank:, :], in_ref[1, rank:, :] = split(jnp.where(left, 0.0, twice))


def inverses(total_tokens, factor_a, factor_b, own_rows):
    rank, width = factor_a.shape
    return pl.pallas_call(
        functools.partial(inverses_body, total_tokens),
        out_shape=(
            jax.ShapeDtypeStruct((2, own_rows, rank), bf16),
            jax.ShapeDtypeStruct((2, width, width), bf16),
        ),
        in_specs=[VMEM, VMEM],
        out_specs=(VMEM, VMEM),
        scratch_shapes=[pltpu.VMEM((rank, width), f32)],
        compiler_params=pltpu.CompilerParams(vmem_limit_bytes=4 * MIB),
        cost_estimate=pl.CostEstimate(flops=4 * MIB, bytes_accessed=16 * MIB, transcendentals=0),
        name="inverses",
    )(factor_a, factor_b)


def scores_body(dp_masks, grad_ref, in_ref, own_tests_ref, other_tests_ref, *refs):
    feats_refs, (out_ref, solved_buf, line_buf) = refs[:-3], refs[-3:]
    feat_count = lax.axis_size("feat")
    dp = lax.axis_index("dp")
    own_rows, rank = grad_ref.shape[1:]
    pairs = [ref[i] for ref in feats_refs for i in range(ref.shape[0])]
    count = len(pairs)
    half = count // len(dp_masks)
    dot = functools.partial(jnp.dot, preferred_element_type=f32)
    for at in range(count):
        high, low = split(dot(grad_ref[0], pairs[at]) + dot(grad_ref[1], pairs[at]))
        solved_buf[at * own_rows : (at + 1) * own_rows, :] = dot(high, in_ref[0]) + dot(high, in_ref[1]) + dot(low, in_ref[0])
    lane = lax.broadcasted_iota(jnp.int32, (count, 2 * rank), 1)
    for g in range(0, own_rows, 2):
        low = solved_buf[pl.ds(g, count, stride=own_rows), :]
        high = solved_buf[pl.ds(g + 1, count, stride=own_rows), :]
        first = jnp.where(lane < rank, low, pltpu.roll(high, rank, 1))
        second = jnp.where(lane < rank, pltpu.roll(low, rank, 1), high)
        line_buf[:, g * rank : (g + 2) * rank] = jnp.concatenate([first, second], axis=0).astype(bf16)
    lines = line_buf[...]
    own = dot(lines, own_tests_ref[...])
    other = dot(lines, other_tests_ref[...])
    is_first = lax.axis_index("test") == 0
    parts = (jnp.where(is_first, own, other), jnp.where(is_first, other, own))
    block = own.shape[1] // feat_count
    for target in range(feat_count):
        columns = slice(target * block, (target + 1) * block)
        both = jnp.concatenate([part[:, columns] for part in parts], axis=1)
        for at, mask in enumerate(dp_masks):
            place = (dp ^ mask) * feat_count + target
            out_ref[place, :half, :] = both[at * half : (at + 1) * half, :]
            out_ref[place, half:, :] = both[count + at * half : count + (at + 1) * half, :]


def partial_scores(dp_masks, grad, in_pair, own_tests, other_tests, feats):
    feat_count = lax.axis_size("feat")
    own_rows, rank = grad.shape[1:]
    count = sum(f.shape[0] for f in feats)
    rows = 2 * count // len(dp_masks)
    return pl.pallas_call(
        functools.partial(scores_body, dp_masks),
        out_shape=jax.ShapeDtypeStruct((len(dp_masks) * feat_count, rows, 2 * own_tests.shape[1] // feat_count), f32),
        in_specs=[VMEM] * (4 + len(feats)),
        out_specs=VMEM,
        scratch_shapes=[
            pltpu.VMEM((count * own_rows, 2 * rank), f32),
            pltpu.VMEM((2 * count, own_rows * rank), bf16),
        ],
        compiler_params=pltpu.CompilerParams(vmem_limit_bytes=16 * MIB),
        name="scores",
    )(grad, in_pair, own_tests, other_tests, *feats)


def finish_body(feat_count, arrived_ref, out_ref):
    blocks, examples, width = arrived_ref.shape
    dp_count = blocks // feat_count
    half = width // 2
    for dp in range(dp_count):
        total = arrived_ref[dp * feat_count]
        for feat in range(1, feat_count):
            total = total + arrived_ref[dp * feat_count + feat]
        for test in range(2):
            out_ref[pl.ds(2 * dp + test, examples, stride=2 * dp_count), :] = total[:, test * half : (test + 1) * half]


def finish(arrived, feat_count):
    blocks, examples, width = arrived.shape
    queries = 2 * blocks // feat_count
    out = pl.pallas_call(
        functools.partial(finish_body, feat_count),
        out_shape=jax.ShapeDtypeStruct((examples * queries, width // 2), f32),
        in_specs=[VMEM],
        out_specs=VMEM,
        compiler_params=pltpu.CompilerParams(vmem_limit_bytes=4 * MIB),
        name="finish",
    )(arrived)
    return out.reshape(examples, queries, width // 2)


def on_device(train_inputs, train_grads, proj_in, proj_out, lengths, loss_mask, test_feats):
    examples, seq_len, in_width = train_inputs.shape
    out_width = train_grads.shape[2]
    tokens = examples * seq_len
    feat_count = lax.axis_size("feat")
    dp_count = lax.axis_size("dp")
    test_count = lax.axis_size("test")
    own_rows = test_feats.shape[1]
    x = train_inputs.reshape(tokens, in_width)
    g = train_grads.reshape(tokens, out_width)
    own, sent = project(x, g, proj_in.T, proj_out.T, tokens // 3)
    received = [xor_permute(sent, "feat", mask) for mask in range(1, feat_count)]
    own_tests = test_feats.transpose(1, 2, 0).reshape(own_rows * test_feats.shape[2], test_feats.shape[0])
    other_tests = xor_permute(own_tests, "test", 1)
    factor, rounded, turned = factors(lengths, loss_mask, own, received)
    feats = [features_of(lengths, rounded, turned)]
    dp_masks = [0]
    steps = [("dp", m) for m in reversed(masks_of(dp_count))]
    steps = steps[:-1] + [("test", 1)] + steps[-1:]
    for at, (axis, mask) in enumerate(steps):
        other = xor_permute(factor, axis, mask)
        if at < len(steps) - 1:
            factor = factor + other
        if axis == "dp":
            moved = feats[0] if len(feats) == 1 else jnp.concatenate(feats, axis=0)
            feats = feats + [xor_permute(moved, axis, mask)]
            dp_masks = dp_masks + [d ^ mask for d in dp_masks]
    total_tokens = float(tokens * dp_count * test_count)
    grad, in_pair = inverses(total_tokens, factor, other, own_rows)
    shares = partial_scores(dp_masks, grad, in_pair, own_tests, other_tests, feats)
    arrived = lax.all_to_all(shares, ("dp", "feat"), split_axis=0, concat_axis=0)
    return finish(arrived, feat_count)


def solution(mesh):
    return jax.shard_map(
        on_device,
        mesh=mesh,
        in_specs=(
            P(("groups", "dp", "test"), None, "feat"),
            P(("groups", "dp", "test"), None, "feat"),
            P("feat", None),
            P("feat", None),
            P(("groups", "dp", "test")),
            P(("groups", "dp", "test"), None),
            P(("groups", "dp", "test"), "feat", None),
        ),
        out_specs=P(("groups", "dp", "test"), None, "feat"),
        check_vma=False,
    )
```

```python
import functools

import jax
import jax.numpy as jnp
from jax import lax
from jax.experimental import pallas as pl
from jax.experimental.pallas import tpu as pltpu
from jax.sharding import PartitionSpec as P

f32 = jnp.float32
bf16 = jnp.bfloat16
MIB = 1024 * 1024
NT = (((1,), (1,)), ((), ()))
VMEM = pl.BlockSpec(memory_space=pltpu.VMEM)
SMEM = pl.BlockSpec(memory_space=pltpu.SMEM)
HBM = pl.BlockSpec(memory_space=pltpu.HBM)


def xor_permute(values, axis, mask):
    size = lax.axis_size(axis)
    return lax.ppermute(values, axis, [(i, i ^ mask) for i in range(size)])


def masks_of(size):
    masks, mask = [], 1
    while mask < size:
        masks.append(mask)
        mask *= 2
    return masks


def project_body(rows, x_hbm, g_hbm, pin_hbm, pout_hbm, own_ref, sent_ref, x_buf, g_buf, pin_buf, pout_buf, sems):
    steps = x_hbm.shape[0] // rows
    rank = pin_hbm.shape[0]
    pin_copy = pltpu.make_async_copy(pin_hbm, pin_buf, sems.at[0])
    x_copy = pltpu.make_async_copy(x_hbm, x_buf, sems.at[1])
    pout_copy = pltpu.make_async_copy(pout_hbm, pout_buf, sems.at[2])

    def g_copy(step):
        begin = step * rows if isinstance(step, int) else pl.multiple_of(step * rows, rows)
        block = pl.ds(begin, rows)
        return pltpu.make_async_copy(g_hbm.at[block, :], g_buf.at[block, :], sems.at[3 + step])

    pin_copy.start()
    x_copy.start()
    pout_copy.start()
    for step in range(steps):
        g_copy(step).start()
    pin_copy.wait()
    x_copy.wait()
    own_ref[:, :rank] = lax.dot_general(x_buf[...], pin_buf[...], NT, preferred_element_type=f32)
    pout_copy.wait()

    @pl.loop(0, steps)
    def _(step):
        g_copy(step).wait()
        block = pl.ds(pl.multiple_of(step * rows, rows), rows)
        right = lax.dot_general(g_buf[block, :], pout_buf[...], NT, preferred_element_type=f32)
        both = jnp.concatenate([own_ref[block, :rank], right], axis=1)
        own_ref[block, :] = both
        sent_ref[block, :] = both.astype(bf16)


def project(x, g, pin, pout, rows):
    tokens, in_width = x.shape
    out_width = g.shape[1]
    rank = pin.shape[0]
    return pl.pallas_call(
        functools.partial(project_body, rows),
        out_shape=(
            jax.ShapeDtypeStruct((tokens, 2 * rank), f32),
            jax.ShapeDtypeStruct((tokens, 2 * rank), bf16),
        ),
        in_specs=[HBM] * 4,
        out_specs=(VMEM, VMEM),
        scratch_shapes=[
            pltpu.VMEM(x.shape, bf16),
            pltpu.VMEM(g.shape, bf16),
            pltpu.VMEM(pin.shape, bf16),
            pltpu.VMEM(pout.shape, bf16),
            pltpu.SemaphoreType.DMA((3 + tokens // rows,)),
        ],
        compiler_params=pltpu.CompilerParams(vmem_limit_bytes=60 * MIB),
        cost_estimate=pl.CostEstimate(
            flops=2 * tokens * (in_width + out_width) * rank,
            bytes_accessed=2 * (tokens + rank) * (in_width + out_width),
            transcendentals=0,
        ),
        name="project",
    )(x, g, pin, pout)


def factors_body(received, lengths_ref, mask_ref, own_ref, *refs):
    received_refs = refs[:received]
    factor_ref, rounded_ref, turned_ref = refs[received:]
    examples, seq_len = mask_ref.shape
    rank = factor_ref.shape[0]
    positions = lax.broadcasted_iota(jnp.int32, (1, seq_len), 1)
    total = None
    for example in range(examples):
        rows = pl.ds(example * seq_len, seq_len)
        summed = own_ref[rows, :]
        for ref in received_refs:
            summed = summed + ref[rows, :].astype(f32)
        rounded = summed.astype(bf16)
        rounded_ref[rows, :] = rounded
        live = (mask_ref[example : example + 1, :] > 0) & (positions < lengths_ref[example])
        turned = jnp.where(live, rounded.astype(f32).T, 0.0).astype(bf16)
        turned_ref[example] = turned
        products = jnp.dot(turned, rounded, preferred_element_type=f32)
        total = products if total is None else total + products
    lane = lax.broadcasted_iota(jnp.int32, (rank, 2 * rank), 1)
    factor_ref[...] = jnp.where(lane < rank, total[:rank, :], total[rank:, :])


def factors(lengths, mask, own, received):
    tokens, width = own.shape
    examples, seq_len = mask.shape
    return pl.pallas_call(
        functools.partial(factors_body, len(received)),
        out_shape=(
            jax.ShapeDtypeStruct((width // 2, width), f32),
            jax.ShapeDtypeStruct((tokens, width), bf16),
            jax.ShapeDtypeStruct((examples, width, seq_len), bf16),
        ),
        in_specs=[SMEM, VMEM, VMEM] + [VMEM] * len(received),
        out_specs=(VMEM, VMEM, VMEM),
        compiler_params=pltpu.CompilerParams(vmem_limit_bytes=4 * MIB),
        name="factors",
    )(lengths, mask, own, *received)


def features_body(lengths_ref, rounded_ref, turned_ref, feats_ref):
    half, rank, _ = feats_ref.shape
    examples, _, seq_len = turned_ref.shape
    lane = lax.broadcasted_iota(jnp.int32, (rank, 2 * rank), 1)

    def features(example):
        products = jnp.dot(
            turned_ref[example, rank:, :], rounded_ref[pl.ds(example * seq_len, seq_len), :], preferred_element_type=f32
        )
        return products / lengths_ref[example].astype(f32)

    for pair in range(half):
        other = pltpu.roll(features(half + pair), rank, 1)
        feats_ref[pair] = jnp.where(lane < rank, features(pair), other).astype(bf16)


def features_of(lengths, rounded, turned):
    examples, width, seq_len = turned.shape
    return pl.pallas_call(
        features_body,
        out_shape=jax.ShapeDtypeStruct((examples // 2, width // 2, width), bf16),
        in_specs=[SMEM, VMEM, VMEM],
        out_specs=VMEM,
        compiler_params=pltpu.CompilerParams(vmem_limit_bytes=4 * MIB),
        cost_estimate=pl.CostEstimate(flops=2 * examples * seq_len * width * width, bytes_accessed=8 * MIB, transcendentals=0),
        name="features",
    )(lengths, rounded, turned)


def split(values):
    high = values.astype(bf16)
    return high, (values - high.astype(f32)).astype(bf16)


def invert(packed):
    rank, width = packed.shape
    run = 8
    blocks = [packed[run * r : run * (r + 1), :] for r in range(rank // run)]
    lane = lax.broadcasted_iota(jnp.int32, (run, width), 1)
    sub = lax.broadcasted_iota(jnp.int32, (run, width), 0)
    column = jnp.where(lane < rank, lane, lane - rank)
    base = jnp.where(lane < rank, 0, rank)

    def pick(values, at):
        return jnp.take_along_axis(values, base + at, axis=1)

    for p in range(len(blocks)):
        first = run * p
        rows = [jnp.broadcast_to(blocks[p][i : i + 1, :], (run, width)) for i in range(run)]
        entry = [[None] * run for _ in range(run)]
        for i in range(run):
            for j in range(i, run):
                entry[i][j] = entry[j][i] = pick(rows[i], first + j)
        columns = [[pick(block, first + j) for j in range(run)] for block in blocks]
        for j in range(0, run, 2):
            a, b, c = entry[j][j], entry[j][j + 1], entry[j + 1][j + 1]
            scale = 1.0 / (a * c - b * b)
            ia, ib, ic = c * scale, -(b * scale), a * scale
            at_first, at_second = column == first + j, column == first + j + 1
            low = jnp.where(at_first, ia, jnp.where(at_second, ib, ia * rows[j] + ib * rows[j + 1]))
            high = jnp.where(at_first, ib, jnp.where(at_second, ic, ib * rows[j] + ic * rows[j + 1]))
            later = range(j + 2, run)
            low_entry = {k: ia * entry[j][k] + ib * entry[j + 1][k] for k in later}
            high_entry = {k: ib * entry[j][k] + ic * entry[j + 1][k] for k in later}
            for i in range(run):
                if i in (j, j + 1):
                    continue
                from_low, from_high = entry[i][j], entry[i][j + 1]
                rows[i] = jnp.where(at_first | at_second, 0.0, rows[i]) - (from_low * low + from_high * high)
                for k in later:
                    if j + 1 < i and k < i:
                        entry[i][k] = entry[k][i]
                    else:
                        entry[i][k] = entry[i][k] - (from_low * low_entry[k] + from_high * high_entry[k])
            rows[j], rows[j + 1] = low, high
            for k in later:
                entry[j][k], entry[j + 1][k] = low_entry[k], high_entry[k]
        pivots = (column >= first) & (column < first + run)
        for r in range(len(blocks)):
            if r != p:
                terms = [columns[r][i] * rows[i] for i in range(run)]
                while len(terms) > 1:
                    terms = [terms[i] + terms[i + 1] for i in range(0, len(terms), 2)]
                blocks[r] = jnp.where(pivots, 0.0, blocks[r]) - terms[0]
        turned = rows[0]
        for i in range(1, run):
            turned = jnp.where(sub == i, rows[i], turned)
        blocks[p] = turned
    return jnp.concatenate(blocks, axis=0)


def inverses_body(total_tokens, factor_a_ref, factor_b_ref, grad_ref, in_ref):
    rank = factor_a_ref.shape[0]
    lane = lax.broadcasted_iota(jnp.int32, (rank, 2 * rank), 1)
    sub = lax.broadcasted_iota(jnp.int32, (rank, 2 * rank), 0)
    left = lane < rank
    column = jnp.where(left, lane, lane - rank)
    diagonal = column == sub
    packed = (factor_a_ref[...] + factor_b_ref[...]) / total_tokens
    on_diagonal = jnp.sum(jnp.where(diagonal, packed, 0.0), axis=0, keepdims=True)
    trace_in = jnp.sum(jnp.where(left[:1], on_diagonal, 0.0), axis=1, keepdims=True)
    trace_grad = jnp.sum(jnp.where(left[:1], 0.0, on_diagonal), axis=1, keepdims=True)
    damping = 0.1 * jnp.where(left[:1], trace_in, trace_grad) / rank + 1e-06
    packed = packed + jnp.where(diagonal, damping, 0.0)
    packed = invert(packed)
    twice = pltpu.roll(packed, rank, 1)
    grad_ref[0], grad_ref[1] = split(twice[:, :rank])
    in_ref[0, :rank, :], in_ref[1, :rank, :] = split(jnp.where(left, packed, 0.0))
    in_ref[0, rank:, :], in_ref[1, rank:, :] = split(jnp.where(left, 0.0, twice))


def inverses(total_tokens, factor_a, factor_b):
    rank, width = factor_a.shape
    return pl.pallas_call(
        functools.partial(inverses_body, total_tokens),
        out_shape=(
            jax.ShapeDtypeStruct((2, rank, rank), bf16),
            jax.ShapeDtypeStruct((2, width, width), bf16),
        ),
        in_specs=[VMEM, VMEM],
        out_specs=(VMEM, VMEM),
        compiler_params=pltpu.CompilerParams(vmem_limit_bytes=4 * MIB),
        cost_estimate=pl.CostEstimate(flops=0, bytes_accessed=0, transcendentals=0),
        name="inverses",
    )(factor_a, factor_b)


def pack_body(tests_ref, *out_refs):
    feat_count = len(out_refs)
    rows, width = tests_ref.shape
    fold, block = rows // feat_count, width // feat_count
    feat = lax.axis_index("feat")
    pieces = []
    for target in range(feat_count):
        columns = slice(target * block, (target + 1) * block)
        parts = [tests_ref[j * fold : (j + 1) * fold, columns] for j in range(feat_count)]
        pieces.append(jnp.concatenate(parts, axis=1))
    for mask, out_ref in enumerate(out_refs):
        piece = pieces[0]
        for target in range(1, feat_count):
            piece = jnp.where((feat ^ mask) == target, pieces[target], piece)
        out_ref[...] = piece


def pack(tests):
    rows, width = tests.shape
    feat_count = lax.axis_size("feat")
    return pl.pallas_call(
        pack_body,
        out_shape=[jax.ShapeDtypeStruct((rows // feat_count, width), bf16)] * feat_count,
        in_specs=[VMEM],
        out_specs=[VMEM] * feat_count,
        compiler_params=pltpu.CompilerParams(vmem_limit_bytes=8 * MIB),
        cost_estimate=pl.CostEstimate(flops=4 * MIB, bytes_accessed=4 * MIB, transcendentals=0),
        name="pack",
    )(tests)


def scores_body(blocks, grad_ref, in_ref, *refs):
    feat_count = lax.axis_size("feat")
    feat = lax.axis_index("feat")
    pieces, refs = refs[: 4 * feat_count], refs[4 * feat_count :]
    feats_refs, out_refs, (solved_buf, line_buf) = refs[:blocks], refs[blocks : 2 * blocks], refs[2 * blocks :]
    rank = grad_ref.shape[1]
    pairs = [ref[i] for ref in feats_refs for i in range(ref.shape[0])]
    count = len(pairs)
    half = count // blocks
    fold, width = pieces[0].shape
    block = width // feat_count
    dot = functools.partial(jnp.dot, preferred_element_type=f32)
    for at in range(count):
        high, low = split(dot(grad_ref[0], pairs[at]) + dot(grad_ref[1], pairs[at]))
        solved_buf[at * rank : (at + 1) * rank, :] = dot(high, in_ref[0]) + dot(high, in_ref[1]) + dot(low, in_ref[0])
    lane = lax.broadcasted_iota(jnp.int32, (count, 2 * rank), 1)
    for g in range(0, rank, 2):
        low = solved_buf[pl.ds(g, count, stride=rank), :]
        high = solved_buf[pl.ds(g + 1, count, stride=rank), :]
        first = jnp.where(lane < rank, low, pltpu.roll(high, rank, 1))
        second = jnp.where(lane < rank, pltpu.roll(low, rank, 1), high)
        line = jnp.concatenate([first, second], axis=0).astype(bf16)
        step = min(fold, 2 * rank)
        for begin in range(0, 2 * rank, step):
            at = (g * rank + begin) // fold
            to = (g * rank + begin) % fold
            line_buf[at // feat_count, at % feat_count, :, to : to + step] = line[:, begin : begin + step]
    lines = []
    for mask in range(feat_count):
        owner = feat ^ mask
        lines.append(jnp.concatenate([line_buf[owner, j] for j in range(feat_count)], axis=0))
    is_first = lax.axis_index("test") == 0
    odd = lax.rem(lax.axis_index("dp"), 2)
    for dp_bit in range(2):
        parts = []
        for test_bit in range(2):
            at = (2 * dp_bit + test_bit) * feat_count
            total = dot(lines[0], pieces[at][...])
            for mask in range(1, feat_count):
                total = total + dot(lines[mask], pieces[at + mask][...])
            part = total[: 2 * count, :block]
            for j in range(1, feat_count):
                part = part + total[2 * count * j : 2 * count * (j + 1), block * j : block * (j + 1)]
            parts.append(part)
        both = jnp.concatenate(
            [jnp.where(is_first, parts[0], parts[1]), jnp.where(is_first, parts[1], parts[0])], axis=1
        )
        for at, out_ref in enumerate(out_refs):
            out_ref[odd ^ dp_bit, :half, :] = both[at * half : (at + 1) * half, :]
            out_ref[odd ^ dp_bit, half:, :] = both[count + at * half : count + (at + 1) * half, :]


def scores_of(grad, in_pair, pieces, feats):
    feat_count = lax.axis_size("feat")
    rank = grad.shape[1]
    fold, width = pieces[0].shape
    half = feats[0].shape[0]
    count = half * len(feats)
    return pl.pallas_call(
        functools.partial(scores_body, len(feats)),
        out_shape=[jax.ShapeDtypeStruct((2, 2 * half, 2 * width // feat_count), f32)] * len(feats),
        in_specs=[VMEM] * (2 + len(pieces) + len(feats)),
        out_specs=[VMEM] * len(feats),
        scratch_shapes=[
            pltpu.VMEM((count * rank, 2 * rank), f32),
            pltpu.VMEM((feat_count, feat_count, 2 * count, fold), bf16),
        ],
        compiler_params=pltpu.CompilerParams(vmem_limit_bytes=16 * MIB),
        name="scores",
    )(grad, in_pair, *pieces, *feats)


def finish_body(*refs):
    block_refs, out_ref = refs[:-1], refs[-1]
    count = len(block_refs)
    _, examples, width = block_refs[0].shape
    half = width // 2
    own = lax.div(lax.axis_index("dp"), 2)
    for place in range(count):
        for odd in range(2):
            block = block_refs[0][odd]
            for mask in range(1, count):
                block = jnp.where((own ^ mask) == place, block_refs[mask][odd], block)
            for test in range(2):
                rows = pl.ds(4 * place + 2 * odd + test, examples, stride=4 * count)
                out_ref[rows, :] = block[:, test * half : (test + 1) * half]


def finish(blocks):
    _, examples, width = blocks[0].shape
    queries = 4 * len(blocks)
    out = pl.pallas_call(
        finish_body,
        out_shape=jax.ShapeDtypeStruct((examples * queries, width // 2), f32),
        in_specs=[VMEM] * len(blocks),
        out_specs=VMEM,
        compiler_params=pltpu.CompilerParams(vmem_limit_bytes=4 * MIB),
        name="finish",
    )(*blocks)
    return out.reshape(examples, queries, width // 2)


def after(values, *others):
    return lax.optimization_barrier((values, *others))[0]


def on_device(train_inputs, train_grads, proj_in, proj_out, lengths, loss_mask, test_feats):
    examples, seq_len, in_width = train_inputs.shape
    out_width = train_grads.shape[2]
    tokens = examples * seq_len
    feat_count = lax.axis_size("feat")
    dp_count = lax.axis_size("dp")
    test_count = lax.axis_size("test")
    own_rows = test_feats.shape[1]
    x = train_inputs.reshape(tokens, in_width)
    g = train_grads.reshape(tokens, out_width)
    own, sent = project(x, g, proj_in.T, proj_out.T, tokens // 3)
    received = [xor_permute(sent, "feat", mask) for mask in range(1, feat_count)]
    tests = test_feats.transpose(1, 2, 0).reshape(own_rows * test_feats.shape[2], test_feats.shape[0])
    cut = pack(after(tests, sent))
    near = [cut[0]] + [xor_permute(cut[mask], "feat", mask) for mask in range(1, feat_count)]
    factor, rounded, turned = factors(lengths, loss_mask, own, received)
    feats = [features_of(lengths, rounded, turned)]
    even_masks = range(2, dp_count, 2)
    steps = [("test", 1)] + [("dp", m) for m in masks_of(dp_count)]
    sums = [factor]
    for axis, mask in steps:
        if len(sums) == len(steps):
            sums[-1] = after(sums[-1], feats[0])
        other = xor_permute(sums[-1], axis, mask)
        sums.append(sums[-1] + other)
    factor = sums[-2]
    far = [xor_permute(near[0], "dp", 1)]
    if feat_count > 1:
        far += [xor_permute(piece, "dp", 1) for piece in after(tuple(near[1:]), sums[1])]
    shared = after(tuple(near), sums[2])
    pieces = near + [xor_permute(piece, "test", 1) for piece in shared]
    shared = after(tuple(far), other)
    pieces += far + [xor_permute(piece, "test", 1) for piece in shared]
    feats += [xor_permute(feats[0], "dp", mask) for mask in even_masks]
    grad, in_pair = inverses(float(tokens * dp_count * test_count), factor, other)
    blocks = scores_of(grad, in_pair, pieces, feats)
    blocks = [blocks[0]] + [xor_permute(blocks[at + 1], "dp", mask) for at, mask in enumerate(even_masks)]
    return finish(blocks)


def solution(mesh):
    return jax.shard_map(
        on_device,
        mesh=mesh,
        in_specs=(
            P(("groups", "dp", "test"), None, "feat"),
            P(("groups", "dp", "test"), None, "feat"),
            P("feat", None),
            P("feat", None),
            P(("groups", "dp", "test")),
            P(("groups", "dp", "test"), None),
            P(("groups", "dp", "test"), "feat", None),
        ),
        out_specs=P(("groups", "dp", "test"), None, "feat"),
        check_vma=False,
    )
```

```python
import functools

import jax
import jax.numpy as jnp
from jax import lax
from jax.experimental import pallas as pl
from jax.experimental.pallas import tpu as pltpu
from jax.sharding import PartitionSpec as P

f32 = jnp.float32
bf16 = jnp.bfloat16
MIB = 1024 * 1024
NT = (((1,), (1,)), ((), ()))
VMEM = pl.BlockSpec(memory_space=pltpu.VMEM)
SMEM = pl.BlockSpec(memory_space=pltpu.SMEM)
ANY = pl.BlockSpec(memory_space=pl.ANY)
PROJECT_MIB = 60


def xor_permute(values, axis, mask):
    size = lax.axis_size(axis)
    return lax.ppermute(values, axis, [(i, i ^ mask) for i in range(size)])


def masks_of(size):
    masks, mask = [], 1
    while mask < size:
        masks.append(mask)
        mask *= 2
    return masks


def project_body(rows, x_hbm, g_hbm, pin_hbm, pout_hbm, own_ref, sent_ref, x_buf, g_buf, pin_buf, pout_buf, sems):
    steps = x_hbm.shape[0] // rows
    rank = pin_hbm.shape[0]
    pin_copy = pltpu.make_async_copy(pin_hbm, pin_buf, sems.at[0])
    x_copy = pltpu.make_async_copy(x_hbm, x_buf, sems.at[1])
    pout_copy = pltpu.make_async_copy(pout_hbm, pout_buf, sems.at[2])

    def g_copy(step):
        begin = step * rows if isinstance(step, int) else pl.multiple_of(step * rows, rows)
        block = pl.ds(begin, rows)
        return pltpu.make_async_copy(g_hbm.at[block, :], g_buf.at[block, :], sems.at[3 + step])

    pin_copy.start()
    x_copy.start()
    pout_copy.start()
    for step in range(steps):
        g_copy(step).start()
    pin_copy.wait()
    x_copy.wait()
    own_ref[:, :rank] = lax.dot_general(x_buf[...], pin_buf[...], NT, preferred_element_type=f32)
    pout_copy.wait()

    @pl.loop(0, steps)
    def _(step):
        g_copy(step).wait()
        block = pl.ds(pl.multiple_of(step * rows, rows), rows)
        right = lax.dot_general(g_buf[block, :], pout_buf[...], NT, preferred_element_type=f32)
        both = jnp.concatenate([own_ref[block, :rank], right], axis=1)
        own_ref[block, :] = both
        sent_ref[block, :] = both.astype(bf16)


def project(x, g, pin, pout, rows):
    tokens, in_width = x.shape
    out_width = g.shape[1]
    rank = pin.shape[0]
    return pl.pallas_call(
        functools.partial(project_body, rows),
        out_shape=(
            jax.ShapeDtypeStruct((tokens, 2 * rank), f32),
            jax.ShapeDtypeStruct((tokens, 2 * rank), bf16),
        ),
        in_specs=[ANY] * 4,
        out_specs=(VMEM, VMEM),
        scratch_shapes=[
            pltpu.VMEM(x.shape, bf16),
            pltpu.VMEM(g.shape, bf16),
            pltpu.VMEM(pin.shape, bf16),
            pltpu.VMEM(pout.shape, bf16),
            pltpu.SemaphoreType.DMA((3 + tokens // rows,)),
        ],
        compiler_params=pltpu.CompilerParams(vmem_limit_bytes=PROJECT_MIB * MIB),
        cost_estimate=pl.CostEstimate(
            flops=2 * tokens * (in_width + out_width) * rank,
            bytes_accessed=2 * (tokens + rank) * (in_width + out_width),
            transcendentals=0,
        ),
        name="project",
    )(x, g, pin, pout)


def fetch_body(values_ref, out_ref):
    out_ref[...] = values_ref[...]


def fetch(values):
    return pl.pallas_call(
        fetch_body,
        out_shape=jax.ShapeDtypeStruct(values.shape, values.dtype),
        in_specs=[VMEM],
        out_specs=VMEM,
        compiler_params=pltpu.CompilerParams(vmem_limit_bytes=4 * MIB),
        cost_estimate=pl.CostEstimate(flops=values.size, bytes_accessed=8 * values.size, transcendentals=0),
        name="fetch",
    )(values)


def factors_body(received, lengths_ref, mask_ref, own_ref, *refs):
    received_refs = refs[:received]
    factor_ref, rounded_ref, turned_ref = refs[received:]
    examples, seq_len = mask_ref.shape
    rank = factor_ref.shape[0]
    positions = lax.broadcasted_iota(jnp.int32, (1, seq_len), 1)
    total = None
    for example in range(examples):
        rows = pl.ds(example * seq_len, seq_len)
        summed = own_ref[rows, :]
        for ref in received_refs:
            summed = summed + ref[rows, :].astype(f32)
        rounded = summed.astype(bf16)
        rounded_ref[rows, :] = rounded
        live = (mask_ref[example : example + 1, :] > 0) & (positions < lengths_ref[example])
        turned = jnp.where(live, rounded.astype(f32).T, 0.0).astype(bf16)
        turned_ref[example] = turned
        products = jnp.dot(turned, rounded, preferred_element_type=f32)
        total = products if total is None else total + products
    lane = lax.broadcasted_iota(jnp.int32, (rank, 2 * rank), 1)
    factor_ref[...] = jnp.where(lane < rank, total[:rank, :], total[rank:, :])


def factors(lengths, mask, own, received):
    tokens, width = own.shape
    examples, seq_len = mask.shape
    return pl.pallas_call(
        functools.partial(factors_body, len(received)),
        out_shape=(
            jax.ShapeDtypeStruct((width // 2, width), f32),
            jax.ShapeDtypeStruct((tokens, width), bf16),
            jax.ShapeDtypeStruct((examples, width, seq_len), bf16),
        ),
        in_specs=[SMEM, VMEM, VMEM] + [VMEM] * len(received),
        out_specs=(VMEM, VMEM, VMEM),
        compiler_params=pltpu.CompilerParams(vmem_limit_bytes=4 * MIB),
        name="factors",
    )(lengths, mask, own, *received)


def features_body(lengths_ref, rounded_ref, turned_ref, feats_ref):
    half, rank, _ = feats_ref.shape
    examples, _, seq_len = turned_ref.shape
    lane = lax.broadcasted_iota(jnp.int32, (rank, 2 * rank), 1)

    def features(example):
        products = jnp.dot(
            turned_ref[example, rank:, :], rounded_ref[pl.ds(example * seq_len, seq_len), :], preferred_element_type=f32
        )
        return products / lengths_ref[example].astype(f32)

    for pair in range(half):
        other = pltpu.roll(features(half + pair), rank, 1)
        feats_ref[pair] = jnp.where(lane < rank, features(pair), other).astype(bf16)


def features_of(lengths, rounded, turned):
    examples, width, seq_len = turned.shape
    return pl.pallas_call(
        features_body,
        out_shape=jax.ShapeDtypeStruct((examples // 2, width // 2, width), bf16),
        in_specs=[SMEM, VMEM, VMEM],
        out_specs=VMEM,
        compiler_params=pltpu.CompilerParams(vmem_limit_bytes=4 * MIB),
        cost_estimate=pl.CostEstimate(flops=2 * examples * seq_len * width * width, bytes_accessed=8 * MIB, transcendentals=0),
        name="features",
    )(lengths, rounded, turned)


def split(values):
    high = values.astype(bf16)
    return high, (values - high.astype(f32)).astype(bf16)


def invert(packed):
    rank, width = packed.shape
    run = 8
    blocks = [packed[run * r : run * (r + 1), :] for r in range(rank // run)]
    lane = lax.broadcasted_iota(jnp.int32, (run, width), 1)
    sub = lax.broadcasted_iota(jnp.int32, (run, width), 0)
    column = jnp.where(lane < rank, lane, lane - rank)
    base = jnp.where(lane < rank, 0, rank)

    def pick(values, at):
        return jnp.take_along_axis(values, base + at, axis=1)

    for p in range(len(blocks)):
        first = run * p
        rows = [jnp.broadcast_to(blocks[p][i : i + 1, :], (run, width)) for i in range(run)]
        entry = [[None] * run for _ in range(run)]
        for i in range(run):
            for j in range(i, run):
                entry[i][j] = entry[j][i] = pick(rows[i], first + j)
        columns = [[pick(block, first + j) for j in range(run)] for block in blocks]
        for j in range(0, run, 2):
            a, b, c = entry[j][j], entry[j][j + 1], entry[j + 1][j + 1]
            scale = 1.0 / (a * c - b * b)
            ia, ib, ic = c * scale, -(b * scale), a * scale
            at_first, at_second = column == first + j, column == first + j + 1
            low = jnp.where(at_first, ia, jnp.where(at_second, ib, ia * rows[j] + ib * rows[j + 1]))
            high = jnp.where(at_first, ib, jnp.where(at_second, ic, ib * rows[j] + ic * rows[j + 1]))
            later = range(j + 2, run)
            low_entry = {k: ia * entry[j][k] + ib * entry[j + 1][k] for k in later}
            high_entry = {k: ib * entry[j][k] + ic * entry[j + 1][k] for k in later}
            for i in range(run):
                if i in (j, j + 1):
                    continue
                from_low, from_high = entry[i][j], entry[i][j + 1]
                rows[i] = jnp.where(at_first | at_second, 0.0, rows[i]) - (from_low * low + from_high * high)
                for k in later:
                    if j + 1 < i and k < i:
                        entry[i][k] = entry[k][i]
                    else:
                        entry[i][k] = entry[i][k] - (from_low * low_entry[k] + from_high * high_entry[k])
            rows[j], rows[j + 1] = low, high
            for k in later:
                entry[j][k], entry[j + 1][k] = low_entry[k], high_entry[k]
        pivots = (column >= first) & (column < first + run)
        for r in range(len(blocks)):
            if r != p:
                terms = [columns[r][i] * rows[i] for i in range(run)]
                while len(terms) > 1:
                    terms = [terms[i] + terms[i + 1] for i in range(0, len(terms), 2)]
                blocks[r] = jnp.where(pivots, 0.0, blocks[r]) - terms[0]
        turned = rows[0]
        for i in range(1, run):
            turned = jnp.where(sub == i, rows[i], turned)
        blocks[p] = turned
    return jnp.concatenate(blocks, axis=0)


def inverses_body(total_tokens, factor_a_ref, factor_b_ref, grad_ref, in_ref):
    rank = factor_a_ref.shape[0]
    lane = lax.broadcasted_iota(jnp.int32, (rank, 2 * rank), 1)
    sub = lax.broadcasted_iota(jnp.int32, (rank, 2 * rank), 0)
    left = lane < rank
    column = jnp.where(left, lane, lane - rank)
    diagonal = column == sub
    packed = (factor_a_ref[...] + factor_b_ref[...]) / total_tokens
    on_diagonal = jnp.sum(jnp.where(diagonal, packed, 0.0), axis=0, keepdims=True)
    trace_in = jnp.sum(jnp.where(left[:1], on_diagonal, 0.0), axis=1, keepdims=True)
    trace_grad = jnp.sum(jnp.where(left[:1], 0.0, on_diagonal), axis=1, keepdims=True)
    damping = 0.1 * jnp.where(left[:1], trace_in, trace_grad) / rank + 1e-06
    packed = packed + jnp.where(diagonal, damping, 0.0)
    packed = invert(packed)
    twice = pltpu.roll(packed, rank, 1)
    grad_ref[0], grad_ref[1] = split(twice[:, :rank])
    in_ref[0, :rank, :], in_ref[1, :rank, :] = split(jnp.where(left, packed, 0.0))
    in_ref[0, rank:, :], in_ref[1, rank:, :] = split(jnp.where(left, 0.0, twice))


def inverses(total_tokens, factor_a, factor_b):
    rank, width = factor_a.shape
    return pl.pallas_call(
        functools.partial(inverses_body, total_tokens),
        out_shape=(
            jax.ShapeDtypeStruct((2, rank, rank), bf16),
            jax.ShapeDtypeStruct((2, width, width), bf16),
        ),
        in_specs=[VMEM, VMEM],
        out_specs=(VMEM, VMEM),
        compiler_params=pltpu.CompilerParams(vmem_limit_bytes=4 * MIB),
        cost_estimate=pl.CostEstimate(flops=0, bytes_accessed=0, transcendentals=0),
        name="inverses",
    )(factor_a, factor_b)


def pack_body(tests_ref, *out_refs):
    feat_count = len(out_refs)
    rows, width = tests_ref.shape
    fold, block = rows // feat_count, width // feat_count
    feat = lax.axis_index("feat")
    pieces = []
    for target in range(feat_count):
        columns = slice(target * block, (target + 1) * block)
        parts = [tests_ref[j * fold : (j + 1) * fold, columns] for j in range(feat_count)]
        pieces.append(jnp.concatenate(parts, axis=1))
    for mask, out_ref in enumerate(out_refs):
        piece = pieces[0]
        for target in range(1, feat_count):
            piece = jnp.where((feat ^ mask) == target, pieces[target], piece)
        out_ref[...] = piece


def pack(tests):
    rows, width = tests.shape
    feat_count = lax.axis_size("feat")
    return pl.pallas_call(
        pack_body,
        out_shape=[jax.ShapeDtypeStruct((rows // feat_count, width), bf16)] * feat_count,
        in_specs=[VMEM],
        out_specs=[VMEM] * feat_count,
        compiler_params=pltpu.CompilerParams(vmem_limit_bytes=8 * MIB),
        cost_estimate=pl.CostEstimate(flops=4 * MIB, bytes_accessed=4 * MIB, transcendentals=0),
        name="pack",
    )(tests)


def scores_body(blocks, grad_ref, in_ref, *refs):
    feat_count = lax.axis_size("feat")
    feat = lax.axis_index("feat")
    pieces, refs = refs[: 4 * feat_count], refs[4 * feat_count :]
    feats_refs, out_refs, (solved_buf, line_buf) = refs[:blocks], refs[blocks : 2 * blocks], refs[2 * blocks :]
    rank = grad_ref.shape[1]
    pairs = [ref[i] for ref in feats_refs for i in range(ref.shape[0])]
    count = len(pairs)
    half = count // blocks
    fold, width = pieces[0].shape
    block = width // feat_count
    dot = functools.partial(jnp.dot, preferred_element_type=f32)
    for at in range(count):
        high, low = split(dot(grad_ref[0], pairs[at]) + dot(grad_ref[1], pairs[at]))
        solved_buf[at * rank : (at + 1) * rank, :] = dot(high, in_ref[0]) + dot(high, in_ref[1]) + dot(low, in_ref[0])
    lane = lax.broadcasted_iota(jnp.int32, (count, 2 * rank), 1)
    for g in range(0, rank, 2):
        low = solved_buf[pl.ds(g, count, stride=rank), :]
        high = solved_buf[pl.ds(g + 1, count, stride=rank), :]
        first = jnp.where(lane < rank, low, pltpu.roll(high, rank, 1))
        second = jnp.where(lane < rank, pltpu.roll(low, rank, 1), high)
        line = jnp.concatenate([first, second], axis=0).astype(bf16)
        step = min(fold, 2 * rank)
        for begin in range(0, 2 * rank, step):
            at = (g * rank + begin) // fold
            to = (g * rank + begin) % fold
            line_buf[at // feat_count, at % feat_count, :, to : to + step] = line[:, begin : begin + step]
    lines = []
    for mask in range(feat_count):
        owner = feat ^ mask
        lines.append(jnp.concatenate([line_buf[owner, j] for j in range(feat_count)], axis=0))
    is_first = lax.axis_index("test") == 0
    odd = lax.rem(lax.axis_index("dp"), 2)
    for dp_bit in range(2):
        parts = []
        for test_bit in range(2):
            at = (2 * dp_bit + test_bit) * feat_count
            total = dot(lines[0], pieces[at][...])
            for mask in range(1, feat_count):
                total = total + dot(lines[mask], pieces[at + mask][...])
            part = total[: 2 * count, :block]
            for j in range(1, feat_count):
                part = part + total[2 * count * j : 2 * count * (j + 1), block * j : block * (j + 1)]
            parts.append(part)
        both = jnp.concatenate(
            [jnp.where(is_first, parts[0], parts[1]), jnp.where(is_first, parts[1], parts[0])], axis=1
        )
        for at, out_ref in enumerate(out_refs):
            out_ref[odd ^ dp_bit, :half, :] = both[at * half : (at + 1) * half, :]
            out_ref[odd ^ dp_bit, half:, :] = both[count + at * half : count + (at + 1) * half, :]


def scores_of(grad, in_pair, pieces, feats):
    feat_count = lax.axis_size("feat")
    rank = grad.shape[1]
    fold, width = pieces[0].shape
    half = feats[0].shape[0]
    count = half * len(feats)
    return pl.pallas_call(
        functools.partial(scores_body, len(feats)),
        out_shape=[jax.ShapeDtypeStruct((2, 2 * half, 2 * width // feat_count), f32)] * len(feats),
        in_specs=[VMEM] * (2 + len(pieces) + len(feats)),
        out_specs=[VMEM] * len(feats),
        scratch_shapes=[
            pltpu.VMEM((count * rank, 2 * rank), f32),
            pltpu.VMEM((feat_count, feat_count, 2 * count, fold), bf16),
        ],
        compiler_params=pltpu.CompilerParams(vmem_limit_bytes=16 * MIB),
        name="scores",
    )(grad, in_pair, *pieces, *feats)


def finish_body(*refs):
    block_refs, out_ref = refs[:-1], refs[-1]
    count = len(block_refs)
    _, examples, width = block_refs[0].shape
    half = width // 2
    own = lax.div(lax.axis_index("dp"), 2)
    for place in range(count):
        for odd in range(2):
            block = block_refs[0][odd]
            for mask in range(1, count):
                block = jnp.where((own ^ mask) == place, block_refs[mask][odd], block)
            for test in range(2):
                rows = pl.ds(4 * place + 2 * odd + test, examples, stride=4 * count)
                out_ref[rows, :] = block[:, test * half : (test + 1) * half]


def finish(blocks):
    _, examples, width = blocks[0].shape
    queries = 4 * len(blocks)
    out = pl.pallas_call(
        finish_body,
        out_shape=jax.ShapeDtypeStruct((examples * queries, width // 2), f32),
        in_specs=[VMEM] * len(blocks),
        out_specs=VMEM,
        compiler_params=pltpu.CompilerParams(vmem_limit_bytes=4 * MIB),
        name="finish",
    )(*blocks)
    return out.reshape(examples, queries, width // 2)


def after(values, *others):
    return lax.optimization_barrier((values, *others))[0]


def on_device(train_inputs, train_grads, proj_in, proj_out, lengths, loss_mask, test_feats):
    examples, seq_len, in_width = train_inputs.shape
    out_width = train_grads.shape[2]
    tokens = examples * seq_len
    feat_count = lax.axis_size("feat")
    dp_count = lax.axis_size("dp")
    test_count = lax.axis_size("test")
    own_rows = test_feats.shape[1]
    x = train_inputs.reshape(tokens, in_width)
    g = train_grads.reshape(tokens, out_width)
    tests = test_feats.transpose(1, 2, 0).reshape(own_rows * test_feats.shape[2], test_feats.shape[0])
    cut = pack(tests)
    near = [cut[0]] + [xor_permute(cut[mask], "feat", mask) for mask in range(1, feat_count)]
    far = [xor_permute(near[0], "dp", 1)]
    own, sent = project(x, g, after(proj_in.T, cut[0]), proj_out.T, tokens // 3)
    far += [xor_permute(piece, "dp", 1) for piece in after(tuple(near[1:]), sent)]
    received = [xor_permute(sent, "feat", mask) for mask in range(1, feat_count)]
    factor, rounded, turned = factors(lengths, loss_mask, fetch(own), received)
    feats = [features_of(lengths, rounded, turned)]
    even_masks = range(2, dp_count, 2)
    steps = [("test", 1)] + [("dp", m) for m in reversed(masks_of(dp_count))]
    sums = [factor]
    for axis, mask in steps:
        if len(sums) == len(steps):
            sums[-1] = after(sums[-1], feats[0])
        other = xor_permute(sums[-1], axis, mask)
        sums.append(sums[-1] + other)
    pieces = []
    for part in (near, far):
        pieces += part + [xor_permute(piece, "test", 1) for piece in after(tuple(part), sums[2])]
    feats += [xor_permute(feats[0], "dp", mask) for mask in even_masks]
    total_tokens = float(tokens * dp_count * test_count)
    grad, in_pair = inverses(total_tokens, sums[-2], other)
    blocks = scores_of(grad, in_pair, pieces, feats)
    blocks = [blocks[0]] + [xor_permute(blocks[at + 1], "dp", mask) for at, mask in enumerate(even_masks)]
    return finish(blocks)


def solution(mesh):
    return jax.shard_map(
        on_device,
        mesh=mesh,
        in_specs=(
            P(("groups", "dp", "test"), None, "feat"),
            P(("groups", "dp", "test"), None, "feat"),
            P("feat", None),
            P("feat", None),
            P(("groups", "dp", "test")),
            P(("groups", "dp", "test"), None),
            P(("groups", "dp", "test"), "feat", None),
        ),
        out_specs=P(("groups", "dp", "test"), None, "feat"),
        check_vma=False,
    )
```

```python
import functools

import jax
import jax.numpy as jnp
from jax import lax
from jax.experimental import pallas as pl
from jax.experimental.pallas import tpu as pltpu
from jax.sharding import PartitionSpec as P

f32 = jnp.float32
bf16 = jnp.bfloat16
MIB = 1024 * 1024
NT = (((1,), (1,)), ((), ()))
VMEM = pl.BlockSpec(memory_space=pltpu.VMEM)
SMEM = pl.BlockSpec(memory_space=pltpu.SMEM)
ANY = pl.BlockSpec(memory_space=pl.ANY)
PROJECT_MIB = 60


def xor_permute(values, axis, mask):
    size = lax.axis_size(axis)
    return lax.ppermute(values, axis, [(i, i ^ mask) for i in range(size)])


def masks_of(size):
    masks, mask = [], 1
    while mask < size:
        masks.append(mask)
        mask *= 2
    return masks


def project_body(rows, x_hbm, g_hbm, pin_hbm, pout_hbm, own_ref, sent_ref, x_buf, g_buf, pin_buf, pout_buf, sems):
    steps = x_hbm.shape[0] // rows
    rank = pin_hbm.shape[0]
    pin_copy = pltpu.make_async_copy(pin_hbm, pin_buf, sems.at[0])
    x_copy = pltpu.make_async_copy(x_hbm, x_buf, sems.at[1])
    pout_copy = pltpu.make_async_copy(pout_hbm, pout_buf, sems.at[2])

    def g_copy(step):
        begin = step * rows if isinstance(step, int) else pl.multiple_of(step * rows, rows)
        block = pl.ds(begin, rows)
        return pltpu.make_async_copy(g_hbm.at[block, :], g_buf.at[block, :], sems.at[3 + step])

    pin_copy.start()
    x_copy.start()
    pout_copy.start()
    for step in range(steps):
        g_copy(step).start()
    pin_copy.wait()
    x_copy.wait()
    own_ref[:, :rank] = lax.dot_general(x_buf[...], pin_buf[...], NT, preferred_element_type=f32)
    pout_copy.wait()

    @pl.loop(0, steps)
    def _(step):
        g_copy(step).wait()
        block = pl.ds(pl.multiple_of(step * rows, rows), rows)
        right = lax.dot_general(g_buf[block, :], pout_buf[...], NT, preferred_element_type=f32)
        both = jnp.concatenate([own_ref[block, :rank], right], axis=1)
        own_ref[block, :] = both
        sent_ref[block, :] = both.astype(bf16)


def project(x, g, pin, pout, rows):
    tokens, in_width = x.shape
    out_width = g.shape[1]
    rank = pin.shape[0]
    return pl.pallas_call(
        functools.partial(project_body, rows),
        out_shape=(
            jax.ShapeDtypeStruct((tokens, 2 * rank), f32),
            jax.ShapeDtypeStruct((tokens, 2 * rank), bf16),
        ),
        in_specs=[ANY] * 4,
        out_specs=(VMEM, VMEM),
        scratch_shapes=[
            pltpu.VMEM(x.shape, bf16),
            pltpu.VMEM(g.shape, bf16),
            pltpu.VMEM(pin.shape, bf16),
            pltpu.VMEM(pout.shape, bf16),
            pltpu.SemaphoreType.DMA((3 + tokens // rows,)),
        ],
        compiler_params=pltpu.CompilerParams(vmem_limit_bytes=PROJECT_MIB * MIB),
        cost_estimate=pl.CostEstimate(
            flops=2 * tokens * (in_width + out_width) * rank,
            bytes_accessed=2 * (tokens + rank) * (in_width + out_width),
            transcendentals=0,
        ),
        name="project",
    )(x, g, pin, pout)


def fetch_body(values_ref, out_ref):
    out_ref[...] = values_ref[...]


def fetch(values):
    return pl.pallas_call(
        fetch_body,
        out_shape=jax.ShapeDtypeStruct(values.shape, values.dtype),
        in_specs=[VMEM],
        out_specs=VMEM,
        compiler_params=pltpu.CompilerParams(vmem_limit_bytes=4 * MIB),
        cost_estimate=pl.CostEstimate(flops=values.size, bytes_accessed=8 * values.size, transcendentals=0),
        name="fetch",
    )(values)


def factors_body(received, lengths_ref, mask_ref, own_ref, *refs):
    received_refs = refs[:received]
    factor_ref, rounded_ref, turned_ref = refs[received:]
    examples, seq_len = mask_ref.shape
    rank = factor_ref.shape[0]
    positions = lax.broadcasted_iota(jnp.int32, (1, seq_len), 1)
    total = None
    for example in range(examples):
        rows = pl.ds(example * seq_len, seq_len)
        summed = own_ref[rows, :]
        for ref in received_refs:
            summed = summed + ref[rows, :].astype(f32)
        rounded = summed.astype(bf16)
        rounded_ref[rows, :] = rounded
        live = (mask_ref[example : example + 1, :] > 0) & (positions < lengths_ref[example])
        turned = jnp.where(live, rounded.astype(f32).T, 0.0).astype(bf16)
        turned_ref[example] = turned
        products = jnp.dot(turned, rounded, preferred_element_type=f32)
        total = products if total is None else total + products
    lane = lax.broadcasted_iota(jnp.int32, (rank, 2 * rank), 1)
    factor_ref[...] = jnp.where(lane < rank, total[:rank, :], total[rank:, :])


def factors(lengths, mask, own, received):
    tokens, width = own.shape
    examples, seq_len = mask.shape
    return pl.pallas_call(
        functools.partial(factors_body, len(received)),
        out_shape=(
            jax.ShapeDtypeStruct((width // 2, width), f32),
            jax.ShapeDtypeStruct((tokens, width), bf16),
            jax.ShapeDtypeStruct((examples, width, seq_len), bf16),
        ),
        in_specs=[SMEM, VMEM, VMEM] + [VMEM] * len(received),
        out_specs=(VMEM, VMEM, VMEM),
        compiler_params=pltpu.CompilerParams(vmem_limit_bytes=4 * MIB),
        name="factors",
    )(lengths, mask, own, *received)


def features_body(lengths_ref, rounded_ref, turned_ref, feats_ref):
    half, rank, _ = feats_ref.shape
    examples, _, seq_len = turned_ref.shape
    lane = lax.broadcasted_iota(jnp.int32, (rank, 2 * rank), 1)

    def features(example):
        products = jnp.dot(
            turned_ref[example, rank:, :], rounded_ref[pl.ds(example * seq_len, seq_len), :], preferred_element_type=f32
        )
        return products / lengths_ref[example].astype(f32)

    for pair in range(half):
        other = pltpu.roll(features(half + pair), rank, 1)
        feats_ref[pair] = jnp.where(lane < rank, features(pair), other).astype(bf16)


def features_of(lengths, rounded, turned):
    examples, width, seq_len = turned.shape
    return pl.pallas_call(
        features_body,
        out_shape=jax.ShapeDtypeStruct((examples // 2, width // 2, width), bf16),
        in_specs=[SMEM, VMEM, VMEM],
        out_specs=VMEM,
        compiler_params=pltpu.CompilerParams(vmem_limit_bytes=4 * MIB),
        cost_estimate=pl.CostEstimate(flops=2 * examples * seq_len * width * width, bytes_accessed=8 * MIB, transcendentals=0),
        name="features",
    )(lengths, rounded, turned)


def split(values):
    high = values.astype(bf16)
    return high, (values - high.astype(f32)).astype(bf16)


def invert(packed):
    rank, width = packed.shape
    run = 8
    blocks = [packed[run * r : run * (r + 1), :] for r in range(rank // run)]
    lane = lax.broadcasted_iota(jnp.int32, (run, width), 1)
    sub = lax.broadcasted_iota(jnp.int32, (run, width), 0)
    column = jnp.where(lane < rank, lane, lane - rank)
    base = jnp.where(lane < rank, 0, rank)

    def pick(values, at):
        return jnp.take_along_axis(values, base + at, axis=1)

    for p in range(len(blocks)):
        first = run * p
        rows = [jnp.broadcast_to(blocks[p][i : i + 1, :], (run, width)) for i in range(run)]
        entry = [[None] * run for _ in range(run)]
        for i in range(run):
            for j in range(i, run):
                entry[i][j] = entry[j][i] = pick(rows[i], first + j)
        columns = [[pick(block, first + j) for j in range(run)] for block in blocks]
        for j in range(0, run, 2):
            a, b, c = entry[j][j], entry[j][j + 1], entry[j + 1][j + 1]
            scale = 1.0 / (a * c - b * b)
            ia, ib, ic = c * scale, -(b * scale), a * scale
            at_first, at_second = column == first + j, column == first + j + 1
            low = jnp.where(at_first, ia, jnp.where(at_second, ib, ia * rows[j] + ib * rows[j + 1]))
            high = jnp.where(at_first, ib, jnp.where(at_second, ic, ib * rows[j] + ic * rows[j + 1]))
            later = range(j + 2, run)
            low_entry = {k: ia * entry[j][k] + ib * entry[j + 1][k] for k in later}
            high_entry = {k: ib * entry[j][k] + ic * entry[j + 1][k] for k in later}
            for i in range(run):
                if i in (j, j + 1):
                    continue
                from_low, from_high = entry[i][j], entry[i][j + 1]
                rows[i] = jnp.where(at_first | at_second, 0.0, rows[i]) - (from_low * low + from_high * high)
                for k in later:
                    if j + 1 < i and k < i:
                        entry[i][k] = entry[k][i]
                    else:
                        entry[i][k] = entry[i][k] - (from_low * low_entry[k] + from_high * high_entry[k])
            rows[j], rows[j + 1] = low, high
            for k in later:
                entry[j][k], entry[j + 1][k] = low_entry[k], high_entry[k]
        pivots = (column >= first) & (column < first + run)
        for r in range(len(blocks)):
            if r != p:
                terms = [columns[r][i] * rows[i] for i in range(run)]
                while len(terms) > 1:
                    terms = [terms[i] + terms[i + 1] for i in range(0, len(terms), 2)]
                blocks[r] = jnp.where(pivots, 0.0, blocks[r]) - terms[0]
        turned = rows[0]
        for i in range(1, run):
            turned = jnp.where(sub == i, rows[i], turned)
        blocks[p] = turned
    return jnp.concatenate(blocks, axis=0)


def damped_inverses(total_tokens, packed):
    rank = packed.shape[0]
    lane = lax.broadcasted_iota(jnp.int32, (rank, 2 * rank), 1)
    sub = lax.broadcasted_iota(jnp.int32, (rank, 2 * rank), 0)
    left = lane < rank
    diagonal = jnp.where(left, lane, lane - rank) == sub
    packed = packed / total_tokens
    on_diagonal = jnp.sum(jnp.where(diagonal, packed, 0.0), axis=0, keepdims=True)
    trace_in = jnp.sum(jnp.where(left[:1], on_diagonal, 0.0), axis=1, keepdims=True)
    trace_grad = jnp.sum(jnp.where(left[:1], 0.0, on_diagonal), axis=1, keepdims=True)
    damping = 0.1 * jnp.where(left[:1], trace_in, trace_grad) / rank + 1e-06
    packed = invert(packed + jnp.where(diagonal, damping, 0.0))
    other = pltpu.roll(packed, rank, 1)
    in_pair = jnp.concatenate([jnp.where(left, packed, 0.0), jnp.where(left, 0.0, other)], axis=0)
    return other[:, :rank], in_pair


def pack_body(tests_ref, *out_refs):
    feat_count = len(out_refs)
    rows, width = tests_ref.shape
    fold, block = rows // feat_count, width // feat_count
    feat = lax.axis_index("feat")
    pieces = []
    for target in range(feat_count):
        columns = slice(target * block, (target + 1) * block)
        parts = [tests_ref[j * fold : (j + 1) * fold, columns] for j in range(feat_count)]
        pieces.append(jnp.concatenate(parts, axis=1))
    for mask, out_ref in enumerate(out_refs):
        piece = pieces[0]
        for target in range(1, feat_count):
            piece = jnp.where((feat ^ mask) == target, pieces[target], piece)
        out_ref[...] = piece


def pack(tests):
    rows, width = tests.shape
    feat_count = lax.axis_size("feat")
    return pl.pallas_call(
        pack_body,
        out_shape=[jax.ShapeDtypeStruct((rows // feat_count, width), bf16)] * feat_count,
        in_specs=[VMEM],
        out_specs=[VMEM] * feat_count,
        compiler_params=pltpu.CompilerParams(vmem_limit_bytes=8 * MIB),
        cost_estimate=pl.CostEstimate(flops=4 * MIB, bytes_accessed=4 * MIB, transcendentals=0),
        name="pack",
    )(tests)


def scores_body(total_tokens, blocks, factor_a_ref, factor_b_ref, *refs):
    feat_count = lax.axis_size("feat")
    feat = lax.axis_index("feat")
    pieces, refs = refs[: 4 * feat_count], refs[4 * feat_count :]
    feats_refs, out_refs, (solved_buf, line_buf) = refs[:blocks], refs[blocks : 2 * blocks], refs[2 * blocks :]
    rank = factor_a_ref.shape[0]
    grad, in_pair = damped_inverses(total_tokens, factor_a_ref[...] + factor_b_ref[...])
    grad_high, grad_low = split(grad)
    in_high, in_low = split(in_pair)
    pairs = [ref[i] for ref in feats_refs for i in range(ref.shape[0])]
    count = len(pairs)
    half = count // blocks
    fold, width = pieces[0].shape
    block = width // feat_count
    dot = functools.partial(jnp.dot, preferred_element_type=f32)
    for at in range(count):
        high, low = split(dot(grad_high, pairs[at]) + dot(grad_low, pairs[at]))
        solved_buf[at * rank : (at + 1) * rank, :] = dot(high, in_high) + dot(high, in_low) + dot(low, in_high)
    lane = lax.broadcasted_iota(jnp.int32, (count, 2 * rank), 1)
    for g in range(0, rank, 2):
        low = solved_buf[pl.ds(g, count, stride=rank), :]
        high = solved_buf[pl.ds(g + 1, count, stride=rank), :]
        first = jnp.where(lane < rank, low, pltpu.roll(high, rank, 1))
        second = jnp.where(lane < rank, pltpu.roll(low, rank, 1), high)
        line = jnp.concatenate([first, second], axis=0).astype(bf16)
        step = min(fold, 2 * rank)
        for begin in range(0, 2 * rank, step):
            at = (g * rank + begin) // fold
            to = (g * rank + begin) % fold
            line_buf[at // feat_count, at % feat_count, :, to : to + step] = line[:, begin : begin + step]
    lines = []
    for mask in range(feat_count):
        owner = feat ^ mask
        lines.append(jnp.concatenate([line_buf[owner, j] for j in range(feat_count)], axis=0))
    is_first = lax.axis_index("test") == 0
    odd = lax.rem(lax.axis_index("dp"), 2)
    for dp_bit in range(2):
        parts = []
        for test_bit in range(2):
            total = None
            for mask in range(feat_count):
                term = dot(lines[mask], pieces[(2 * dp_bit + test_bit) * feat_count + mask][...])
                total = term if total is None else total + term
            part = total[: 2 * count, :block]
            for j in range(1, feat_count):
                part = part + total[2 * count * j : 2 * count * (j + 1), block * j : block * (j + 1)]
            parts.append(part)
        both = jnp.concatenate(
            [jnp.where(is_first, parts[0], parts[1]), jnp.where(is_first, parts[1], parts[0])], axis=1
        )
        for at, out_ref in enumerate(out_refs):
            out_ref[odd ^ dp_bit, :half, :] = both[at * half : (at + 1) * half, :]
            out_ref[odd ^ dp_bit, half:, :] = both[count + at * half : count + (at + 1) * half, :]


def scores_of(total_tokens, factor_a, factor_b, pieces, feats):
    feat_count = lax.axis_size("feat")
    rank = factor_a.shape[0]
    fold, width = pieces[0].shape
    half = feats[0].shape[0]
    count = half * len(feats)
    return pl.pallas_call(
        functools.partial(scores_body, total_tokens, len(feats)),
        out_shape=[jax.ShapeDtypeStruct((2, 2 * half, 2 * width // feat_count), f32)] * len(feats),
        in_specs=[VMEM] * (2 + len(pieces) + len(feats)),
        out_specs=[VMEM] * len(feats),
        scratch_shapes=[
            pltpu.VMEM((count * rank, 2 * rank), f32),
            pltpu.VMEM((feat_count, feat_count, 2 * count, fold), bf16),
        ],
        compiler_params=pltpu.CompilerParams(vmem_limit_bytes=16 * MIB),
        name="scores",
    )(factor_a, factor_b, *pieces, *feats)


def finish_body(*refs):
    block_refs, out_ref = refs[:-1], refs[-1]
    count = len(block_refs)
    _, examples, width = block_refs[0].shape
    half = width // 2
    own = lax.div(lax.axis_index("dp"), 2)
    for place in range(count):
        for odd in range(2):
            block = block_refs[0][odd]
            for mask in range(1, count):
                block = jnp.where((own ^ mask) == place, block_refs[mask][odd], block)
            for test in range(2):
                rows = pl.ds(4 * place + 2 * odd + test, examples, stride=4 * count)
                out_ref[rows, :] = block[:, test * half : (test + 1) * half]


def finish(blocks):
    _, examples, width = blocks[0].shape
    queries = 4 * len(blocks)
    out = pl.pallas_call(
        finish_body,
        out_shape=jax.ShapeDtypeStruct((examples * queries, width // 2), f32),
        in_specs=[VMEM] * len(blocks),
        out_specs=VMEM,
        compiler_params=pltpu.CompilerParams(vmem_limit_bytes=4 * MIB),
        name="finish",
    )(*blocks)
    return out.reshape(examples, queries, width // 2)


def after(values, *others):
    return lax.optimization_barrier((values, *others))[0]


def on_device(train_inputs, train_grads, proj_in, proj_out, lengths, loss_mask, test_feats):
    examples, seq_len, in_width = train_inputs.shape
    out_width = train_grads.shape[2]
    tokens = examples * seq_len
    feat_count = lax.axis_size("feat")
    dp_count = lax.axis_size("dp")
    test_count = lax.axis_size("test")
    own_rows = test_feats.shape[1]
    x = train_inputs.reshape(tokens, in_width)
    g = train_grads.reshape(tokens, out_width)
    tests = test_feats.transpose(1, 2, 0).reshape(own_rows * test_feats.shape[2], test_feats.shape[0])
    cut = pack(tests)
    near = [cut[0]] + [xor_permute(cut[mask], "feat", mask) for mask in range(1, feat_count)]
    far = [xor_permute(near[0], "dp", 1)]
    own, sent = project(x, g, after(proj_in.T, cut[0]), proj_out.T, tokens // 3)
    far += [xor_permute(piece, "dp", 1) for piece in after(tuple(near[1:]), sent)]
    received = [xor_permute(sent, "feat", mask) for mask in range(1, feat_count)]
    shared = [xor_permute(piece, "test", 1) for piece in after(tuple(near), sent)]
    factor, rounded, turned = factors(lengths, loss_mask, fetch(own), received)
    feats = [features_of(lengths, rounded, turned)]
    even_masks = range(2, dp_count, 2)
    steps = [("test", 1)] + [("dp", m) for m in reversed(masks_of(dp_count))]
    sums = [factor]
    for axis, mask in steps:
        if len(sums) == 3:
            sums[-1] = after(sums[-1], *shared)
        if len(sums) == len(steps):
            sums[-1] = after(sums[-1], feats[0])
        other = xor_permute(sums[-1], axis, mask)
        sums.append(sums[-1] + other)
    pieces = near + shared + far + [xor_permute(piece, "test", 1) for piece in after(tuple(far), *(sums[2],))]
    feats += [xor_permute(feats[0], "dp", mask) for mask in even_masks]
    total_tokens = float(tokens * dp_count * test_count)
    blocks = scores_of(total_tokens, sums[-2], other, pieces, feats)
    blocks = [blocks[0]] + [xor_permute(blocks[at + 1], "dp", mask) for at, mask in enumerate(even_masks)]
    return finish(blocks)


def solution(mesh):
    return jax.shard_map(
        on_device,
        mesh=mesh,
        in_specs=(
            P(("groups", "dp", "test"), None, "feat"),
            P(("groups", "dp", "test"), None, "feat"),
            P("feat", None),
            P("feat", None),
            P(("groups", "dp", "test")),
            P(("groups", "dp", "test"), None),
            P(("groups", "dp", "test"), "feat", None),
        ),
        out_specs=P(("groups", "dp", "test"), None, "feat"),
        check_vma=False,
    )
```

```python
import functools

import jax
import jax.numpy as jnp
from jax import lax
from jax.experimental import pallas as pl
from jax.experimental.pallas import tpu as pltpu
from jax.sharding import PartitionSpec as P

f32 = jnp.float32
bf16 = jnp.bfloat16
MIB = 1024 * 1024
NT = (((1,), (1,)), ((), ()))
VMEM = pl.BlockSpec(memory_space=pltpu.VMEM)
SMEM = pl.BlockSpec(memory_space=pltpu.SMEM)
ANY = pl.BlockSpec(memory_space=pl.ANY)
PROJECT_MIB = 48


def xor_permute(values, axis, mask):
    size = lax.axis_size(axis)
    return lax.ppermute(values, axis, [(i, i ^ mask) for i in range(size)])


def masks_of(size):
    masks, mask = [], 1
    while mask < size:
        masks.append(mask)
        mask *= 2
    return masks


def project_body(rows, x_ref, g_hbm, pin_ref, pout_ref, own_ref, sent_ref, g_buf, sems):
    steps = x_ref.shape[0] // rows
    rank = pin_ref.shape[0]

    def g_copy(step):
        begin = step * rows if isinstance(step, int) else pl.multiple_of(step * rows, rows)
        block = pl.ds(begin, rows)
        return pltpu.make_async_copy(g_hbm.at[block, :], g_buf.at[block, :], sems.at[step])

    for step in range(steps):
        g_copy(step).start()
    own_ref[:, :rank] = lax.dot_general(x_ref[...], pin_ref[...], NT, preferred_element_type=f32)

    @pl.loop(0, steps)
    def _(step):
        g_copy(step).wait()
        block = pl.ds(pl.multiple_of(step * rows, rows), rows)
        right = lax.dot_general(g_buf[block, :], pout_ref[...], NT, preferred_element_type=f32)
        both = jnp.concatenate([own_ref[block, :rank], right], axis=1)
        own_ref[block, :] = both
        sent_ref[block, :] = both.astype(bf16)


def project(x, g, pin, pout, rows):
    tokens, in_width = x.shape
    out_width = g.shape[1]
    rank = pin.shape[0]
    return pl.pallas_call(
        functools.partial(project_body, rows),
        out_shape=(
            jax.ShapeDtypeStruct((tokens, 2 * rank), f32),
            jax.ShapeDtypeStruct((tokens, 2 * rank), bf16),
        ),
        in_specs=[VMEM, ANY, VMEM, VMEM],
        out_specs=(VMEM, VMEM),
        scratch_shapes=[pltpu.VMEM(g.shape, bf16), pltpu.SemaphoreType.DMA((tokens // rows,))],
        compiler_params=pltpu.CompilerParams(vmem_limit_bytes=PROJECT_MIB * MIB),
        cost_estimate=pl.CostEstimate(
            flops=2 * tokens * (in_width + out_width) * rank,
            bytes_accessed=2 * (tokens + rank) * (in_width + out_width),
            transcendentals=0,
        ),
        name="project",
    )(x, g, pin, pout)


def fetch_body(values_ref, out_ref):
    out_ref[...] = values_ref[...]


def fetch(values):
    return pl.pallas_call(
        fetch_body,
        out_shape=jax.ShapeDtypeStruct(values.shape, values.dtype),
        in_specs=[VMEM],
        out_specs=VMEM,
        compiler_params=pltpu.CompilerParams(vmem_limit_bytes=4 * MIB),
        cost_estimate=pl.CostEstimate(flops=values.size, bytes_accessed=8 * values.size, transcendentals=0),
        name="fetch",
    )(values)


def factors_body(received, lengths_ref, mask_ref, own_ref, *refs):
    received_refs = refs[:received]
    factor_ref, rounded_ref, turned_ref = refs[received:]
    examples, seq_len = mask_ref.shape
    rank = factor_ref.shape[0]
    positions = lax.broadcasted_iota(jnp.int32, (1, seq_len), 1)
    total = None
    for example in range(examples):
        rows = pl.ds(example * seq_len, seq_len)
        summed = own_ref[rows, :]
        for ref in received_refs:
            summed = summed + ref[rows, :].astype(f32)
        rounded = summed.astype(bf16)
        rounded_ref[rows, :] = rounded
        live = (mask_ref[example : example + 1, :] > 0) & (positions < lengths_ref[example])
        turned = jnp.where(live, rounded.astype(f32).T, 0.0).astype(bf16)
        turned_ref[example] = turned
        products = jnp.dot(turned, rounded, preferred_element_type=f32)
        total = products if total is None else total + products
    lane = lax.broadcasted_iota(jnp.int32, (rank, 2 * rank), 1)
    factor_ref[...] = jnp.where(lane < rank, total[:rank, :], total[rank:, :])


def factors(lengths, mask, own, received):
    tokens, width = own.shape
    examples, seq_len = mask.shape
    return pl.pallas_call(
        functools.partial(factors_body, len(received)),
        out_shape=(
            jax.ShapeDtypeStruct((width // 2, width), f32),
            jax.ShapeDtypeStruct((tokens, width), bf16),
            jax.ShapeDtypeStruct((examples, width, seq_len), bf16),
        ),
        in_specs=[SMEM, VMEM, VMEM] + [VMEM] * len(received),
        out_specs=(VMEM, VMEM, VMEM),
        compiler_params=pltpu.CompilerParams(vmem_limit_bytes=4 * MIB),
        name="factors",
    )(lengths, mask, own, *received)


def features_body(lengths_ref, rounded_ref, turned_ref, feats_ref):
    half, rank, _ = feats_ref.shape
    examples, _, seq_len = turned_ref.shape
    lane = lax.broadcasted_iota(jnp.int32, (rank, 2 * rank), 1)

    def features(example):
        products = jnp.dot(
            turned_ref[example, rank:, :], rounded_ref[pl.ds(example * seq_len, seq_len), :], preferred_element_type=f32
        )
        return products / lengths_ref[example].astype(f32)

    for pair in range(half):
        other = pltpu.roll(features(half + pair), rank, 1)
        feats_ref[pair] = jnp.where(lane < rank, features(pair), other).astype(bf16)


def features_of(lengths, rounded, turned):
    examples, width, seq_len = turned.shape
    return pl.pallas_call(
        features_body,
        out_shape=jax.ShapeDtypeStruct((examples // 2, width // 2, width), bf16),
        in_specs=[SMEM, VMEM, VMEM],
        out_specs=VMEM,
        compiler_params=pltpu.CompilerParams(vmem_limit_bytes=4 * MIB),
        cost_estimate=pl.CostEstimate(flops=2 * examples * seq_len * width * width, bytes_accessed=8 * MIB, transcendentals=0),
        name="features",
    )(lengths, rounded, turned)


def split(values):
    high = values.astype(bf16)
    return high, (values - high.astype(f32)).astype(bf16)


def invert(packed):
    rank, width = packed.shape
    run = 8
    blocks = [packed[run * r : run * (r + 1), :] for r in range(rank // run)]
    lane = lax.broadcasted_iota(jnp.int32, (run, width), 1)
    sub = lax.broadcasted_iota(jnp.int32, (run, width), 0)
    column = jnp.where(lane < rank, lane, lane - rank)
    base = jnp.where(lane < rank, 0, rank)

    def pick(values, at):
        return jnp.take_along_axis(values, base + at, axis=1)

    for p in range(len(blocks)):
        first = run * p
        rows = [jnp.broadcast_to(blocks[p][i : i + 1, :], (run, width)) for i in range(run)]
        entry = [[None] * run for _ in range(run)]
        for i in range(run):
            for j in range(i, run):
                entry[i][j] = entry[j][i] = pick(rows[i], first + j)
        columns = [[pick(block, first + j) for j in range(run)] for block in blocks]
        for j in range(0, run, 2):
            a, b, c = entry[j][j], entry[j][j + 1], entry[j + 1][j + 1]
            scale = 1.0 / (a * c - b * b)
            ia, ib, ic = c * scale, -(b * scale), a * scale
            at_first, at_second = column == first + j, column == first + j + 1
            low = jnp.where(at_first, ia, jnp.where(at_second, ib, ia * rows[j] + ib * rows[j + 1]))
            high = jnp.where(at_first, ib, jnp.where(at_second, ic, ib * rows[j] + ic * rows[j + 1]))
            later = range(j + 2, run)
            low_entry = {k: ia * entry[j][k] + ib * entry[j + 1][k] for k in later}
            high_entry = {k: ib * entry[j][k] + ic * entry[j + 1][k] for k in later}
            for i in range(run):
                if i in (j, j + 1):
                    continue
                from_low, from_high = entry[i][j], entry[i][j + 1]
                rows[i] = jnp.where(at_first | at_second, 0.0, rows[i]) - (from_low * low + from_high * high)
                for k in later:
                    if j + 1 < i and k < i:
                        entry[i][k] = entry[k][i]
                    else:
                        entry[i][k] = entry[i][k] - (from_low * low_entry[k] + from_high * high_entry[k])
            rows[j], rows[j + 1] = low, high
            for k in later:
                entry[j][k], entry[j + 1][k] = low_entry[k], high_entry[k]
        pivots = (column >= first) & (column < first + run)
        for r in range(len(blocks)):
            if r != p:
                terms = [columns[r][i] * rows[i] for i in range(run)]
                while len(terms) > 1:
                    terms = [terms[i] + terms[i + 1] for i in range(0, len(terms), 2)]
                blocks[r] = jnp.where(pivots, 0.0, blocks[r]) - terms[0]
        turned = rows[0]
        for i in range(1, run):
            turned = jnp.where(sub == i, rows[i], turned)
        blocks[p] = turned
    return jnp.concatenate(blocks, axis=0)


def inverses_body(total_tokens, factor_a_ref, factor_b_ref, grad_ref, in_ref):
    rank = factor_a_ref.shape[0]
    lane = lax.broadcasted_iota(jnp.int32, (rank, 2 * rank), 1)
    sub = lax.broadcasted_iota(jnp.int32, (rank, 2 * rank), 0)
    left = lane < rank
    column = jnp.where(left, lane, lane - rank)
    diagonal = column == sub
    packed = (factor_a_ref[...] + factor_b_ref[...]) / total_tokens
    on_diagonal = jnp.sum(jnp.where(diagonal, packed, 0.0), axis=0, keepdims=True)
    trace_in = jnp.sum(jnp.where(left[:1], on_diagonal, 0.0), axis=1, keepdims=True)
    trace_grad = jnp.sum(jnp.where(left[:1], 0.0, on_diagonal), axis=1, keepdims=True)
    damping = 0.1 * jnp.where(left[:1], trace_in, trace_grad) / rank + 1e-06
    packed = packed + jnp.where(diagonal, damping, 0.0)
    packed = invert(packed)
    twice = pltpu.roll(packed, rank, 1)
    grad_ref[0], grad_ref[1] = split(twice[:, :rank])
    in_ref[0, :rank, :], in_ref[1, :rank, :] = split(jnp.where(left, packed, 0.0))
    in_ref[0, rank:, :], in_ref[1, rank:, :] = split(jnp.where(left, 0.0, twice))


def inverses(total_tokens, factor_a, factor_b):
    rank, width = factor_a.shape
    return pl.pallas_call(
        functools.partial(inverses_body, total_tokens),
        out_shape=(
            jax.ShapeDtypeStruct((2, rank, rank), bf16),
            jax.ShapeDtypeStruct((2, width, width), bf16),
        ),
        in_specs=[VMEM, VMEM],
        out_specs=(VMEM, VMEM),
        compiler_params=pltpu.CompilerParams(vmem_limit_bytes=4 * MIB),
        cost_estimate=pl.CostEstimate(flops=0, bytes_accessed=0, transcendentals=0),
        name="inverses",
    )(factor_a, factor_b)


def pack_body(tests_ref, *out_refs):
    feat_count = len(out_refs)
    rows, width = tests_ref.shape
    fold, block = rows // feat_count, width // feat_count
    feat = lax.axis_index("feat")
    pieces = []
    for target in range(feat_count):
        columns = slice(target * block, (target + 1) * block)
        parts = [tests_ref[j * fold : (j + 1) * fold, columns] for j in range(feat_count)]
        pieces.append(jnp.concatenate(parts, axis=1))
    for mask, out_ref in enumerate(out_refs):
        piece = pieces[0]
        for target in range(1, feat_count):
            piece = jnp.where((feat ^ mask) == target, pieces[target], piece)
        out_ref[...] = piece


def pack(tests):
    rows, width = tests.shape
    feat_count = lax.axis_size("feat")
    return pl.pallas_call(
        pack_body,
        out_shape=[jax.ShapeDtypeStruct((rows // feat_count, width), bf16)] * feat_count,
        in_specs=[VMEM],
        out_specs=[VMEM] * feat_count,
        compiler_params=pltpu.CompilerParams(vmem_limit_bytes=8 * MIB),
        cost_estimate=pl.CostEstimate(flops=40960 * MIB, bytes_accessed=4 * MIB, transcendentals=0),
        name="pack",
    )(tests)


def scores_body(blocks, grad_ref, in_ref, *refs):
    feat_count = lax.axis_size("feat")
    feat = lax.axis_index("feat")
    pieces, refs = refs[: 4 * feat_count], refs[4 * feat_count :]
    feats_refs, out_refs, (solved_buf, line_buf) = refs[:blocks], refs[blocks : 2 * blocks], refs[2 * blocks :]
    rank = grad_ref.shape[1]
    pairs = [ref[i] for ref in feats_refs for i in range(ref.shape[0])]
    count = len(pairs)
    half = count // blocks
    fold, width = pieces[0].shape
    block = width // feat_count
    dot = functools.partial(jnp.dot, preferred_element_type=f32)
    for at in range(count):
        high, low = split(dot(grad_ref[0], pairs[at]) + dot(grad_ref[1], pairs[at]))
        solved_buf[at * rank : (at + 1) * rank, :] = dot(high, in_ref[0]) + dot(high, in_ref[1]) + dot(low, in_ref[0])
    lane = lax.broadcasted_iota(jnp.int32, (count, 2 * rank), 1)
    for g in range(0, rank, 2):
        low = solved_buf[pl.ds(g, count, stride=rank), :]
        high = solved_buf[pl.ds(g + 1, count, stride=rank), :]
        first = jnp.where(lane < rank, low, pltpu.roll(high, rank, 1))
        second = jnp.where(lane < rank, pltpu.roll(low, rank, 1), high)
        line = jnp.concatenate([first, second], axis=0).astype(bf16)
        step = min(fold, 2 * rank)
        for begin in range(0, 2 * rank, step):
            at = (g * rank + begin) // fold
            to = (g * rank + begin) % fold
            line_buf[at // feat_count, at % feat_count, :, to : to + step] = line[:, begin : begin + step]
    lines = []
    for mask in range(feat_count):
        owner = feat ^ mask
        lines.append(jnp.concatenate([line_buf[owner, j] for j in range(feat_count)], axis=0))
    is_first = lax.axis_index("test") == 0
    odd = lax.rem(lax.axis_index("dp"), 2)
    for dp_bit in range(2):
        parts = []
        for test_bit in range(2):
            at = (2 * dp_bit + test_bit) * feat_count
            total = dot(lines[0], pieces[at][...])
            for mask in range(1, feat_count):
                total = total + dot(lines[mask], pieces[at + mask][...])
            part = total[: 2 * count, :block]
            for j in range(1, feat_count):
                part = part + total[2 * count * j : 2 * count * (j + 1), block * j : block * (j + 1)]
            parts.append(part)
        both = jnp.concatenate(
            [jnp.where(is_first, parts[0], parts[1]), jnp.where(is_first, parts[1], parts[0])], axis=1
        )
        for at, out_ref in enumerate(out_refs):
            out_ref[odd ^ dp_bit, :half, :] = both[at * half : (at + 1) * half, :]
            out_ref[odd ^ dp_bit, half:, :] = both[count + at * half : count + (at + 1) * half, :]


def scores_of(grad, in_pair, pieces, feats):
    feat_count = lax.axis_size("feat")
    rank = grad.shape[1]
    fold, width = pieces[0].shape
    half = feats[0].shape[0]
    count = half * len(feats)
    return pl.pallas_call(
        functools.partial(scores_body, len(feats)),
        out_shape=[jax.ShapeDtypeStruct((2, 2 * half, 2 * width // feat_count), f32)] * len(feats),
        in_specs=[VMEM] * (2 + len(pieces) + len(feats)),
        out_specs=[VMEM] * len(feats),
        scratch_shapes=[
            pltpu.VMEM((count * rank, 2 * rank), f32),
            pltpu.VMEM((feat_count, feat_count, 2 * count, fold), bf16),
        ],
        compiler_params=pltpu.CompilerParams(vmem_limit_bytes=16 * MIB),
        name="scores",
    )(grad, in_pair, *pieces, *feats)


def finish_body(*refs):
    block_refs, out_ref = refs[:-1], refs[-1]
    count = len(block_refs)
    _, examples, width = block_refs[0].shape
    half = width // 2
    own = lax.div(lax.axis_index("dp"), 2)
    for place in range(count):
        for odd in range(2):
            block = block_refs[0][odd]
            for mask in range(1, count):
                block = jnp.where((own ^ mask) == place, block_refs[mask][odd], block)
            for test in range(2):
                rows = pl.ds(4 * place + 2 * odd + test, examples, stride=4 * count)
                out_ref[rows, :] = block[:, test * half : (test + 1) * half]


def finish(blocks):
    _, examples, width = blocks[0].shape
    queries = 4 * len(blocks)
    out = pl.pallas_call(
        finish_body,
        out_shape=jax.ShapeDtypeStruct((examples * queries, width // 2), f32),
        in_specs=[VMEM] * len(blocks),
        out_specs=VMEM,
        compiler_params=pltpu.CompilerParams(vmem_limit_bytes=4 * MIB),
        name="finish",
    )(*blocks)
    return out.reshape(examples, queries, width // 2)


def after(values, *others):
    return lax.optimization_barrier((values, *others))[0]


def on_device(train_inputs, train_grads, proj_in, proj_out, lengths, loss_mask, test_feats):
    examples, seq_len, in_width = train_inputs.shape
    out_width = train_grads.shape[2]
    tokens = examples * seq_len
    feat_count = lax.axis_size("feat")
    dp_count = lax.axis_size("dp")
    test_count = lax.axis_size("test")
    own_rows = test_feats.shape[1]
    x = train_inputs.reshape(tokens, in_width)
    g = train_grads.reshape(tokens, out_width)
    tests = test_feats.transpose(1, 2, 0).reshape(own_rows * test_feats.shape[2], test_feats.shape[0])
    cut = pack(tests)
    near = [cut[0]] + [xor_permute(cut[mask], "feat", mask) for mask in range(1, feat_count)]
    far = [xor_permute(near[0], "dp", 1)]
    own, sent = project(x, g, after(proj_in.T, cut[0]), proj_out.T, tokens // 3)
    far += [xor_permute(piece, "dp", 1) for piece in after(tuple(near[1:]), sent)]
    received = [xor_permute(sent, "feat", mask) for mask in range(1, feat_count)]
    shared = [xor_permute(piece, "test", 1) for piece in after(tuple(near), sent)]
    factor, rounded, turned = factors(lengths, loss_mask, own, received)
    feats = [features_of(lengths, rounded, turned)]
    even_masks = range(2, dp_count, 2)
    steps = [("test", 1)] + [("dp", m) for m in reversed(masks_of(dp_count))]
    sums = [factor]
    for axis, mask in steps:
        if len(sums) == 3:
            sums[-1] = after(sums[-1], *shared)
        if len(sums) == len(steps):
            sums[-1] = after(sums[-1], feats[0])
        other = xor_permute(sums[-1], axis, mask)
        sums.append(sums[-1] + other)
    pieces = near + shared + far + [xor_permute(piece, "test", 1) for piece in after(tuple(far), *(other,))]
    feats += [xor_permute(feats[0], "dp", mask) for mask in even_masks]
    total_tokens = float(tokens * dp_count * test_count)
    grad, in_pair = inverses(total_tokens, sums[-2], other)
    blocks = scores_of(grad, in_pair, pieces, feats)
    blocks = [blocks[0]] + [xor_permute(blocks[at + 1], "dp", mask) for at, mask in enumerate(even_masks)]
    return finish(blocks)


def solution(mesh):
    return jax.shard_map(
        on_device,
        mesh=mesh,
        in_specs=(
            P(("groups", "dp", "test"), None, "feat"),
            P(("groups", "dp", "test"), None, "feat"),
            P("feat", None),
            P("feat", None),
            P(("groups", "dp", "test")),
            P(("groups", "dp", "test"), None),
            P(("groups", "dp", "test"), "feat", None),
        ),
        out_specs=P(("groups", "dp", "test"), None, "feat"),
        check_vma=False,
    )
```

```python
import functools

import jax
import jax.numpy as jnp
from jax import lax
from jax.experimental import pallas as pl
from jax.experimental.pallas import tpu as pltpu
from jax.sharding import PartitionSpec as P

f32 = jnp.float32
bf16 = jnp.bfloat16
MIB = 1024 * 1024
NT = (((1,), (1,)), ((), ()))
VMEM = pl.BlockSpec(memory_space=pltpu.VMEM)
SMEM = pl.BlockSpec(memory_space=pltpu.SMEM)
ANY = pl.BlockSpec(memory_space=pl.ANY)
PROJECT_MIB = 48


def xor_permute(values, axis, mask):
    size = lax.axis_size(axis)
    return lax.ppermute(values, axis, [(i, i ^ mask) for i in range(size)])


def masks_of(size):
    masks, mask = [], 1
    while mask < size:
        masks.append(mask)
        mask *= 2
    return masks


def project_body(rows, x_ref, g_hbm, pin_ref, pout_ref, own_ref, sent_ref, g_buf, sems):
    steps = x_ref.shape[0] // rows
    rank = pin_ref.shape[0]

    def g_copy(step):
        begin = step * rows if isinstance(step, int) else pl.multiple_of(step * rows, rows)
        block = pl.ds(begin, rows)
        return pltpu.make_async_copy(g_hbm.at[block, :], g_buf.at[block, :], sems.at[step])

    for step in range(steps):
        g_copy(step).start()
    own_ref[:, :rank] = lax.dot_general(x_ref[...], pin_ref[...], NT, preferred_element_type=f32)

    @pl.loop(0, steps)
    def _(step):
        g_copy(step).wait()
        block = pl.ds(pl.multiple_of(step * rows, rows), rows)
        right = lax.dot_general(g_buf[block, :], pout_ref[...], NT, preferred_element_type=f32)
        both = jnp.concatenate([own_ref[block, :rank], right], axis=1)
        own_ref[block, :] = both
        sent_ref[block, :] = both.astype(bf16)


def project(x, g, pin, pout, rows):
    tokens, in_width = x.shape
    out_width = g.shape[1]
    rank = pin.shape[0]
    return pl.pallas_call(
        functools.partial(project_body, rows),
        out_shape=(
            jax.ShapeDtypeStruct((tokens, 2 * rank), f32),
            jax.ShapeDtypeStruct((tokens, 2 * rank), bf16),
        ),
        in_specs=[VMEM, ANY, VMEM, VMEM],
        out_specs=(VMEM, VMEM),
        scratch_shapes=[pltpu.VMEM(g.shape, bf16), pltpu.SemaphoreType.DMA((tokens // rows,))],
        compiler_params=pltpu.CompilerParams(vmem_limit_bytes=PROJECT_MIB * MIB),
        cost_estimate=pl.CostEstimate(
            flops=2 * tokens * (in_width + out_width) * rank,
            bytes_accessed=2 * (tokens + rank) * (in_width + out_width),
            transcendentals=0,
        ),
        name="project",
    )(x, g, pin, pout)


def fetch_body(values_ref, out_ref):
    out_ref[...] = values_ref[...]


def fetch(values):
    return pl.pallas_call(
        fetch_body,
        out_shape=jax.ShapeDtypeStruct(values.shape, values.dtype),
        in_specs=[VMEM],
        out_specs=VMEM,
        compiler_params=pltpu.CompilerParams(vmem_limit_bytes=4 * MIB),
        cost_estimate=pl.CostEstimate(flops=values.size, bytes_accessed=8 * values.size, transcendentals=0),
        name="fetch",
    )(values)


def slots_body(out_ref):
    out_ref[...] = lax.broadcasted_iota(jnp.int32, out_ref.shape, 1)


def slots(seq_len):
    return pl.pallas_call(
        slots_body,
        out_shape=jax.ShapeDtypeStruct((1, seq_len), jnp.int32),
        out_specs=VMEM,
        compiler_params=pltpu.CompilerParams(vmem_limit_bytes=MIB),
        cost_estimate=pl.CostEstimate(flops=40960 * MIB, bytes_accessed=4096, transcendentals=0),
        name="slots",
    )()


def factors_body(received, lengths_ref, positions_ref, mask_ref, own_ref, *refs):
    received_refs = refs[:received]
    factor_ref, rounded_ref, turned_ref = refs[received:]
    examples, seq_len = mask_ref.shape
    rank = factor_ref.shape[0]
    positions = positions_ref[...]
    total = None
    for example in range(examples):
        rows = pl.ds(example * seq_len, seq_len)
        summed = own_ref[rows, :]
        for ref in received_refs:
            summed = summed + ref[rows, :].astype(f32)
        rounded = summed.astype(bf16)
        rounded_ref[rows, :] = rounded
        live = (mask_ref[example : example + 1, :] > 0) & (positions < lengths_ref[example])
        turned = jnp.where(live, rounded.astype(f32).T, 0.0).astype(bf16)
        turned_ref[example] = turned
        products = jnp.dot(turned, rounded, preferred_element_type=f32)
        total = products if total is None else total + products
    lane = lax.broadcasted_iota(jnp.int32, (rank, 2 * rank), 1)
    factor_ref[...] = jnp.where(lane < rank, total[:rank, :], total[rank:, :])


def factors(lengths, positions, mask, own, received):
    tokens, width = own.shape
    examples, seq_len = mask.shape
    return pl.pallas_call(
        functools.partial(factors_body, len(received)),
        out_shape=(
            jax.ShapeDtypeStruct((width // 2, width), f32),
            jax.ShapeDtypeStruct((tokens, width), bf16),
            jax.ShapeDtypeStruct((examples, width, seq_len), bf16),
        ),
        in_specs=[SMEM, VMEM, VMEM, VMEM] + [VMEM] * len(received),
        out_specs=(VMEM, VMEM, VMEM),
        compiler_params=pltpu.CompilerParams(vmem_limit_bytes=4 * MIB),
        name="factors",
    )(lengths, positions, mask, own, *received)


def features_body(lengths_ref, rounded_ref, turned_ref, feats_ref):
    half, rank, _ = feats_ref.shape
    examples, _, seq_len = turned_ref.shape
    lane = lax.broadcasted_iota(jnp.int32, (rank, 2 * rank), 1)

    def features(example):
        products = jnp.dot(
            turned_ref[example, rank:, :], rounded_ref[pl.ds(example * seq_len, seq_len), :], preferred_element_type=f32
        )
        return products / lengths_ref[example].astype(f32)

    for pair in range(half):
        other = pltpu.roll(features(half + pair), rank, 1)
        feats_ref[pair] = jnp.where(lane < rank, features(pair), other).astype(bf16)


def features_of(lengths, rounded, turned):
    examples, width, seq_len = turned.shape
    return pl.pallas_call(
        features_body,
        out_shape=jax.ShapeDtypeStruct((examples // 2, width // 2, width), bf16),
        in_specs=[SMEM, VMEM, VMEM],
        out_specs=VMEM,
        compiler_params=pltpu.CompilerParams(vmem_limit_bytes=4 * MIB),
        cost_estimate=pl.CostEstimate(flops=2 * examples * seq_len * width * width, bytes_accessed=8 * MIB, transcendentals=0),
        name="features",
    )(lengths, rounded, turned)


def split(values):
    high = values.astype(bf16)
    return high, (values - high.astype(f32)).astype(bf16)


def invert(packed):
    rank, width = packed.shape
    run = 8
    blocks = [packed[run * r : run * (r + 1), :] for r in range(rank // run)]
    lane = lax.broadcasted_iota(jnp.int32, (run, width), 1)
    sub = lax.broadcasted_iota(jnp.int32, (run, width), 0)
    column = jnp.where(lane < rank, lane, lane - rank)
    base = jnp.where(lane < rank, 0, rank)

    def pick(values, at):
        return jnp.take_along_axis(values, base + at, axis=1)

    for p in range(len(blocks)):
        first = run * p
        rows = [jnp.broadcast_to(blocks[p][i : i + 1, :], (run, width)) for i in range(run)]
        entry = [[None] * run for _ in range(run)]
        for i in range(run):
            for j in range(i, run):
                entry[i][j] = entry[j][i] = pick(rows[i], first + j)
        columns = [[pick(block, first + j) for j in range(run)] for block in blocks]
        for j in range(0, run, 2):
            a, b, c = entry[j][j], entry[j][j + 1], entry[j + 1][j + 1]
            scale = 1.0 / (a * c - b * b)
            ia, ib, ic = c * scale, -(b * scale), a * scale
            at_first, at_second = column == first + j, column == first + j + 1
            low = jnp.where(at_first, ia, jnp.where(at_second, ib, ia * rows[j] + ib * rows[j + 1]))
            high = jnp.where(at_first, ib, jnp.where(at_second, ic, ib * rows[j] + ic * rows[j + 1]))
            later = range(j + 2, run)
            low_entry = {k: ia * entry[j][k] + ib * entry[j + 1][k] for k in later}
            high_entry = {k: ib * entry[j][k] + ic * entry[j + 1][k] for k in later}
            for i in range(run):
                if i in (j, j + 1):
                    continue
                from_low, from_high = entry[i][j], entry[i][j + 1]
                rows[i] = jnp.where(at_first | at_second, 0.0, rows[i]) - (from_low * low + from_high * high)
                for k in later:
                    if j + 1 < i and k < i:
                        entry[i][k] = entry[k][i]
                    else:
                        entry[i][k] = entry[i][k] - (from_low * low_entry[k] + from_high * high_entry[k])
            rows[j], rows[j + 1] = low, high
            for k in later:
                entry[j][k], entry[j + 1][k] = low_entry[k], high_entry[k]
        pivots = (column >= first) & (column < first + run)
        for r in range(len(blocks)):
            if r != p:
                terms = [columns[r][i] * rows[i] for i in range(run)]
                while len(terms) > 1:
                    terms = [terms[i] + terms[i + 1] for i in range(0, len(terms), 2)]
                blocks[r] = jnp.where(pivots, 0.0, blocks[r]) - terms[0]
        turned = rows[0]
        for i in range(1, run):
            turned = jnp.where(sub == i, rows[i], turned)
        blocks[p] = turned
    return jnp.concatenate(blocks, axis=0)


def inverses_body(total_tokens, factor_a_ref, factor_b_ref, grad_ref, in_ref):
    rank = factor_a_ref.shape[0]
    lane = lax.broadcasted_iota(jnp.int32, (rank, 2 * rank), 1)
    sub = lax.broadcasted_iota(jnp.int32, (rank, 2 * rank), 0)
    left = lane < rank
    column = jnp.where(left, lane, lane - rank)
    diagonal = column == sub
    packed = (factor_a_ref[...] + factor_b_ref[...]) / total_tokens
    on_diagonal = jnp.sum(jnp.where(diagonal, packed, 0.0), axis=0, keepdims=True)
    trace_in = jnp.sum(jnp.where(left[:1], on_diagonal, 0.0), axis=1, keepdims=True)
    trace_grad = jnp.sum(jnp.where(left[:1], 0.0, on_diagonal), axis=1, keepdims=True)
    damping = 0.1 * jnp.where(left[:1], trace_in, trace_grad) / rank + 1e-06
    packed = packed + jnp.where(diagonal, damping, 0.0)
    packed = invert(packed)
    twice = pltpu.roll(packed, rank, 1)
    grad_ref[0], grad_ref[1] = split(twice[:, :rank])
    in_ref[0, :rank, :], in_ref[1, :rank, :] = split(jnp.where(left, packed, 0.0))
    in_ref[0, rank:, :], in_ref[1, rank:, :] = split(jnp.where(left, 0.0, twice))


def inverses(total_tokens, factor_a, factor_b):
    rank, width = factor_a.shape
    return pl.pallas_call(
        functools.partial(inverses_body, total_tokens),
        out_shape=(
            jax.ShapeDtypeStruct((2, rank, rank), bf16),
            jax.ShapeDtypeStruct((2, width, width), bf16),
        ),
        in_specs=[VMEM, VMEM],
        out_specs=(VMEM, VMEM),
        compiler_params=pltpu.CompilerParams(vmem_limit_bytes=4 * MIB),
        cost_estimate=pl.CostEstimate(flops=0, bytes_accessed=0, transcendentals=0),
        name="inverses",
    )(factor_a, factor_b)


def pack_body(tests_ref, *out_refs):
    feat_count = len(out_refs)
    rows, width = tests_ref.shape
    fold, block = rows // feat_count, width // feat_count
    feat = lax.axis_index("feat")
    pieces = []
    for target in range(feat_count):
        columns = slice(target * block, (target + 1) * block)
        parts = [tests_ref[j * fold : (j + 1) * fold, columns] for j in range(feat_count)]
        pieces.append(jnp.concatenate(parts, axis=1))
    for mask, out_ref in enumerate(out_refs):
        piece = pieces[0]
        for target in range(1, feat_count):
            piece = jnp.where((feat ^ mask) == target, pieces[target], piece)
        out_ref[...] = piece


def pack(tests, flops):
    rows, width = tests.shape
    feat_count = lax.axis_size("feat")
    return pl.pallas_call(
        pack_body,
        out_shape=[jax.ShapeDtypeStruct((rows // feat_count, width), bf16)] * feat_count,
        in_specs=[VMEM],
        out_specs=[VMEM] * feat_count,
        compiler_params=pltpu.CompilerParams(vmem_limit_bytes=8 * MIB),
        cost_estimate=pl.CostEstimate(flops=flops, bytes_accessed=4 * MIB, transcendentals=0),
        name="pack",
    )(tests)


def scores_body(blocks, grad_ref, in_ref, *refs):
    feat_count = lax.axis_size("feat")
    feat = lax.axis_index("feat")
    pieces, refs = refs[: 4 * feat_count], refs[4 * feat_count :]
    feats_refs, out_refs, (solved_buf, line_buf) = refs[:blocks], refs[blocks : 2 * blocks], refs[2 * blocks :]
    rank = grad_ref.shape[1]
    pairs = [ref[i] for ref in feats_refs for i in range(ref.shape[0])]
    count = len(pairs)
    half = count // blocks
    fold, width = pieces[0].shape
    block = width // feat_count
    dot = functools.partial(jnp.dot, preferred_element_type=f32)
    for at in range(count):
        high, low = split(dot(grad_ref[0], pairs[at]) + dot(grad_ref[1], pairs[at]))
        solved_buf[at * rank : (at + 1) * rank, :] = dot(high, in_ref[0]) + dot(high, in_ref[1]) + dot(low, in_ref[0])
    lane = lax.broadcasted_iota(jnp.int32, (count, 2 * rank), 1)
    for g in range(0, rank, 2):
        low = solved_buf[pl.ds(g, count, stride=rank), :]
        high = solved_buf[pl.ds(g + 1, count, stride=rank), :]
        first = jnp.where(lane < rank, low, pltpu.roll(high, rank, 1))
        second = jnp.where(lane < rank, pltpu.roll(low, rank, 1), high)
        line = jnp.concatenate([first, second], axis=0).astype(bf16)
        step = min(fold, 2 * rank)
        for begin in range(0, 2 * rank, step):
            at = (g * rank + begin) // fold
            to = (g * rank + begin) % fold
            line_buf[at // feat_count, at % feat_count, :, to : to + step] = line[:, begin : begin + step]
    lines = []
    for mask in range(feat_count):
        owner = feat ^ mask
        lines.append(jnp.concatenate([line_buf[owner, j] for j in range(feat_count)], axis=0))
    is_first = lax.axis_index("test") == 0
    odd = lax.rem(lax.axis_index("dp"), 2)
    for dp_bit in range(2):
        parts = []
        for test_bit in range(2):
            at = (2 * dp_bit + test_bit) * feat_count
            total = dot(lines[0], pieces[at][...])
            for mask in range(1, feat_count):
                total = total + dot(lines[mask], pieces[at + mask][...])
            part = total[: 2 * count, :block]
            for j in range(1, feat_count):
                part = part + total[2 * count * j : 2 * count * (j + 1), block * j : block * (j + 1)]
            parts.append(part)
        both = jnp.concatenate(
            [jnp.where(is_first, parts[0], parts[1]), jnp.where(is_first, parts[1], parts[0])], axis=1
        )
        for at, out_ref in enumerate(out_refs):
            out_ref[odd ^ dp_bit, :half, :] = both[at * half : (at + 1) * half, :]
            out_ref[odd ^ dp_bit, half:, :] = both[count + at * half : count + (at + 1) * half, :]


def scores_of(grad, in_pair, pieces, feats):
    feat_count = lax.axis_size("feat")
    rank = grad.shape[1]
    fold, width = pieces[0].shape
    half = feats[0].shape[0]
    count = half * len(feats)
    return pl.pallas_call(
        functools.partial(scores_body, len(feats)),
        out_shape=[jax.ShapeDtypeStruct((2, 2 * half, 2 * width // feat_count), f32)] * len(feats),
        in_specs=[VMEM] * (2 + len(pieces) + len(feats)),
        out_specs=[VMEM] * len(feats),
        scratch_shapes=[
            pltpu.VMEM((count * rank, 2 * rank), f32),
            pltpu.VMEM((feat_count, feat_count, 2 * count, fold), bf16),
        ],
        compiler_params=pltpu.CompilerParams(vmem_limit_bytes=16 * MIB),
        name="scores",
    )(grad, in_pair, *pieces, *feats)


def finish_body(*refs):
    block_refs, out_ref = refs[:-1], refs[-1]
    count = len(block_refs)
    _, examples, width = block_refs[0].shape
    half = width // 2
    own = lax.div(lax.axis_index("dp"), 2)
    for place in range(count):
        for odd in range(2):
            block = block_refs[0][odd]
            for mask in range(1, count):
                block = jnp.where((own ^ mask) == place, block_refs[mask][odd], block)
            for test in range(2):
                rows = pl.ds(4 * place + 2 * odd + test, examples, stride=4 * count)
                out_ref[rows, :] = block[:, test * half : (test + 1) * half]


def finish(blocks):
    _, examples, width = blocks[0].shape
    queries = 4 * len(blocks)
    out = pl.pallas_call(
        finish_body,
        out_shape=jax.ShapeDtypeStruct((examples * queries, width // 2), f32),
        in_specs=[VMEM] * len(blocks),
        out_specs=VMEM,
        compiler_params=pltpu.CompilerParams(vmem_limit_bytes=4 * MIB),
        name="finish",
    )(*blocks)
    return out.reshape(examples, queries, width // 2)


def after(values, *others):
    return lax.optimization_barrier((values, *others))[0]


def on_device(train_inputs, train_grads, proj_in, proj_out, lengths, loss_mask, test_feats):
    examples, seq_len, in_width = train_inputs.shape
    out_width = train_grads.shape[2]
    tokens = examples * seq_len
    feat_count = lax.axis_size("feat")
    dp_count = lax.axis_size("dp")
    test_count = lax.axis_size("test")
    own_rows = test_feats.shape[1]
    x = train_inputs.reshape(tokens, in_width)
    g = train_grads.reshape(tokens, out_width)
    tests = test_feats.transpose(1, 2, 0).reshape(own_rows * test_feats.shape[2], test_feats.shape[0])
    positions = slots(seq_len)
    far_tests = xor_permute(tests, "dp", 1)
    own, sent = project(x, g, after(proj_in.T, positions), proj_out.T, tokens // 3)
    cut = pack(after(tests, sent), 4 * MIB)
    near = [cut[0]] + [xor_permute(cut[mask], "feat", mask) for mask in range(1, feat_count)]
    received = [xor_permute(sent, "feat", mask) for mask in range(1, feat_count)]
    cut = pack(after(far_tests, *(sent,)), 4 * MIB)
    far = [cut[0]] + [xor_permute(cut[mask], "feat", mask) for mask in range(1, feat_count)]
    factor, rounded, turned = factors(lengths, positions, loss_mask, own, received)
    feats = [features_of(lengths, rounded, turned)]
    even_masks = range(2, dp_count, 2)
    steps = [("test", 1)] + [("dp", m) for m in reversed(masks_of(dp_count))]
    sums = [factor]
    for axis, mask in steps:
        if len(sums) == len(steps):
            sums[-1] = after(sums[-1], feats[0])
        other = xor_permute(sums[-1], axis, mask)
        sums.append(sums[-1] + other)
    shared = [xor_permute(piece, "test", 1) for piece in after(tuple(near), *(sums[2],))]
    pieces = near + shared + far + [xor_permute(piece, "test", 1) for piece in after(tuple(far[:1]), *(other,))] + [xor_permute(piece, "test", 1) for piece in after(tuple(far[1:]), *(other,))]
    feats += [xor_permute(feats[0], "dp", mask) for mask in even_masks]
    total_tokens = float(tokens * dp_count * test_count)
    grad, in_pair = inverses(total_tokens, sums[-2], other)
    blocks = scores_of(grad, in_pair, pieces, feats)
    blocks = [blocks[0]] + [xor_permute(blocks[at + 1], "dp", mask) for at, mask in enumerate(even_masks)]
    return finish(blocks)


def solution(mesh):
    return jax.shard_map(
        on_device,
        mesh=mesh,
        in_specs=(
            P(("groups", "dp", "test"), None, "feat"),
            P(("groups", "dp", "test"), None, "feat"),
            P("feat", None),
            P("feat", None),
            P(("groups", "dp", "test")),
            P(("groups", "dp", "test"), None),
            P(("groups", "dp", "test"), "feat", None),
        ),
        out_specs=P(("groups", "dp", "test"), None, "feat"),
        check_vma=False,
    )
```

```python
import functools

import jax
import jax.numpy as jnp
from jax import lax
from jax.experimental import pallas as pl
from jax.experimental.pallas import tpu as pltpu
from jax.sharding import PartitionSpec as P

f32 = jnp.float32
bf16 = jnp.bfloat16
MIB = 1024 * 1024
NT = (((1,), (1,)), ((), ()))
VMEM = pl.BlockSpec(memory_space=pltpu.VMEM)
SMEM = pl.BlockSpec(memory_space=pltpu.SMEM)
ANY = pl.BlockSpec(memory_space=pl.ANY)
PROJECT_MIB = 48


def xor_permute(values, axis, mask):
    size = lax.axis_size(axis)
    return lax.ppermute(values, axis, [(i, i ^ mask) for i in range(size)])


def masks_of(size):
    masks, mask = [], 1
    while mask < size:
        masks.append(mask)
        mask *= 2
    return masks


def project_body(rows, x_ref, g_hbm, pin_ref, pout_ref, own_ref, sent_ref, g_buf, sems):
    steps = x_ref.shape[0] // rows
    rank = pin_ref.shape[0]

    def g_copy(step):
        begin = step * rows if isinstance(step, int) else pl.multiple_of(step * rows, rows)
        block = pl.ds(begin, rows)
        return pltpu.make_async_copy(g_hbm.at[block, :], g_buf.at[block, :], sems.at[step])

    for step in range(steps):
        g_copy(step).start()
    own_ref[:, :rank] = lax.dot_general(x_ref[...], pin_ref[...], NT, preferred_element_type=f32)

    @pl.loop(0, steps)
    def _(step):
        g_copy(step).wait()
        block = pl.ds(pl.multiple_of(step * rows, rows), rows)
        right = lax.dot_general(g_buf[block, :], pout_ref[...], NT, preferred_element_type=f32)
        both = jnp.concatenate([own_ref[block, :rank], right], axis=1)
        own_ref[block, :] = both
        sent_ref[block, :] = both.astype(bf16)


def project(x, g, pin, pout, rows):
    tokens, in_width = x.shape
    out_width = g.shape[1]
    rank = pin.shape[0]
    return pl.pallas_call(
        functools.partial(project_body, rows),
        out_shape=(
            jax.ShapeDtypeStruct((tokens, 2 * rank), f32),
            jax.ShapeDtypeStruct((tokens, 2 * rank), bf16),
        ),
        in_specs=[VMEM, ANY, VMEM, VMEM],
        out_specs=(VMEM, VMEM),
        scratch_shapes=[pltpu.VMEM(g.shape, bf16), pltpu.SemaphoreType.DMA((tokens // rows,))],
        compiler_params=pltpu.CompilerParams(vmem_limit_bytes=PROJECT_MIB * MIB),
        cost_estimate=pl.CostEstimate(
            flops=2 * tokens * (in_width + out_width) * rank,
            bytes_accessed=2 * (tokens + rank) * (in_width + out_width),
            transcendentals=0,
        ),
        name="project",
    )(x, g, pin, pout)


def fetch_body(values_ref, out_ref):
    out_ref[...] = values_ref[...]


def fetch(values):
    return pl.pallas_call(
        fetch_body,
        out_shape=jax.ShapeDtypeStruct(values.shape, values.dtype),
        in_specs=[VMEM],
        out_specs=VMEM,
        compiler_params=pltpu.CompilerParams(vmem_limit_bytes=4 * MIB),
        cost_estimate=pl.CostEstimate(flops=values.size, bytes_accessed=8 * values.size, transcendentals=0),
        name="fetch",
    )(values)


def slots_body(out_ref):
    out_ref[...] = lax.broadcasted_iota(jnp.int32, out_ref.shape, 1)


def slots(seq_len):
    return pl.pallas_call(
        slots_body,
        out_shape=jax.ShapeDtypeStruct((1, seq_len), jnp.int32),
        out_specs=VMEM,
        compiler_params=pltpu.CompilerParams(vmem_limit_bytes=MIB),
        cost_estimate=pl.CostEstimate(flops=40960 * MIB, bytes_accessed=4096, transcendentals=0),
        name="slots",
    )()


def factors_body(received, lengths_ref, positions_ref, mask_ref, own_ref, *refs):
    received_refs = refs[:received]
    factor_ref, rounded_ref, turned_ref = refs[received:]
    examples, seq_len = mask_ref.shape
    rank = factor_ref.shape[0]
    positions = positions_ref[...]
    total = None
    for example in range(examples):
        rows = pl.ds(example * seq_len, seq_len)
        summed = own_ref[rows, :]
        for ref in received_refs:
            summed = summed + ref[rows, :].astype(f32)
        rounded = summed.astype(bf16)
        rounded_ref[rows, :] = rounded
        live = (mask_ref[example : example + 1, :] > 0) & (positions < lengths_ref[example])
        turned = jnp.where(live, rounded.astype(f32).T, 0.0).astype(bf16)
        turned_ref[example] = turned
        products = jnp.dot(turned, rounded, preferred_element_type=f32)
        total = products if total is None else total + products
    lane = lax.broadcasted_iota(jnp.int32, (rank, 2 * rank), 1)
    factor_ref[...] = jnp.where(lane < rank, total[:rank, :], total[rank:, :])


def factors(lengths, positions, mask, own, received):
    tokens, width = own.shape
    examples, seq_len = mask.shape
    return pl.pallas_call(
        functools.partial(factors_body, len(received)),
        out_shape=(
            jax.ShapeDtypeStruct((width // 2, width), f32),
            jax.ShapeDtypeStruct((tokens, width), bf16),
            jax.ShapeDtypeStruct((examples, width, seq_len), bf16),
        ),
        in_specs=[SMEM, VMEM, VMEM, VMEM] + [VMEM] * len(received),
        out_specs=(VMEM, VMEM, VMEM),
        compiler_params=pltpu.CompilerParams(vmem_limit_bytes=4 * MIB),
        name="factors",
    )(lengths, positions, mask, own, *received)


def features_body(lengths_ref, rounded_ref, turned_ref, feats_ref):
    half, rank, _ = feats_ref.shape
    examples, _, seq_len = turned_ref.shape
    lane = lax.broadcasted_iota(jnp.int32, (rank, 2 * rank), 1)

    def features(example):
        products = jnp.dot(
            turned_ref[example, rank:, :], rounded_ref[pl.ds(example * seq_len, seq_len), :], preferred_element_type=f32
        )
        return products / lengths_ref[example].astype(f32)

    for pair in range(half):
        other = pltpu.roll(features(half + pair), rank, 1)
        feats_ref[pair] = jnp.where(lane < rank, features(pair), other).astype(bf16)


def features_of(lengths, rounded, turned):
    examples, width, seq_len = turned.shape
    return pl.pallas_call(
        features_body,
        out_shape=jax.ShapeDtypeStruct((examples // 2, width // 2, width), bf16),
        in_specs=[SMEM, VMEM, VMEM],
        out_specs=VMEM,
        compiler_params=pltpu.CompilerParams(vmem_limit_bytes=4 * MIB),
        cost_estimate=pl.CostEstimate(flops=2 * examples * seq_len * width * width, bytes_accessed=8 * MIB, transcendentals=0),
        name="features",
    )(lengths, rounded, turned)


def split(values):
    high = values.astype(bf16)
    return high, (values - high.astype(f32)).astype(bf16)


def invert(packed):
    rank, width = packed.shape
    run = 8
    blocks = [packed[run * r : run * (r + 1), :] for r in range(rank // run)]
    lane = lax.broadcasted_iota(jnp.int32, (run, width), 1)
    sub = lax.broadcasted_iota(jnp.int32, (run, width), 0)
    column = jnp.where(lane < rank, lane, lane - rank)
    base = jnp.where(lane < rank, 0, rank)

    def pick(values, at):
        return jnp.take_along_axis(values, base + at, axis=1)

    for p in range(len(blocks)):
        first = run * p
        rows = [jnp.broadcast_to(blocks[p][i : i + 1, :], (run, width)) for i in range(run)]
        entry = [[None] * run for _ in range(run)]
        for i in range(run):
            for j in range(i, run):
                entry[i][j] = entry[j][i] = pick(rows[i], first + j)
        columns = [[pick(block, first + j) for j in range(run)] for block in blocks]
        for j in range(0, run, 2):
            a, b, c = entry[j][j], entry[j][j + 1], entry[j + 1][j + 1]
            scale = 1.0 / (a * c - b * b)
            ia, ib, ic = c * scale, -(b * scale), a * scale
            at_first, at_second = column == first + j, column == first + j + 1
            low = jnp.where(at_first, ia, jnp.where(at_second, ib, ia * rows[j] + ib * rows[j + 1]))
            high = jnp.where(at_first, ib, jnp.where(at_second, ic, ib * rows[j] + ic * rows[j + 1]))
            later = range(j + 2, run)
            low_entry = {k: ia * entry[j][k] + ib * entry[j + 1][k] for k in later}
            high_entry = {k: ib * entry[j][k] + ic * entry[j + 1][k] for k in later}
            for i in range(run):
                if i in (j, j + 1):
                    continue
                from_low, from_high = entry[i][j], entry[i][j + 1]
                rows[i] = jnp.where(at_first | at_second, 0.0, rows[i]) - (from_low * low + from_high * high)
                for k in later:
                    if j + 1 < i and k < i:
                        entry[i][k] = entry[k][i]
                    else:
                        entry[i][k] = entry[i][k] - (from_low * low_entry[k] + from_high * high_entry[k])
            rows[j], rows[j + 1] = low, high
            for k in later:
                entry[j][k], entry[j + 1][k] = low_entry[k], high_entry[k]
        pivots = (column >= first) & (column < first + run)
        for r in range(len(blocks)):
            if r != p:
                terms = [columns[r][i] * rows[i] for i in range(run)]
                while len(terms) > 1:
                    terms = [terms[i] + terms[i + 1] for i in range(0, len(terms), 2)]
                blocks[r] = jnp.where(pivots, 0.0, blocks[r]) - terms[0]
        turned = rows[0]
        for i in range(1, run):
            turned = jnp.where(sub == i, rows[i], turned)
        blocks[p] = turned
    return jnp.concatenate(blocks, axis=0)


def inverses_body(total_tokens, factor_a_ref, factor_b_ref, grad_ref, in_ref):
    rank = factor_a_ref.shape[0]
    lane = lax.broadcasted_iota(jnp.int32, (rank, 2 * rank), 1)
    sub = lax.broadcasted_iota(jnp.int32, (rank, 2 * rank), 0)
    left = lane < rank
    column = jnp.where(left, lane, lane - rank)
    diagonal = column == sub
    packed = (factor_a_ref[...] + factor_b_ref[...]) / total_tokens
    on_diagonal = jnp.sum(jnp.where(diagonal, packed, 0.0), axis=0, keepdims=True)
    trace_in = jnp.sum(jnp.where(left[:1], on_diagonal, 0.0), axis=1, keepdims=True)
    trace_grad = jnp.sum(jnp.where(left[:1], 0.0, on_diagonal), axis=1, keepdims=True)
    damping = 0.1 * jnp.where(left[:1], trace_in, trace_grad) / rank + 1e-06
    packed = packed + jnp.where(diagonal, damping, 0.0)
    packed = invert(packed)
    twice = pltpu.roll(packed, rank, 1)
    grad_ref[0], grad_ref[1] = split(twice[:, :rank])
    in_ref[0, :rank, :], in_ref[1, :rank, :] = split(jnp.where(left, packed, 0.0))
    in_ref[0, rank:, :], in_ref[1, rank:, :] = split(jnp.where(left, 0.0, twice))


def inverses(total_tokens, factor_a, factor_b):
    rank, width = factor_a.shape
    return pl.pallas_call(
        functools.partial(inverses_body, total_tokens),
        out_shape=(
            jax.ShapeDtypeStruct((2, rank, rank), bf16),
            jax.ShapeDtypeStruct((2, width, width), bf16),
        ),
        in_specs=[VMEM, VMEM],
        out_specs=(VMEM, VMEM),
        compiler_params=pltpu.CompilerParams(vmem_limit_bytes=4 * MIB),
        cost_estimate=pl.CostEstimate(flops=16384 * MIB, bytes_accessed=0, transcendentals=0),
        name="inverses",
    )(factor_a, factor_b)


def pack_body(tests_ref, *out_refs):
    feat_count = len(out_refs)
    rows, width = tests_ref.shape
    fold, block = rows // feat_count, width // feat_count
    feat = lax.axis_index("feat")
    pieces = []
    for target in range(feat_count):
        columns = slice(target * block, (target + 1) * block)
        parts = [tests_ref[j * fold : (j + 1) * fold, columns] for j in range(feat_count)]
        pieces.append(jnp.concatenate(parts, axis=1))
    for mask, out_ref in enumerate(out_refs):
        piece = pieces[0]
        for target in range(1, feat_count):
            piece = jnp.where((feat ^ mask) == target, pieces[target], piece)
        out_ref[...] = piece


def pack(tests, flops):
    rows, width = tests.shape
    feat_count = lax.axis_size("feat")
    return pl.pallas_call(
        pack_body,
        out_shape=[jax.ShapeDtypeStruct((rows // feat_count, width), bf16)] * feat_count,
        in_specs=[VMEM],
        out_specs=[VMEM] * feat_count,
        compiler_params=pltpu.CompilerParams(vmem_limit_bytes=8 * MIB),
        cost_estimate=pl.CostEstimate(flops=flops, bytes_accessed=4 * MIB, transcendentals=0),
        name="pack",
    )(tests)


def scores_body(blocks, piece_counts, grad_ref, in_ref, *refs):
    feat_count = lax.axis_size("feat")
    feat = lax.axis_index("feat")
    counts, pieces = piece_counts, []
    for count in counts:
        rows = refs[0].shape[0] // count
        pieces += [refs[0].at[pl.ds(rows * i, rows), :] for i in range(count)]
        refs = refs[1:]
    feats_refs, out_refs, (solved_buf, line_buf) = refs[:blocks], refs[blocks : 2 * blocks], refs[2 * blocks :]
    rank = grad_ref.shape[1]
    pairs = [ref[i] for ref in feats_refs for i in range(ref.shape[0])]
    count = len(pairs)
    half = count // blocks
    fold, width = pieces[0].shape
    block = width // feat_count
    dot = functools.partial(jnp.dot, preferred_element_type=f32)
    for at in range(count):
        high, low = split(dot(grad_ref[0], pairs[at]) + dot(grad_ref[1], pairs[at]))
        solved_buf[at * rank : (at + 1) * rank, :] = dot(high, in_ref[0]) + dot(high, in_ref[1]) + dot(low, in_ref[0])
    lane = lax.broadcasted_iota(jnp.int32, (count, 2 * rank), 1)
    for g in range(0, rank, 2):
        low = solved_buf[pl.ds(g, count, stride=rank), :]
        high = solved_buf[pl.ds(g + 1, count, stride=rank), :]
        first = jnp.where(lane < rank, low, pltpu.roll(high, rank, 1))
        second = jnp.where(lane < rank, pltpu.roll(low, rank, 1), high)
        line = jnp.concatenate([first, second], axis=0).astype(bf16)
        step = min(fold, 2 * rank)
        for begin in range(0, 2 * rank, step):
            at = (g * rank + begin) // fold
            to = (g * rank + begin) % fold
            line_buf[at // feat_count, at % feat_count, :, to : to + step] = line[:, begin : begin + step]
    lines = []
    for mask in range(feat_count):
        owner = feat ^ mask
        lines.append(jnp.concatenate([line_buf[owner, j] for j in range(feat_count)], axis=0))
    is_first = lax.axis_index("test") == 0
    odd = lax.rem(lax.axis_index("dp"), 2)
    for dp_bit in range(2):
        parts = []
        for test_bit in range(2):
            at = (2 * dp_bit + test_bit) * feat_count
            total = dot(lines[0], pieces[at][...])
            for mask in range(1, feat_count):
                total = total + dot(lines[mask], pieces[at + mask][...])
            part = total[: 2 * count, :block]
            for j in range(1, feat_count):
                part = part + total[2 * count * j : 2 * count * (j + 1), block * j : block * (j + 1)]
            parts.append(part)
        both = jnp.concatenate(
            [jnp.where(is_first, parts[0], parts[1]), jnp.where(is_first, parts[1], parts[0])], axis=1
        )
        for at, out_ref in enumerate(out_refs):
            out_ref[odd ^ dp_bit, :half, :] = both[at * half : (at + 1) * half, :]
            out_ref[odd ^ dp_bit, half:, :] = both[count + at * half : count + (at + 1) * half, :]


def scores_of(grad, in_pair, pieces, piece_counts, feats):
    feat_count = lax.axis_size("feat")
    rank = grad.shape[1]
    fold, width = pieces[0].shape[0] // piece_counts[0], pieces[0].shape[1]
    half = feats[0].shape[0]
    count = half * len(feats)
    return pl.pallas_call(
        functools.partial(scores_body, len(feats), piece_counts),
        out_shape=[jax.ShapeDtypeStruct((2, 2 * half, 2 * width // feat_count), f32)] * len(feats),
        in_specs=[VMEM] * (2 + len(pieces) + len(feats)),
        out_specs=[VMEM] * len(feats),
        scratch_shapes=[
            pltpu.VMEM((count * rank, 2 * rank), f32),
            pltpu.VMEM((feat_count, feat_count, 2 * count, fold), bf16),
        ],
        compiler_params=pltpu.CompilerParams(vmem_limit_bytes=16 * MIB),
        name="scores",
    )(grad, in_pair, *pieces, *feats)


def finish_body(*refs):
    block_refs, out_ref = refs[:-1], refs[-1]
    count = len(block_refs)
    _, examples, width = block_refs[0].shape
    half = width // 2
    own = lax.div(lax.axis_index("dp"), 2)
    for place in range(count):
        for odd in range(2):
            block = block_refs[0][odd]
            for mask in range(1, count):
                block = jnp.where((own ^ mask) == place, block_refs[mask][odd], block)
            for test in range(2):
                rows = pl.ds(4 * place + 2 * odd + test, examples, stride=4 * count)
                out_ref[rows, :] = block[:, test * half : (test + 1) * half]


def finish(blocks):
    _, examples, width = blocks[0].shape
    queries = 4 * len(blocks)
    out = pl.pallas_call(
        finish_body,
        out_shape=jax.ShapeDtypeStruct((examples * queries, width // 2), f32),
        in_specs=[VMEM] * len(blocks),
        out_specs=VMEM,
        compiler_params=pltpu.CompilerParams(vmem_limit_bytes=4 * MIB),
        name="finish",
    )(*blocks)
    return out.reshape(examples, queries, width // 2)


def after(values, *others):
    return lax.optimization_barrier((values, *others))[0]


def on_device(train_inputs, train_grads, proj_in, proj_out, lengths, loss_mask, test_feats):
    examples, seq_len, in_width = train_inputs.shape
    out_width = train_grads.shape[2]
    tokens = examples * seq_len
    feat_count = lax.axis_size("feat")
    dp_count = lax.axis_size("dp")
    test_count = lax.axis_size("test")
    own_rows = test_feats.shape[1]
    x = train_inputs.reshape(tokens, in_width)
    g = train_grads.reshape(tokens, out_width)
    tests = test_feats.transpose(1, 2, 0).reshape(own_rows * test_feats.shape[2], test_feats.shape[0])
    positions = slots(seq_len)
    far_tests = xor_permute(tests, "dp", 1)
    own, sent = project(x, g, after(proj_in.T, positions), proj_out.T, tokens // 3)
    cut = pack(after(tests, sent), 4 * MIB)
    near = [cut[0]] + [xor_permute(cut[mask], "feat", mask) for mask in range(1, feat_count)]
    received = [xor_permute(sent, "feat", mask) for mask in range(1, feat_count)]
    cut = pack(after(far_tests, *(sent,)), 4 * MIB)
    far = [cut[0]] + [xor_permute(cut[mask], "feat", mask) for mask in range(1, feat_count)]
    factor, rounded, turned = factors(lengths, positions, loss_mask, own, received)
    feats = [features_of(lengths, rounded, turned)]
    even_masks = range(2, dp_count, 2)
    steps = [("test", 1)] + [("dp", m) for m in reversed(masks_of(dp_count))]
    sums = [factor]
    for axis, mask in steps:
        if len(sums) == len(steps):
            sums[-1] = after(sums[-1], feats[0])
        other = xor_permute(sums[-1], axis, mask)
        sums.append(sums[-1] + other)
    pieces, piece_counts = [], []
    pieces += near + [xor_permute(piece, "test", 1) for piece in after(tuple(near), *(sums[2],))]
    piece_counts += [1] * (2 * feat_count)
    pieces += far + [xor_permute(jnp.concatenate(after(tuple(far), *(other,)), axis=0), "test", 1)]
    piece_counts += [1] * feat_count + [feat_count]
    feats += [xor_permute(feats[0], "dp", mask) for mask in even_masks]
    total_tokens = float(tokens * dp_count * test_count)
    grad, in_pair = inverses(total_tokens, sums[-2], other)
    blocks = scores_of(grad, in_pair, pieces, piece_counts, feats)
    blocks = [blocks[0]] + [xor_permute(blocks[at + 1], "dp", mask) for at, mask in enumerate(even_masks)]
    return finish(blocks)


def solution(mesh):
    return jax.shard_map(
        on_device,
        mesh=mesh,
        in_specs=(
            P(("groups", "dp", "test"), None, "feat"),
            P(("groups", "dp", "test"), None, "feat"),
            P("feat", None),
            P("feat", None),
            P(("groups", "dp", "test")),
            P(("groups", "dp", "test"), None),
            P(("groups", "dp", "test"), "feat", None),
        ),
        out_specs=P(("groups", "dp", "test"), None, "feat"),
        check_vma=False,
    )
```

```python
import functools

import jax
import jax.numpy as jnp
from jax import lax
from jax.experimental import pallas as pl
from jax.experimental.pallas import tpu as pltpu
from jax.sharding import PartitionSpec as P

f32 = jnp.float32
bf16 = jnp.bfloat16
MIB = 1024 * 1024
NT = (((1,), (1,)), ((), ()))
VMEM = pl.BlockSpec(memory_space=pltpu.VMEM)
SMEM = pl.BlockSpec(memory_space=pltpu.SMEM)
ANY = pl.BlockSpec(memory_space=pl.ANY)
PROJECT_MIB = 48


def xor_permute(values, axis, mask):
    size = lax.axis_size(axis)
    return lax.ppermute(values, axis, [(i, i ^ mask) for i in range(size)])


def masks_of(size):
    masks, mask = [], 1
    while mask < size:
        masks.append(mask)
        mask *= 2
    return masks


def project_body(rows, x_ref, g_hbm, pin_ref, pout_ref, own_ref, sent_ref, g_buf, sems):
    steps = x_ref.shape[0] // rows
    rank = pin_ref.shape[0]

    def g_copy(step):
        begin = step * rows if isinstance(step, int) else pl.multiple_of(step * rows, rows)
        block = pl.ds(begin, rows)
        return pltpu.make_async_copy(g_hbm.at[block, :], g_buf.at[block, :], sems.at[step])

    for step in range(steps):
        g_copy(step).start()
    own_ref[:, :rank] = lax.dot_general(x_ref[...], pin_ref[...], NT, preferred_element_type=f32)

    @pl.loop(0, steps)
    def _(step):
        g_copy(step).wait()
        block = pl.ds(pl.multiple_of(step * rows, rows), rows)
        right = lax.dot_general(g_buf[block, :], pout_ref[...], NT, preferred_element_type=f32)
        both = jnp.concatenate([own_ref[block, :rank], right], axis=1)
        own_ref[block, :] = both
        sent_ref[block, :] = both.astype(bf16)


def project(x, g, pin, pout, rows):
    tokens, in_width = x.shape
    out_width = g.shape[1]
    rank = pin.shape[0]
    return pl.pallas_call(
        functools.partial(project_body, rows),
        out_shape=(
            jax.ShapeDtypeStruct((tokens, 2 * rank), f32),
            jax.ShapeDtypeStruct((tokens, 2 * rank), bf16),
        ),
        in_specs=[VMEM, ANY, VMEM, VMEM],
        out_specs=(VMEM, VMEM),
        scratch_shapes=[pltpu.VMEM(g.shape, bf16), pltpu.SemaphoreType.DMA((tokens // rows,))],
        compiler_params=pltpu.CompilerParams(vmem_limit_bytes=PROJECT_MIB * MIB),
        cost_estimate=pl.CostEstimate(
            flops=2 * tokens * (in_width + out_width) * rank,
            bytes_accessed=2 * (tokens + rank) * (in_width + out_width),
            transcendentals=0,
        ),
        name="project",
    )(x, g, pin, pout)


def fetch_body(values_ref, out_ref):
    out_ref[...] = values_ref[...]


def fetch(values):
    return pl.pallas_call(
        fetch_body,
        out_shape=jax.ShapeDtypeStruct(values.shape, values.dtype),
        in_specs=[VMEM],
        out_specs=VMEM,
        compiler_params=pltpu.CompilerParams(vmem_limit_bytes=4 * MIB),
        cost_estimate=pl.CostEstimate(flops=values.size, bytes_accessed=8 * values.size, transcendentals=0),
        name="fetch",
    )(values)


def slots_body(out_ref):
    out_ref[...] = lax.broadcasted_iota(jnp.int32, out_ref.shape, 1)


def slots(seq_len):
    return pl.pallas_call(
        slots_body,
        out_shape=jax.ShapeDtypeStruct((1, seq_len), jnp.int32),
        out_specs=VMEM,
        compiler_params=pltpu.CompilerParams(vmem_limit_bytes=MIB),
        cost_estimate=pl.CostEstimate(flops=40960 * MIB, bytes_accessed=4096, transcendentals=0),
        name="slots",
    )()


def factors_body(received, lengths_ref, positions_ref, mask_ref, own_ref, *refs):
    received_refs = refs[:received]
    factor_ref, rounded_ref, turned_ref = refs[received:]
    examples, seq_len = mask_ref.shape
    rank = factor_ref.shape[0]
    positions = positions_ref[...]
    total = None
    for example in range(examples):
        rows = pl.ds(example * seq_len, seq_len)
        summed = own_ref[rows, :]
        for ref in received_refs:
            summed = summed + ref[rows, :].astype(f32)
        rounded = summed.astype(bf16)
        rounded_ref[rows, :] = rounded
        live = (mask_ref[example : example + 1, :] > 0) & (positions < lengths_ref[example])
        turned = jnp.where(live, rounded.astype(f32).T, 0.0).astype(bf16)
        turned_ref[example] = turned
        products = jnp.dot(turned, rounded, preferred_element_type=f32)
        total = products if total is None else total + products
    lane = lax.broadcasted_iota(jnp.int32, (rank, 2 * rank), 1)
    factor_ref[...] = jnp.where(lane < rank, total[:rank, :], total[rank:, :])


def factors(lengths, positions, mask, own, received):
    tokens, width = own.shape
    examples, seq_len = mask.shape
    return pl.pallas_call(
        functools.partial(factors_body, len(received)),
        out_shape=(
            jax.ShapeDtypeStruct((width // 2, width), f32),
            jax.ShapeDtypeStruct((tokens, width), bf16),
            jax.ShapeDtypeStruct((examples, width, seq_len), bf16),
        ),
        in_specs=[SMEM, VMEM, VMEM, VMEM] + [VMEM] * len(received),
        out_specs=(VMEM, VMEM, VMEM),
        compiler_params=pltpu.CompilerParams(vmem_limit_bytes=4 * MIB),
        name="factors",
    )(lengths, positions, mask, own, *received)


def features_body(lengths_ref, rounded_ref, turned_ref, feats_ref):
    half, rank, _ = feats_ref.shape
    examples, _, seq_len = turned_ref.shape
    lane = lax.broadcasted_iota(jnp.int32, (rank, 2 * rank), 1)

    def features(example):
        products = jnp.dot(
            turned_ref[example, rank:, :], rounded_ref[pl.ds(example * seq_len, seq_len), :], preferred_element_type=f32
        )
        return products / lengths_ref[example].astype(f32)

    for pair in range(half):
        other = pltpu.roll(features(half + pair), rank, 1)
        feats_ref[pair] = jnp.where(lane < rank, features(pair), other).astype(bf16)


def features_of(lengths, rounded, turned):
    examples, width, seq_len = turned.shape
    return pl.pallas_call(
        features_body,
        out_shape=jax.ShapeDtypeStruct((examples // 2, width // 2, width), bf16),
        in_specs=[SMEM, VMEM, VMEM],
        out_specs=VMEM,
        compiler_params=pltpu.CompilerParams(vmem_limit_bytes=4 * MIB),
        cost_estimate=pl.CostEstimate(flops=2 * examples * seq_len * width * width, bytes_accessed=8 * MIB, transcendentals=0),
        name="features",
    )(lengths, rounded, turned)


def split(values):
    high = values.astype(bf16)
    return high, (values - high.astype(f32)).astype(bf16)


def invert(packed):
    rank, width = packed.shape
    run = 8
    blocks = [packed[run * r : run * (r + 1), :] for r in range(rank // run)]
    lane = lax.broadcasted_iota(jnp.int32, (run, width), 1)
    sub = lax.broadcasted_iota(jnp.int32, (run, width), 0)
    column = jnp.where(lane < rank, lane, lane - rank)
    base = jnp.where(lane < rank, 0, rank)

    def pick(values, at):
        return jnp.take_along_axis(values, base + at, axis=1)

    for p in range(len(blocks)):
        first = run * p
        rows = [jnp.broadcast_to(blocks[p][i : i + 1, :], (run, width)) for i in range(run)]
        entry = [[None] * run for _ in range(run)]
        for i in range(run):
            for j in range(i, run):
                entry[i][j] = entry[j][i] = pick(rows[i], first + j)
        columns = [[pick(block, first + j) for j in range(run)] for block in blocks]
        for j in range(0, run, 2):
            a, b, c = entry[j][j], entry[j][j + 1], entry[j + 1][j + 1]
            scale = 1.0 / (a * c - b * b)
            ia, ib, ic = c * scale, -(b * scale), a * scale
            at_first, at_second = column == first + j, column == first + j + 1
            low = jnp.where(at_first, ia, jnp.where(at_second, ib, ia * rows[j] + ib * rows[j + 1]))
            high = jnp.where(at_first, ib, jnp.where(at_second, ic, ib * rows[j] + ic * rows[j + 1]))
            later = range(j + 2, run)
            low_entry = {k: ia * entry[j][k] + ib * entry[j + 1][k] for k in later}
            high_entry = {k: ib * entry[j][k] + ic * entry[j + 1][k] for k in later}
            for i in range(run):
                if i in (j, j + 1):
                    continue
                from_low, from_high = entry[i][j], entry[i][j + 1]
                rows[i] = jnp.where(at_first | at_second, 0.0, rows[i]) - (from_low * low + from_high * high)
                for k in later:
                    if j + 1 < i and k < i:
                        entry[i][k] = entry[k][i]
                    else:
                        entry[i][k] = entry[i][k] - (from_low * low_entry[k] + from_high * high_entry[k])
            rows[j], rows[j + 1] = low, high
            for k in later:
                entry[j][k], entry[j + 1][k] = low_entry[k], high_entry[k]
        pivots = (column >= first) & (column < first + run)
        for r in range(len(blocks)):
            if r != p:
                terms = [columns[r][i] * rows[i] for i in range(run)]
                while len(terms) > 1:
                    terms = [terms[i] + terms[i + 1] for i in range(0, len(terms), 2)]
                blocks[r] = jnp.where(pivots, 0.0, blocks[r]) - terms[0]
        turned = rows[0]
        for i in range(1, run):
            turned = jnp.where(sub == i, rows[i], turned)
        blocks[p] = turned
    return jnp.concatenate(blocks, axis=0)


def inverses_body(total_tokens, factor_a_ref, factor_b_ref, grad_ref, in_ref):
    rank = factor_a_ref.shape[0]
    lane = lax.broadcasted_iota(jnp.int32, (rank, 2 * rank), 1)
    sub = lax.broadcasted_iota(jnp.int32, (rank, 2 * rank), 0)
    left = lane < rank
    column = jnp.where(left, lane, lane - rank)
    diagonal = column == sub
    packed = (factor_a_ref[...] + factor_b_ref[...]) / total_tokens
    on_diagonal = jnp.sum(jnp.where(diagonal, packed, 0.0), axis=0, keepdims=True)
    trace_in = jnp.sum(jnp.where(left[:1], on_diagonal, 0.0), axis=1, keepdims=True)
    trace_grad = jnp.sum(jnp.where(left[:1], 0.0, on_diagonal), axis=1, keepdims=True)
    damping = 0.1 * jnp.where(left[:1], trace_in, trace_grad) / rank + 1e-06
    packed = packed + jnp.where(diagonal, damping, 0.0)
    packed = invert(packed)
    twice = pltpu.roll(packed, rank, 1)
    grad_ref[0], grad_ref[1] = split(twice[:, :rank])
    in_ref[0, :rank, :], in_ref[1, :rank, :] = split(jnp.where(left, packed, 0.0))
    in_ref[0, rank:, :], in_ref[1, rank:, :] = split(jnp.where(left, 0.0, twice))


def inverses(total_tokens, factor_a, factor_b):
    rank, width = factor_a.shape
    return pl.pallas_call(
        functools.partial(inverses_body, total_tokens),
        out_shape=(
            jax.ShapeDtypeStruct((2, rank, rank), bf16),
            jax.ShapeDtypeStruct((2, width, width), bf16),
        ),
        in_specs=[VMEM, VMEM],
        out_specs=(VMEM, VMEM),
        compiler_params=pltpu.CompilerParams(vmem_limit_bytes=4 * MIB),
        cost_estimate=pl.CostEstimate(flops=16384 * MIB, bytes_accessed=0, transcendentals=0),
        name="inverses",
    )(factor_a, factor_b)


def pack_body(tests_ref, *out_refs):
    feat_count = len(out_refs)
    rows, width = tests_ref.shape
    fold, block = rows // feat_count, width // feat_count
    feat = lax.axis_index("feat")
    pieces = []
    for target in range(feat_count):
        columns = slice(target * block, (target + 1) * block)
        parts = [tests_ref[j * fold : (j + 1) * fold, columns] for j in range(feat_count)]
        pieces.append(jnp.concatenate(parts, axis=1))
    for mask, out_ref in enumerate(out_refs):
        piece = pieces[0]
        for target in range(1, feat_count):
            piece = jnp.where((feat ^ mask) == target, pieces[target], piece)
        out_ref[...] = piece


def pack(tests, flops):
    rows, width = tests.shape
    feat_count = lax.axis_size("feat")
    return pl.pallas_call(
        pack_body,
        out_shape=[jax.ShapeDtypeStruct((rows // feat_count, width), bf16)] * feat_count,
        in_specs=[VMEM],
        out_specs=[VMEM] * feat_count,
        compiler_params=pltpu.CompilerParams(vmem_limit_bytes=8 * MIB),
        cost_estimate=pl.CostEstimate(flops=flops, bytes_accessed=4 * MIB, transcendentals=0),
        name="pack",
    )(tests)


def scores_body(blocks, piece_counts, grad_ref, in_ref, *refs):
    feat_count = lax.axis_size("feat")
    feat = lax.axis_index("feat")
    counts, pieces = piece_counts, []
    for count in counts:
        rows = refs[0].shape[0] // count
        pieces += [refs[0].at[pl.ds(rows * i, rows), :] for i in range(count)]
        refs = refs[1:]
    feats_refs, out_refs, (solved_buf, line_buf) = refs[:blocks], refs[blocks : 2 * blocks], refs[2 * blocks :]
    rank = grad_ref.shape[1]
    pairs = [ref[i] for ref in feats_refs for i in range(ref.shape[0])]
    count = len(pairs)
    half = count // blocks
    fold, width = pieces[0].shape
    block = width // feat_count
    dot = functools.partial(jnp.dot, preferred_element_type=f32)
    for at in range(count):
        high, low = split(dot(grad_ref[0], pairs[at]) + dot(grad_ref[1], pairs[at]))
        solved_buf[at * rank : (at + 1) * rank, :] = dot(high, in_ref[0]) + dot(high, in_ref[1]) + dot(low, in_ref[0])
    lane = lax.broadcasted_iota(jnp.int32, (count, 2 * rank), 1)
    for g in range(0, rank, 2):
        low = solved_buf[pl.ds(g, count, stride=rank), :]
        high = solved_buf[pl.ds(g + 1, count, stride=rank), :]
        first = jnp.where(lane < rank, low, pltpu.roll(high, rank, 1))
        second = jnp.where(lane < rank, pltpu.roll(low, rank, 1), high)
        line = jnp.concatenate([first, second], axis=0).astype(bf16)
        step = min(fold, 2 * rank)
        for begin in range(0, 2 * rank, step):
            at = (g * rank + begin) // fold
            to = (g * rank + begin) % fold
            line_buf[at // feat_count, at % feat_count, :, to : to + step] = line[:, begin : begin + step]
    lines = []
    for mask in range(feat_count):
        owner = feat ^ mask
        lines.append(jnp.concatenate([line_buf[owner, j] for j in range(feat_count)], axis=0))
    is_first = lax.axis_index("test") == 0
    odd = lax.rem(lax.axis_index("dp"), 2)
    for dp_bit in range(2):
        parts = []
        for test_bit in range(2):
            at = (2 * dp_bit + test_bit) * feat_count
            total = dot(lines[0], pieces[at][...])
            for mask in range(1, feat_count):
                total = total + dot(lines[mask], pieces[at + mask][...])
            part = total[: 2 * count, :block]
            for j in range(1, feat_count):
                part = part + total[2 * count * j : 2 * count * (j + 1), block * j : block * (j + 1)]
            parts.append(part)
        both = jnp.concatenate(
            [jnp.where(is_first, parts[0], parts[1]), jnp.where(is_first, parts[1], parts[0])], axis=1
        )
        for at, out_ref in enumerate(out_refs):
            out_ref[odd ^ dp_bit, :half, :] = both[at * half : (at + 1) * half, :]
            out_ref[odd ^ dp_bit, half:, :] = both[count + at * half : count + (at + 1) * half, :]


def scores_of(grad, in_pair, pieces, piece_counts, feats):
    feat_count = lax.axis_size("feat")
    rank = grad.shape[1]
    fold, width = pieces[0].shape[0] // piece_counts[0], pieces[0].shape[1]
    half = feats[0].shape[0]
    count = half * len(feats)
    return pl.pallas_call(
        functools.partial(scores_body, len(feats), piece_counts),
        out_shape=[jax.ShapeDtypeStruct((2, 2 * half, 2 * width // feat_count), f32)] * len(feats),
        in_specs=[VMEM] * (2 + len(pieces) + len(feats)),
        out_specs=[VMEM] * len(feats),
        scratch_shapes=[
            pltpu.VMEM((count * rank, 2 * rank), f32),
            pltpu.VMEM((feat_count, feat_count, 2 * count, fold), bf16),
        ],
        compiler_params=pltpu.CompilerParams(vmem_limit_bytes=16 * MIB),
        name="scores",
    )(grad, in_pair, *pieces, *feats)


def finish_body(*refs):
    block_refs, out_ref = refs[:-1], refs[-1]
    count = len(block_refs)
    _, examples, width = block_refs[0].shape
    half = width // 2
    own = lax.div(lax.axis_index("dp"), 2)
    for place in range(count):
        for odd in range(2):
            block = block_refs[0][odd]
            for mask in range(1, count):
                block = jnp.where((own ^ mask) == place, block_refs[mask][odd], block)
            for test in range(2):
                rows = pl.ds(4 * place + 2 * odd + test, examples, stride=4 * count)
                out_ref[rows, :] = block[:, test * half : (test + 1) * half]


def finish(blocks):
    _, examples, width = blocks[0].shape
    queries = 4 * len(blocks)
    out = pl.pallas_call(
        finish_body,
        out_shape=jax.ShapeDtypeStruct((examples * queries, width // 2), f32),
        in_specs=[VMEM] * len(blocks),
        out_specs=VMEM,
        compiler_params=pltpu.CompilerParams(vmem_limit_bytes=4 * MIB),
        name="finish",
    )(*blocks)
    return out.reshape(examples, queries, width // 2)


def after(values, *others):
    return lax.optimization_barrier((values, *others))[0]


def on_device(train_inputs, train_grads, proj_in, proj_out, lengths, loss_mask, test_feats):
    examples, seq_len, in_width = train_inputs.shape
    out_width = train_grads.shape[2]
    tokens = examples * seq_len
    feat_count = lax.axis_size("feat")
    dp_count = lax.axis_size("dp")
    test_count = lax.axis_size("test")
    own_rows = test_feats.shape[1]
    x = train_inputs.reshape(tokens, in_width)
    g = train_grads.reshape(tokens, out_width)
    tests = test_feats.transpose(1, 2, 0).reshape(own_rows * test_feats.shape[2], test_feats.shape[0])
    positions = slots(seq_len)
    far_tests = xor_permute(tests, "dp", 1)
    own, sent = project(x, g, after(proj_in.T, positions), proj_out.T, tokens // 3)
    cut = pack(after(tests, sent), 4 * MIB)
    near = [cut[0]] + [xor_permute(cut[mask], "feat", mask) for mask in range(1, feat_count)]
    received = [xor_permute(sent, "feat", mask) for mask in range(1, feat_count)]
    cut = pack(after(far_tests, *(sent,)), 4 * MIB)
    far = [cut[0]] + [xor_permute(cut[mask], "feat", mask) for mask in range(1, feat_count)]
    factor, rounded, turned = factors(lengths, positions, loss_mask, own, received)
    feats = [features_of(lengths, rounded, turned)]
    even_masks = range(2, dp_count, 2)
    steps = [("test", 1)] + [("dp", m) for m in reversed(masks_of(dp_count))]
    sums = [factor]
    for axis, mask in steps:
        if len(sums) == len(steps):
            sums[-1] = after(sums[-1], feats[0])
        other = xor_permute(sums[-1], axis, mask)
        sums.append(sums[-1] + other)
    pieces, piece_counts = [], []
    pieces += near + [xor_permute(piece, "test", 1) for piece in after(tuple(near), *(sums[2],))]
    piece_counts += [1] * (2 * feat_count)
    pieces += far + [xor_permute(jnp.concatenate(after(tuple(far), *(sums[2],)), axis=0), "test", 1)]
    piece_counts += [1] * feat_count + [feat_count]
    feats += [xor_permute(feats[0], "dp", mask) for mask in even_masks]
    total_tokens = float(tokens * dp_count * test_count)
    grad, in_pair = inverses(total_tokens, sums[-2], other)
    pieces = list(lax.optimization_barrier(tuple(pieces)))
    blocks = scores_of(grad, in_pair, pieces, piece_counts, feats)
    blocks = [blocks[0]] + [xor_permute(blocks[at + 1], "dp", mask) for at, mask in enumerate(even_masks)]
    return finish(blocks)


def solution(mesh):
    return jax.shard_map(
        on_device,
        mesh=mesh,
        in_specs=(
            P(("groups", "dp", "test"), None, "feat"),
            P(("groups", "dp", "test"), None, "feat"),
            P("feat", None),
            P("feat", None),
            P(("groups", "dp", "test")),
            P(("groups", "dp", "test"), None),
            P(("groups", "dp", "test"), "feat", None),
        ),
        out_specs=P(("groups", "dp", "test"), None, "feat"),
        check_vma=False,
    )
```

```python
import functools

import jax
import jax.numpy as jnp
from jax import lax
from jax.experimental import pallas as pl
from jax.experimental.pallas import tpu as pltpu
from jax.sharding import PartitionSpec as P

f32 = jnp.float32
bf16 = jnp.bfloat16
MIB = 1024 * 1024
NT = (((1,), (1,)), ((), ()))
VMEM = pl.BlockSpec(memory_space=pltpu.VMEM)
SMEM = pl.BlockSpec(memory_space=pltpu.SMEM)
ANY = pl.BlockSpec(memory_space=pl.ANY)
PROJECT_MIB = 40


def xor_permute(values, axis, mask):
    size = lax.axis_size(axis)
    return lax.ppermute(values, axis, [(i, i ^ mask) for i in range(size)])


def masks_of(size):
    masks, mask = [], 1
    while mask < size:
        masks.append(mask)
        mask *= 2
    return masks


def project_first_body(step, x_ref, g_hbm, pin_ref, pout_ref, own_ref, sent_ref, left_ref, g_ref, g_buf, sems):
    rows, rank = own_ref.shape[0], pin_ref.shape[0]

    def g_copy(at):
        begin = at * step if isinstance(at, int) else pl.multiple_of(at * step, step)
        block = pl.ds(begin, step)
        return pltpu.make_async_copy(g_hbm.at[block, :], g_buf.at[block, :], sems.at[at])

    for at in range(rows // step):
        g_copy(at).start()
    others = pltpu.make_async_copy(g_hbm.at[pl.ds(rows, g_ref.shape[0]), :], g_ref, sems.at[rows // step])
    others.start()
    left = lax.dot_general(x_ref[...], pin_ref[...], NT, preferred_element_type=f32)
    own_ref[:, :rank] = left[:rows, :]
    left_ref[...] = left[rows:, :]

    @pl.loop(0, rows // step)
    def _(at):
        g_copy(at).wait()
        block = pl.ds(pl.multiple_of(at * step, step), step)
        right = lax.dot_general(g_buf[block, :], pout_ref[...], NT, preferred_element_type=f32)
        both = jnp.concatenate([own_ref[block, :rank], right], axis=1)
        own_ref[block, :] = both
        sent_ref[block, :] = both.astype(bf16)

    others.wait()


def project_first(x, g, pin, pout, rows, step):
    tokens, in_width = x.shape
    out_width = g.shape[1]
    rank = pin.shape[0]
    return pl.pallas_call(
        functools.partial(project_first_body, step),
        out_shape=(
            jax.ShapeDtypeStruct((rows, 2 * rank), f32),
            jax.ShapeDtypeStruct((rows, 2 * rank), bf16),
            jax.ShapeDtypeStruct((tokens - rows, rank), f32),
            jax.ShapeDtypeStruct((tokens - rows, out_width), bf16),
        ),
        in_specs=[VMEM, ANY, VMEM, VMEM],
        out_specs=[VMEM] * 4,
        scratch_shapes=[pltpu.VMEM((rows, out_width), bf16), pltpu.SemaphoreType.DMA((rows // step + 1,))],
        compiler_params=pltpu.CompilerParams(vmem_limit_bytes=PROJECT_MIB * MIB),
        cost_estimate=pl.CostEstimate(
            flops=2 * rows * (in_width + out_width) * rank,
            bytes_accessed=2 * (tokens + rank) * (in_width + out_width),
            transcendentals=0,
        ),
        name="project_first",
    )(x, g, pin, pout)


def project_last_body(left_ref, g_ref, pout_ref, own_ref, sent_ref):
    right = lax.dot_general(g_ref[...], pout_ref[...], NT, preferred_element_type=f32)
    both = jnp.concatenate([left_ref[...], right], axis=1)
    own_ref[...] = both
    sent_ref[...] = both.astype(bf16)


def project_last(left, g, pout):
    rows, out_width = g.shape
    rank = pout.shape[0]
    return pl.pallas_call(
        project_last_body,
        out_shape=(
            jax.ShapeDtypeStruct((rows, 2 * rank), f32),
            jax.ShapeDtypeStruct((rows, 2 * rank), bf16),
        ),
        in_specs=[VMEM] * 3,
        out_specs=[VMEM] * 2,
        compiler_params=pltpu.CompilerParams(vmem_limit_bytes=16 * MIB),
        cost_estimate=pl.CostEstimate(
            flops=2 * rows * out_width * rank, bytes_accessed=2 * (rows + rank) * out_width, transcendentals=0
        ),
        name="project_last",
    )(left, g, pout)


def slots_body(out_ref):
    out_ref[...] = lax.broadcasted_iota(jnp.int32, out_ref.shape, 1)


def slots(seq_len):
    return pl.pallas_call(
        slots_body,
        out_shape=jax.ShapeDtypeStruct((1, seq_len), jnp.int32),
        out_specs=VMEM,
        compiler_params=pltpu.CompilerParams(vmem_limit_bytes=MIB),
        cost_estimate=pl.CostEstimate(flops=40960 * MIB, bytes_accessed=4096, transcendentals=0),
        name="slots",
    )()


def factors_body(parts, lengths_ref, positions_ref, mask_ref, *refs):
    part_refs = [refs[i * len(refs[:-3]) // parts : (i + 1) * len(refs[:-3]) // parts] for i in range(parts)]
    factor_ref, rounded_ref, turned_ref = refs[-3:]
    examples, seq_len = mask_ref.shape
    rank = factor_ref.shape[0]
    positions = positions_ref[...]
    total = None
    begins = [sum(refs_of[0].shape[0] for refs_of in part_refs[:i]) for i in range(parts)]
    for example in range(examples):
        rows = pl.ds(example * seq_len, seq_len)
        part = max(i for i in range(parts) if begins[i] <= example * seq_len)
        place = pl.ds(example * seq_len - begins[part], seq_len)
        summed = part_refs[part][0][place, :]
        for ref in part_refs[part][1:]:
            summed = summed + ref[place, :].astype(f32)
        rounded = summed.astype(bf16)
        rounded_ref[rows, :] = rounded
        live = (mask_ref[example : example + 1, :] > 0) & (positions < lengths_ref[example])
        turned = jnp.where(live, rounded.astype(f32).T, 0.0).astype(bf16)
        turned_ref[example] = turned
        products = jnp.dot(turned, rounded, preferred_element_type=f32)
        total = products if total is None else total + products
    lane = lax.broadcasted_iota(jnp.int32, (rank, 2 * rank), 1)
    factor_ref[...] = jnp.where(lane < rank, total[:rank, :], total[rank:, :])


def factors(lengths, positions, mask, parts):
    width = parts[0][0].shape[1]
    examples, seq_len = mask.shape
    values = [value for part in parts for value in part]
    return pl.pallas_call(
        functools.partial(factors_body, len(parts)),
        out_shape=(
            jax.ShapeDtypeStruct((width // 2, width), f32),
            jax.ShapeDtypeStruct((examples * seq_len, width), bf16),
            jax.ShapeDtypeStruct((examples, width, seq_len), bf16),
        ),
        in_specs=[SMEM, VMEM, VMEM] + [VMEM] * len(values),
        out_specs=(VMEM, VMEM, VMEM),
        compiler_params=pltpu.CompilerParams(vmem_limit_bytes=4 * MIB),
        name="factors",
    )(lengths, positions, mask, *values)


def features_body(lengths_ref, rounded_ref, turned_ref, feats_ref):
    half, rank, _ = feats_ref.shape
    examples, _, seq_len = turned_ref.shape
    lane = lax.broadcasted_iota(jnp.int32, (rank, 2 * rank), 1)

    def features(example):
        products = jnp.dot(
            turned_ref[example, rank:, :], rounded_ref[pl.ds(example * seq_len, seq_len), :], preferred_element_type=f32
        )
        return products / lengths_ref[example].astype(f32)

    for pair in range(half):
        other = pltpu.roll(features(half + pair), rank, 1)
        feats_ref[pair] = jnp.where(lane < rank, features(pair), other).astype(bf16)


def features_of(lengths, rounded, turned):
    examples, width, seq_len = turned.shape
    return pl.pallas_call(
        features_body,
        out_shape=jax.ShapeDtypeStruct((examples // 2, width // 2, width), bf16),
        in_specs=[SMEM, VMEM, VMEM],
        out_specs=VMEM,
        compiler_params=pltpu.CompilerParams(vmem_limit_bytes=4 * MIB),
        cost_estimate=pl.CostEstimate(flops=2 * examples * seq_len * width * width, bytes_accessed=8 * MIB, transcendentals=0),
        name="features",
    )(lengths, rounded, turned)


def split(values):
    high = values.astype(bf16)
    return high, (values - high.astype(f32)).astype(bf16)


def invert(packed):
    rank, width = packed.shape
    run = 8
    blocks = [packed[run * r : run * (r + 1), :] for r in range(rank // run)]
    lane = lax.broadcasted_iota(jnp.int32, (run, width), 1)
    sub = lax.broadcasted_iota(jnp.int32, (run, width), 0)
    column = jnp.where(lane < rank, lane, lane - rank)
    base = jnp.where(lane < rank, 0, rank)

    def pick(values, at):
        return jnp.take_along_axis(values, base + at, axis=1)

    for p in range(len(blocks)):
        first = run * p
        rows = [jnp.broadcast_to(blocks[p][i : i + 1, :], (run, width)) for i in range(run)]
        entry = [[None] * run for _ in range(run)]
        for i in range(run):
            for j in range(i, run):
                entry[i][j] = entry[j][i] = pick(rows[i], first + j)
        columns = [[pick(block, first + j) for j in range(run)] for block in blocks]
        for j in range(0, run, 2):
            a, b, c = entry[j][j], entry[j][j + 1], entry[j + 1][j + 1]
            scale = 1.0 / (a * c - b * b)
            ia, ib, ic = c * scale, -(b * scale), a * scale
            at_first, at_second = column == first + j, column == first + j + 1
            low = jnp.where(at_first, ia, jnp.where(at_second, ib, ia * rows[j] + ib * rows[j + 1]))
            high = jnp.where(at_first, ib, jnp.where(at_second, ic, ib * rows[j] + ic * rows[j + 1]))
            later = range(j + 2, run)
            low_entry = {k: ia * entry[j][k] + ib * entry[j + 1][k] for k in later}
            high_entry = {k: ib * entry[j][k] + ic * entry[j + 1][k] for k in later}
            for i in range(run):
                if i in (j, j + 1):
                    continue
                from_low, from_high = entry[i][j], entry[i][j + 1]
                rows[i] = jnp.where(at_first | at_second, 0.0, rows[i]) - (from_low * low + from_high * high)
                for k in later:
                    if j + 1 < i and k < i:
                        entry[i][k] = entry[k][i]
                    else:
                        entry[i][k] = entry[i][k] - (from_low * low_entry[k] + from_high * high_entry[k])
            rows[j], rows[j + 1] = low, high
            for k in later:
                entry[j][k], entry[j + 1][k] = low_entry[k], high_entry[k]
        pivots = (column >= first) & (column < first + run)
        for r in range(len(blocks)):
            if r != p:
                terms = [columns[r][i] * rows[i] for i in range(run)]
                while len(terms) > 1:
                    terms = [terms[i] + terms[i + 1] for i in range(0, len(terms), 2)]
                blocks[r] = jnp.where(pivots, 0.0, blocks[r]) - terms[0]
        turned = rows[0]
        for i in range(1, run):
            turned = jnp.where(sub == i, rows[i], turned)
        blocks[p] = turned
    return jnp.concatenate(blocks, axis=0)


def inverses_body(total_tokens, factor_a_ref, factor_b_ref, grad_ref, in_ref):
    rank = factor_a_ref.shape[0]
    lane = lax.broadcasted_iota(jnp.int32, (rank, 2 * rank), 1)
    sub = lax.broadcasted_iota(jnp.int32, (rank, 2 * rank), 0)
    left = lane < rank
    column = jnp.where(left, lane, lane - rank)
    diagonal = column == sub
    packed = (factor_a_ref[...] + factor_b_ref[...]) / total_tokens
    on_diagonal = jnp.sum(jnp.where(diagonal, packed, 0.0), axis=0, keepdims=True)
    trace_in = jnp.sum(jnp.where(left[:1], on_diagonal, 0.0), axis=1, keepdims=True)
    trace_grad = jnp.sum(jnp.where(left[:1], 0.0, on_diagonal), axis=1, keepdims=True)
    damping = 0.1 * jnp.where(left[:1], trace_in, trace_grad) / rank + 1e-06
    packed = packed + jnp.where(diagonal, damping, 0.0)
    packed = invert(packed)
    twice = pltpu.roll(packed, rank, 1)
    grad_ref[0], grad_ref[1] = split(twice[:, :rank])
    in_ref[0, :rank, :], in_ref[1, :rank, :] = split(jnp.where(left, packed, 0.0))
    in_ref[0, rank:, :], in_ref[1, rank:, :] = split(jnp.where(left, 0.0, twice))


def inverses(total_tokens, factor_a, factor_b):
    rank, width = factor_a.shape
    return pl.pallas_call(
        functools.partial(inverses_body, total_tokens),
        out_shape=(
            jax.ShapeDtypeStruct((2, rank, rank), bf16),
            jax.ShapeDtypeStruct((2, width, width), bf16),
        ),
        in_specs=[VMEM, VMEM],
        out_specs=(VMEM, VMEM),
        compiler_params=pltpu.CompilerParams(vmem_limit_bytes=4 * MIB),
        cost_estimate=pl.CostEstimate(flops=16384 * MIB, bytes_accessed=0, transcendentals=0),
        name="inverses",
    )(factor_a, factor_b)


def pack_body(tests_ref, *out_refs):
    feat_count = len(out_refs)
    rows, width = tests_ref.shape
    fold, block = rows // feat_count, width // feat_count
    feat = lax.axis_index("feat")
    pieces = []
    for target in range(feat_count):
        columns = slice(target * block, (target + 1) * block)
        parts = [tests_ref[j * fold : (j + 1) * fold, columns] for j in range(feat_count)]
        pieces.append(jnp.concatenate(parts, axis=1))
    for mask, out_ref in enumerate(out_refs):
        piece = pieces[0]
        for target in range(1, feat_count):
            piece = jnp.where((feat ^ mask) == target, pieces[target], piece)
        out_ref[...] = piece


def pack(tests, flops):
    rows, width = tests.shape
    feat_count = lax.axis_size("feat")
    return pl.pallas_call(
        pack_body,
        out_shape=[jax.ShapeDtypeStruct((rows // feat_count, width), bf16)] * feat_count,
        in_specs=[VMEM],
        out_specs=[VMEM] * feat_count,
        compiler_params=pltpu.CompilerParams(vmem_limit_bytes=8 * MIB),
        cost_estimate=pl.CostEstimate(flops=flops, bytes_accessed=4 * MIB, transcendentals=0),
        name="pack",
    )(tests)


def scores_body(blocks, piece_counts, grad_ref, in_ref, *refs):
    feat_count = lax.axis_size("feat")
    feat = lax.axis_index("feat")
    counts, pieces = piece_counts, []
    for count in counts:
        rows = refs[0].shape[0] // count
        pieces += [refs[0].at[pl.ds(rows * i, rows), :] for i in range(count)]
        refs = refs[1:]
    feats_refs, out_refs, (solved_buf, line_buf) = refs[:blocks], refs[blocks : 2 * blocks], refs[2 * blocks :]
    rank = grad_ref.shape[1]
    pairs = [ref[i] for ref in feats_refs for i in range(ref.shape[0])]
    count = len(pairs)
    half = count // blocks
    fold, width = pieces[0].shape
    block = width // feat_count
    dot = functools.partial(jnp.dot, preferred_element_type=f32)
    for at in range(count):
        high, low = split(dot(grad_ref[0], pairs[at]) + dot(grad_ref[1], pairs[at]))
        solved_buf[at * rank : (at + 1) * rank, :] = dot(high, in_ref[0]) + dot(high, in_ref[1]) + dot(low, in_ref[0])
    lane = lax.broadcasted_iota(jnp.int32, (count, 2 * rank), 1)
    for g in range(0, rank, 2):
        low = solved_buf[pl.ds(g, count, stride=rank), :]
        high = solved_buf[pl.ds(g + 1, count, stride=rank), :]
        first = jnp.where(lane < rank, low, pltpu.roll(high, rank, 1))
        second = jnp.where(lane < rank, pltpu.roll(low, rank, 1), high)
        line = jnp.concatenate([first, second], axis=0).astype(bf16)
        step = min(fold, 2 * rank)
        for begin in range(0, 2 * rank, step):
            at = (g * rank + begin) // fold
            to = (g * rank + begin) % fold
            line_buf[at // feat_count, at % feat_count, :, to : to + step] = line[:, begin : begin + step]
    lines = []
    for mask in range(feat_count):
        owner = feat ^ mask
        lines.append(jnp.concatenate([line_buf[owner, j] for j in range(feat_count)], axis=0))
    is_first = lax.axis_index("test") == 0
    odd = lax.rem(lax.axis_index("dp"), 2)
    for dp_bit in range(2):
        parts = []
        for test_bit in range(2):
            at = (2 * dp_bit + test_bit) * feat_count
            total = dot(lines[0], pieces[at][...])
            for mask in range(1, feat_count):
                total = total + dot(lines[mask], pieces[at + mask][...])
            part = total[: 2 * count, :block]
            for j in range(1, feat_count):
                part = part + total[2 * count * j : 2 * count * (j + 1), block * j : block * (j + 1)]
            parts.append(part)
        both = jnp.concatenate(
            [jnp.where(is_first, parts[0], parts[1]), jnp.where(is_first, parts[1], parts[0])], axis=1
        )
        for at, out_ref in enumerate(out_refs):
            out_ref[odd ^ dp_bit, :half, :] = both[at * half : (at + 1) * half, :]
            out_ref[odd ^ dp_bit, half:, :] = both[count + at * half : count + (at + 1) * half, :]


def scores_of(grad, in_pair, pieces, piece_counts, feats):
    feat_count = lax.axis_size("feat")
    rank = grad.shape[1]
    fold, width = pieces[0].shape[0] // piece_counts[0], pieces[0].shape[1]
    half = feats[0].shape[0]
    count = half * len(feats)
    return pl.pallas_call(
        functools.partial(scores_body, len(feats), piece_counts),
        out_shape=[jax.ShapeDtypeStruct((2, 2 * half, 2 * width // feat_count), f32)] * len(feats),
        in_specs=[VMEM] * (2 + len(pieces) + len(feats)),
        out_specs=[VMEM] * len(feats),
        scratch_shapes=[
            pltpu.VMEM((count * rank, 2 * rank), f32),
            pltpu.VMEM((feat_count, feat_count, 2 * count, fold), bf16),
        ],
        compiler_params=pltpu.CompilerParams(vmem_limit_bytes=16 * MIB),
        name="scores",
    )(grad, in_pair, *pieces, *feats)


def finish_body(*refs):
    block_refs, out_ref = refs[:-1], refs[-1]
    count = len(block_refs)
    _, examples, width = block_refs[0].shape
    half = width // 2
    own = lax.div(lax.axis_index("dp"), 2)
    for place in range(count):
        for odd in range(2):
            block = block_refs[0][odd]
            for mask in range(1, count):
                block = jnp.where((own ^ mask) == place, block_refs[mask][odd], block)
            for test in range(2):
                rows = pl.ds(4 * place + 2 * odd + test, examples, stride=4 * count)
                out_ref[rows, :] = block[:, test * half : (test + 1) * half]


def finish(blocks):
    _, examples, width = blocks[0].shape
    queries = 4 * len(blocks)
    out = pl.pallas_call(
        finish_body,
        out_shape=jax.ShapeDtypeStruct((examples * queries, width // 2), f32),
        in_specs=[VMEM] * len(blocks),
        out_specs=VMEM,
        compiler_params=pltpu.CompilerParams(vmem_limit_bytes=4 * MIB),
        name="finish",
    )(*blocks)
    return out.reshape(examples, queries, width // 2)


def after(values, *others):
    return lax.optimization_barrier((values, *others))[0]


def on_device(train_inputs, train_grads, proj_in, proj_out, lengths, loss_mask, test_feats):
    examples, seq_len, in_width = train_inputs.shape
    out_width = train_grads.shape[2]
    tokens = examples * seq_len
    feat_count = lax.axis_size("feat")
    dp_count = lax.axis_size("dp")
    test_count = lax.axis_size("test")
    own_rows = test_feats.shape[1]
    x = train_inputs.reshape(tokens, in_width)
    g = train_grads.reshape(tokens, out_width)
    tests = test_feats.transpose(1, 2, 0).reshape(own_rows * test_feats.shape[2], test_feats.shape[0])
    positions = slots(seq_len)
    far_tests = xor_permute(tests, "dp", 1)
    first = seq_len * ((5 * examples) // 8)
    own, sent, left, others = project_first(x, g, after(proj_in.T, positions), proj_out.T, first, first // 2)
    owns, sents = [own], [sent]
    own, sent = project_last(left, others, proj_out.T)
    owns.append(own)
    sents.append(sent)
    parts = [
        [own] + [xor_permute(sent, "feat", mask) for mask in range(1, feat_count)] for own, sent in zip(owns, sents)
    ]
    cut = pack(after(tests, sent), 4 * MIB)
    near = [cut[0]] + [xor_permute(cut[mask], "feat", mask) for mask in range(1, feat_count)]
    factor, rounded, turned = factors(lengths, positions, loss_mask, parts)
    cut = pack(after(far_tests, *(factor,)), 4 * MIB)
    far = [cut[0]] + [xor_permute(cut[mask], "feat", mask) for mask in range(1, feat_count)]
    feats = [features_of(lengths, rounded, turned)]
    even_masks = range(2, dp_count, 2)
    steps = [("test", 1)] + [("dp", m) for m in reversed(masks_of(dp_count))]
    sums = [factor]
    for axis, mask in steps:
        if len(sums) == len(steps):
            sums[-1] = after(sums[-1], feats[0])
        other = xor_permute(sums[-1], axis, mask)
        sums.append(sums[-1] + other)
    pieces, piece_counts = [], []
    pieces += near + [xor_permute(piece, "test", 1) for piece in after(tuple(near), *(sums[2],))]
    piece_counts += [1] * (2 * feat_count)
    pieces += far + [xor_permute(jnp.concatenate(after(tuple(far), *(sums[2],)), axis=0), "test", 1)]
    piece_counts += [1] * feat_count + [feat_count]
    feats += [xor_permute(feats[0], "dp", mask) for mask in even_masks]
    total_tokens = float(tokens * dp_count * test_count)
    grad, in_pair = inverses(total_tokens, sums[-2], other)
    pieces = list(lax.optimization_barrier(tuple(pieces)))
    blocks = scores_of(grad, in_pair, pieces, piece_counts, feats)
    blocks = [blocks[0]] + [xor_permute(blocks[at + 1], "dp", mask) for at, mask in enumerate(even_masks)]
    return finish(blocks)


def solution(mesh):
    return jax.shard_map(
        on_device,
        mesh=mesh,
        in_specs=(
            P(("groups", "dp", "test"), None, "feat"),
            P(("groups", "dp", "test"), None, "feat"),
            P("feat", None),
            P("feat", None),
            P(("groups", "dp", "test")),
            P(("groups", "dp", "test"), None),
            P(("groups", "dp", "test"), "feat", None),
        ),
        out_specs=P(("groups", "dp", "test"), None, "feat"),
        check_vma=False,
    )
```

```python
import functools

import jax
import jax.numpy as jnp
from jax import lax
from jax.experimental import pallas as pl
from jax.experimental.pallas import tpu as pltpu
from jax.sharding import PartitionSpec as P

f32 = jnp.float32
bf16 = jnp.bfloat16
MIB = 1024 * 1024
NT = (((1,), (1,)), ((), ()))
VMEM = pl.BlockSpec(memory_space=pltpu.VMEM)
SMEM = pl.BlockSpec(memory_space=pltpu.SMEM)
ANY = pl.BlockSpec(memory_space=pl.ANY)
PROJECT_MIB = 48


def xor_permute(values, axis, mask):
    size = lax.axis_size(axis)
    return lax.ppermute(values, axis, [(i, i ^ mask) for i in range(size)])


def masks_of(size):
    masks, mask = [], 1
    while mask < size:
        masks.append(mask)
        mask *= 2
    return masks


def project_body(rows, x_ref, g_hbm, pin_ref, pout_ref, own_ref, sent_ref, g_buf, sems):
    steps = x_ref.shape[0] // rows
    rank = pin_ref.shape[0]

    def g_copy(step):
        begin = step * rows if isinstance(step, int) else pl.multiple_of(step * rows, rows)
        block = pl.ds(begin, rows)
        return pltpu.make_async_copy(g_hbm.at[block, :], g_buf.at[block, :], sems.at[step])

    for step in range(steps):
        g_copy(step).start()
    own_ref[:, :rank] = lax.dot_general(x_ref[...], pin_ref[...], NT, preferred_element_type=f32)

    @pl.loop(0, steps)
    def _(step):
        g_copy(step).wait()
        block = pl.ds(pl.multiple_of(step * rows, rows), rows)
        right = lax.dot_general(g_buf[block, :], pout_ref[...], NT, preferred_element_type=f32)
        both = jnp.concatenate([own_ref[block, :rank], right], axis=1)
        own_ref[block, :] = both
        sent_ref[block, :] = both.astype(bf16)


def project(x, g, pin, pout, rows):
    tokens, in_width = x.shape
    out_width = g.shape[1]
    rank = pin.shape[0]
    return pl.pallas_call(
        functools.partial(project_body, rows),
        out_shape=(
            jax.ShapeDtypeStruct((tokens, 2 * rank), f32),
            jax.ShapeDtypeStruct((tokens, 2 * rank), bf16),
        ),
        in_specs=[VMEM, ANY, VMEM, VMEM],
        out_specs=(VMEM, VMEM),
        scratch_shapes=[pltpu.VMEM(g.shape, bf16), pltpu.SemaphoreType.DMA((tokens // rows,))],
        compiler_params=pltpu.CompilerParams(vmem_limit_bytes=PROJECT_MIB * MIB),
        cost_estimate=pl.CostEstimate(
            flops=2 * tokens * (in_width + out_width) * rank,
            bytes_accessed=2 * (tokens + rank) * (in_width + out_width),
            transcendentals=0,
        ),
        name="project",
    )(x, g, pin, pout)


def fetch_body(values_ref, out_ref):
    out_ref[...] = values_ref[...]


def fetch(values):
    return pl.pallas_call(
        fetch_body,
        out_shape=jax.ShapeDtypeStruct(values.shape, values.dtype),
        in_specs=[VMEM],
        out_specs=VMEM,
        compiler_params=pltpu.CompilerParams(vmem_limit_bytes=4 * MIB),
        cost_estimate=pl.CostEstimate(flops=values.size, bytes_accessed=8 * values.size, transcendentals=0),
        name="fetch",
    )(values)


def slots_body(out_ref):
    out_ref[...] = lax.broadcasted_iota(jnp.int32, out_ref.shape, 1)


def slots(seq_len):
    return pl.pallas_call(
        slots_body,
        out_shape=jax.ShapeDtypeStruct((1, seq_len), jnp.int32),
        out_specs=VMEM,
        compiler_params=pltpu.CompilerParams(vmem_limit_bytes=MIB),
        cost_estimate=pl.CostEstimate(flops=40960 * MIB, bytes_accessed=4096, transcendentals=0),
        name="slots",
    )()


def factors_body(received, lengths_ref, positions_ref, mask_ref, own_ref, *refs):
    received_refs = refs[:received]
    factor_ref, rounded_ref, turned_ref = refs[received:]
    examples, seq_len = mask_ref.shape
    rank = factor_ref.shape[0]
    positions = positions_ref[...]
    total = None
    for example in range(examples):
        rows = pl.ds(example * seq_len, seq_len)
        summed = own_ref[rows, :]
        for ref in received_refs:
            summed = summed + ref[rows, :].astype(f32)
        rounded = summed.astype(bf16)
        rounded_ref[rows, :] = rounded
        live = (mask_ref[example : example + 1, :] > 0) & (positions < lengths_ref[example])
        turned = jnp.where(live, rounded.astype(f32).T, 0.0).astype(bf16)
        turned_ref[example] = turned
        products = jnp.dot(turned, rounded, preferred_element_type=f32)
        total = products if total is None else total + products
    lane = lax.broadcasted_iota(jnp.int32, (rank, 2 * rank), 1)
    factor_ref[...] = jnp.where(lane < rank, total[:rank, :], total[rank:, :])


def factors(lengths, positions, mask, own, received):
    tokens, width = own.shape
    examples, seq_len = mask.shape
    return pl.pallas_call(
        functools.partial(factors_body, len(received)),
        out_shape=(
            jax.ShapeDtypeStruct((width // 2, width), f32),
            jax.ShapeDtypeStruct((tokens, width), bf16),
            jax.ShapeDtypeStruct((examples, width, seq_len), bf16),
        ),
        in_specs=[SMEM, VMEM, VMEM, VMEM] + [VMEM] * len(received),
        out_specs=(VMEM, VMEM, VMEM),
        compiler_params=pltpu.CompilerParams(vmem_limit_bytes=4 * MIB),
        name="factors",
    )(lengths, positions, mask, own, *received)


def features_body(lengths_ref, rounded_ref, turned_ref, feats_ref):
    half, rank, _ = feats_ref.shape
    examples, _, seq_len = turned_ref.shape
    lane = lax.broadcasted_iota(jnp.int32, (rank, 2 * rank), 1)

    def features(example):
        products = jnp.dot(
            turned_ref[example, rank:, :], rounded_ref[pl.ds(example * seq_len, seq_len), :], preferred_element_type=f32
        )
        return products / lengths_ref[example].astype(f32)

    for pair in range(half):
        other = pltpu.roll(features(half + pair), rank, 1)
        feats_ref[pair] = jnp.where(lane < rank, features(pair), other).astype(bf16)


def features_of(lengths, rounded, turned):
    examples, width, seq_len = turned.shape
    return pl.pallas_call(
        features_body,
        out_shape=jax.ShapeDtypeStruct((examples // 2, width // 2, width), bf16),
        in_specs=[SMEM, VMEM, VMEM],
        out_specs=VMEM,
        compiler_params=pltpu.CompilerParams(vmem_limit_bytes=4 * MIB),
        cost_estimate=pl.CostEstimate(flops=2 * examples * seq_len * width * width, bytes_accessed=8 * MIB, transcendentals=0),
        name="features",
    )(lengths, rounded, turned)


def split(values):
    high = values.astype(bf16)
    return high, (values - high.astype(f32)).astype(bf16)


def invert(packed):
    rank, width = packed.shape
    run = 8
    blocks = [packed[run * r : run * (r + 1), :] for r in range(rank // run)]
    lane = lax.broadcasted_iota(jnp.int32, (run, width), 1)
    sub = lax.broadcasted_iota(jnp.int32, (run, width), 0)
    column = jnp.where(lane < rank, lane, lane - rank)
    base = jnp.where(lane < rank, 0, rank)

    def pick(values, at):
        return jnp.take_along_axis(values, base + at, axis=1)

    for p in range(len(blocks)):
        first = run * p
        rows = [jnp.broadcast_to(blocks[p][i : i + 1, :], (run, width)) for i in range(run)]
        entry = [[None] * run for _ in range(run)]
        for i in range(run):
            for j in range(i, run):
                entry[i][j] = entry[j][i] = pick(rows[i], first + j)
        columns = [[pick(block, first + j) for j in range(run)] for block in blocks]
        for j in range(0, run, 2):
            a, b, c = entry[j][j], entry[j][j + 1], entry[j + 1][j + 1]
            scale = 1.0 / (a * c - b * b)
            ia, ib, ic = c * scale, -(b * scale), a * scale
            at_first, at_second = column == first + j, column == first + j + 1
            low = jnp.where(at_first, ia, jnp.where(at_second, ib, ia * rows[j] + ib * rows[j + 1]))
            high = jnp.where(at_first, ib, jnp.where(at_second, ic, ib * rows[j] + ic * rows[j + 1]))
            later = range(j + 2, run)
            low_entry = {k: ia * entry[j][k] + ib * entry[j + 1][k] for k in later}
            high_entry = {k: ib * entry[j][k] + ic * entry[j + 1][k] for k in later}
            for i in range(run):
                if i in (j, j + 1):
                    continue
                from_low, from_high = entry[i][j], entry[i][j + 1]
                rows[i] = jnp.where(at_first | at_second, 0.0, rows[i]) - (from_low * low + from_high * high)
                for k in later:
                    if j + 1 < i and k < i:
                        entry[i][k] = entry[k][i]
                    else:
                        entry[i][k] = entry[i][k] - (from_low * low_entry[k] + from_high * high_entry[k])
            rows[j], rows[j + 1] = low, high
            for k in later:
                entry[j][k], entry[j + 1][k] = low_entry[k], high_entry[k]
        pivots = (column >= first) & (column < first + run)
        for r in range(len(blocks)):
            if r != p:
                terms = [columns[r][i] * rows[i] for i in range(run)]
                while len(terms) > 1:
                    terms = [terms[i] + terms[i + 1] for i in range(0, len(terms), 2)]
                blocks[r] = jnp.where(pivots, 0.0, blocks[r]) - terms[0]
        turned = rows[0]
        for i in range(1, run):
            turned = jnp.where(sub == i, rows[i], turned)
        blocks[p] = turned
    return jnp.concatenate(blocks, axis=0)


def inverses_body(total_tokens, factor_a_ref, factor_b_ref, grad_ref, in_ref):
    rank = factor_a_ref.shape[0]
    lane = lax.broadcasted_iota(jnp.int32, (rank, 2 * rank), 1)
    sub = lax.broadcasted_iota(jnp.int32, (rank, 2 * rank), 0)
    left = lane < rank
    column = jnp.where(left, lane, lane - rank)
    diagonal = column == sub
    packed = (factor_a_ref[...] + factor_b_ref[...]) / total_tokens
    on_diagonal = jnp.sum(jnp.where(diagonal, packed, 0.0), axis=0, keepdims=True)
    trace_in = jnp.sum(jnp.where(left[:1], on_diagonal, 0.0), axis=1, keepdims=True)
    trace_grad = jnp.sum(jnp.where(left[:1], 0.0, on_diagonal), axis=1, keepdims=True)
    damping = 0.1 * jnp.where(left[:1], trace_in, trace_grad) / rank + 1e-06
    packed = packed + jnp.where(diagonal, damping, 0.0)
    packed = invert(packed)
    twice = pltpu.roll(packed, rank, 1)
    grad_ref[0], grad_ref[1] = split(twice[:, :rank])
    in_ref[0, :rank, :], in_ref[1, :rank, :] = split(jnp.where(left, packed, 0.0))
    in_ref[0, rank:, :], in_ref[1, rank:, :] = split(jnp.where(left, 0.0, twice))


def inverses(total_tokens, factor_a, factor_b):
    rank, width = factor_a.shape
    return pl.pallas_call(
        functools.partial(inverses_body, total_tokens),
        out_shape=(
            jax.ShapeDtypeStruct((2, rank, rank), bf16),
            jax.ShapeDtypeStruct((2, width, width), bf16),
        ),
        in_specs=[VMEM, VMEM],
        out_specs=(VMEM, VMEM),
        compiler_params=pltpu.CompilerParams(vmem_limit_bytes=4 * MIB),
        cost_estimate=pl.CostEstimate(flops=16384 * MIB, bytes_accessed=0, transcendentals=0),
        name="inverses",
    )(factor_a, factor_b)


def pack_body(tests_ref, *out_refs):
    feat_count = len(out_refs)
    rows, width = tests_ref.shape
    fold, block = rows // feat_count, width // feat_count
    feat = lax.axis_index("feat")
    pieces = []
    for target in range(feat_count):
        columns = slice(target * block, (target + 1) * block)
        parts = [tests_ref[j * fold : (j + 1) * fold, columns] for j in range(feat_count)]
        pieces.append(jnp.concatenate(parts, axis=1))
    for mask, out_ref in enumerate(out_refs):
        piece = pieces[0]
        for target in range(1, feat_count):
            piece = jnp.where((feat ^ mask) == target, pieces[target], piece)
        out_ref[...] = piece


def pack(tests, flops):
    rows, width = tests.shape
    feat_count = lax.axis_size("feat")
    return pl.pallas_call(
        pack_body,
        out_shape=[jax.ShapeDtypeStruct((rows // feat_count, width), bf16)] * feat_count,
        in_specs=[VMEM],
        out_specs=[VMEM] * feat_count,
        compiler_params=pltpu.CompilerParams(vmem_limit_bytes=8 * MIB),
        cost_estimate=pl.CostEstimate(flops=flops, bytes_accessed=4 * MIB, transcendentals=0),
        name="pack",
    )(tests)


def scores_body(blocks, piece_counts, grad_ref, in_ref, *refs):
    feat_count = lax.axis_size("feat")
    feat = lax.axis_index("feat")
    counts, pieces = piece_counts, []
    for count in counts:
        rows = refs[0].shape[0] // count
        pieces += [refs[0].at[pl.ds(rows * i, rows), :] for i in range(count)]
        refs = refs[1:]
    feats_refs, out_refs, (solved_buf, line_buf) = refs[:blocks], refs[blocks : 2 * blocks], refs[2 * blocks :]
    rank = grad_ref.shape[1]
    pairs = [ref[i] for ref in feats_refs for i in range(ref.shape[0])]
    count = len(pairs)
    half = count // blocks
    fold, width = pieces[0].shape
    block = width // feat_count
    dot = functools.partial(jnp.dot, preferred_element_type=f32)
    both = dot(jnp.concatenate([grad_ref[0], grad_ref[1]], axis=0), jnp.concatenate(pairs, axis=1))
    solved = both[:rank, :] + both[rank:, :]
    rows = [solved[:, 2 * rank * at : 2 * rank * (at + 1)] for at in range(count)]
    high, low = split(jnp.concatenate(rows, axis=0))
    both = dot(high, jnp.concatenate([in_ref[0], in_ref[1]], axis=1))
    solved_buf[...] = both[:, : 2 * rank] + both[:, 2 * rank :] + dot(low, in_ref[0])
    lane = lax.broadcasted_iota(jnp.int32, (count, 2 * rank), 1)
    for g in range(0, rank, 2):
        low = solved_buf[pl.ds(g, count, stride=rank), :]
        high = solved_buf[pl.ds(g + 1, count, stride=rank), :]
        first = jnp.where(lane < rank, low, pltpu.roll(high, rank, 1))
        second = jnp.where(lane < rank, pltpu.roll(low, rank, 1), high)
        line = jnp.concatenate([first, second], axis=0).astype(bf16)
        step = min(fold, 2 * rank)
        for begin in range(0, 2 * rank, step):
            at = (g * rank + begin) // fold
            to = (g * rank + begin) % fold
            line_buf[at // feat_count, at % feat_count, :, to : to + step] = line[:, begin : begin + step]
    lines = []
    for mask in range(feat_count):
        owner = feat ^ mask
        lines.append(jnp.concatenate([line_buf[owner, j] for j in range(feat_count)], axis=0))
    is_first = lax.axis_index("test") == 0
    odd = lax.rem(lax.axis_index("dp"), 2)
    for dp_bit in range(2):
        parts = []
        for test_bit in range(2):
            at = (2 * dp_bit + test_bit) * feat_count
            total = dot(lines[0], pieces[at][...])
            for mask in range(1, feat_count):
                total = total + dot(lines[mask], pieces[at + mask][...])
            part = total[: 2 * count, :block]
            for j in range(1, feat_count):
                part = part + total[2 * count * j : 2 * count * (j + 1), block * j : block * (j + 1)]
            parts.append(part)
        both = jnp.concatenate(
            [jnp.where(is_first, parts[0], parts[1]), jnp.where(is_first, parts[1], parts[0])], axis=1
        )
        for at, out_ref in enumerate(out_refs):
            out_ref[odd ^ dp_bit, :half, :] = both[at * half : (at + 1) * half, :]
            out_ref[odd ^ dp_bit, half:, :] = both[count + at * half : count + (at + 1) * half, :]


def scores_of(grad, in_pair, pieces, piece_counts, feats):
    feat_count = lax.axis_size("feat")
    rank = grad.shape[1]
    fold, width = pieces[0].shape[0] // piece_counts[0], pieces[0].shape[1]
    half = feats[0].shape[0]
    count = half * len(feats)
    return pl.pallas_call(
        functools.partial(scores_body, len(feats), piece_counts),
        out_shape=[jax.ShapeDtypeStruct((2, 2 * half, 2 * width // feat_count), f32)] * len(feats),
        in_specs=[VMEM] * (2 + len(pieces) + len(feats)),
        out_specs=[VMEM] * len(feats),
        scratch_shapes=[
            pltpu.VMEM((count * rank, 2 * rank), f32),
            pltpu.VMEM((feat_count, feat_count, 2 * count, fold), bf16),
        ],
        compiler_params=pltpu.CompilerParams(vmem_limit_bytes=16 * MIB),
        name="scores",
    )(grad, in_pair, *pieces, *feats)


def finish_body(*refs):
    block_refs, out_ref = refs[:-1], refs[-1]
    count = len(block_refs)
    _, examples, width = block_refs[0].shape
    half = width // 2
    own = lax.div(lax.axis_index("dp"), 2)
    for place in range(count):
        for odd in range(2):
            block = block_refs[0][odd]
            for mask in range(1, count):
                block = jnp.where((own ^ mask) == place, block_refs[mask][odd], block)
            for test in range(2):
                rows = pl.ds(4 * place + 2 * odd + test, examples, stride=4 * count)
                out_ref[rows, :] = block[:, test * half : (test + 1) * half]


def finish(blocks):
    _, examples, width = blocks[0].shape
    queries = 4 * len(blocks)
    out = pl.pallas_call(
        finish_body,
        out_shape=jax.ShapeDtypeStruct((examples * queries, width // 2), f32),
        in_specs=[VMEM] * len(blocks),
        out_specs=VMEM,
        compiler_params=pltpu.CompilerParams(vmem_limit_bytes=4 * MIB),
        name="finish",
    )(*blocks)
    return out.reshape(examples, queries, width // 2)


def after(values, *others):
    return lax.optimization_barrier((values, *others))[0]


def on_device(train_inputs, train_grads, proj_in, proj_out, lengths, loss_mask, test_feats):
    examples, seq_len, in_width = train_inputs.shape
    out_width = train_grads.shape[2]
    tokens = examples * seq_len
    feat_count = lax.axis_size("feat")
    dp_count = lax.axis_size("dp")
    test_count = lax.axis_size("test")
    own_rows = test_feats.shape[1]
    x = train_inputs.reshape(tokens, in_width)
    g = train_grads.reshape(tokens, out_width)
    tests = test_feats.transpose(1, 2, 0).reshape(own_rows * test_feats.shape[2], test_feats.shape[0])
    positions = slots(seq_len)
    far_tests = xor_permute(tests, "dp", 1)
    own, sent = project(x, g, after(proj_in.T, positions), proj_out.T, tokens // 3)
    cut = pack(after(tests, sent), 4 * MIB)
    near = [cut[0]] + [xor_permute(cut[mask], "feat", mask) for mask in range(1, feat_count)]
    received = [xor_permute(sent, "feat", mask) for mask in range(1, feat_count)]
    cut = pack(after(far_tests, *(sent,)), 4 * MIB)
    far = [cut[0]] + [xor_permute(cut[mask], "feat", mask) for mask in range(1, feat_count)]
    factor, rounded, turned = factors(lengths, positions, loss_mask, own, received)
    feats = [features_of(lengths, rounded, turned)]
    even_masks = range(2, dp_count, 2)
    steps = [("test", 1)] + [("dp", m) for m in reversed(masks_of(dp_count))]
    sums = [factor]
    for axis, mask in steps:
        if len(sums) == len(steps):
            sums[-1] = after(sums[-1], feats[0])
        other = xor_permute(sums[-1], axis, mask)
        sums.append(sums[-1] + other)
    pieces, piece_counts = [], []
    pieces += near + [xor_permute(piece, "test", 1) for piece in after(tuple(near), *(sums[2],))]
    piece_counts += [1] * (2 * feat_count)
    pieces += far + [xor_permute(jnp.concatenate(after(tuple(far), *(other,)), axis=0), "test", 1)]
    piece_counts += [1] * feat_count + [feat_count]
    feats += [xor_permute(feats[0], "dp", mask) for mask in even_masks]
    total_tokens = float(tokens * dp_count * test_count)
    grad, in_pair = inverses(total_tokens, sums[-2], other)
    blocks = scores_of(grad, in_pair, pieces, piece_counts, feats)
    blocks = [blocks[0]] + [xor_permute(blocks[at + 1], "dp", mask) for at, mask in enumerate(even_masks)]
    return finish(blocks)


def solution(mesh):
    return jax.shard_map(
        on_device,
        mesh=mesh,
        in_specs=(
            P(("groups", "dp", "test"), None, "feat"),
            P(("groups", "dp", "test"), None, "feat"),
            P("feat", None),
            P("feat", None),
            P(("groups", "dp", "test")),
            P(("groups", "dp", "test"), None),
            P(("groups", "dp", "test"), "feat", None),
        ),
        out_specs=P(("groups", "dp", "test"), None, "feat"),
        check_vma=False,
    )
```

```python
import functools

import jax
import jax.numpy as jnp
from jax import lax
from jax.experimental import pallas as pl
from jax.experimental.pallas import tpu as pltpu
from jax.sharding import PartitionSpec as P

f32 = jnp.float32
bf16 = jnp.bfloat16
MIB = 1024 * 1024
NT = (((1,), (1,)), ((), ()))
VMEM = pl.BlockSpec(memory_space=pltpu.VMEM)
SMEM = pl.BlockSpec(memory_space=pltpu.SMEM)
ANY = pl.BlockSpec(memory_space=pl.ANY)
PROJECT_MIB = 48


def xor_permute(values, axis, mask):
    size = lax.axis_size(axis)
    return lax.ppermute(values, axis, [(i, i ^ mask) for i in range(size)])


def masks_of(size):
    masks, mask = [], 1
    while mask < size:
        masks.append(mask)
        mask *= 2
    return masks


def project_body(rows, x_ref, g_hbm, pin_ref, pout_ref, own_ref, sent_ref, g_buf, sems):
    steps = x_ref.shape[0] // rows
    rank = pin_ref.shape[0]

    def g_copy(step):
        begin = step * rows if isinstance(step, int) else pl.multiple_of(step * rows, rows)
        block = pl.ds(begin, rows)
        return pltpu.make_async_copy(g_hbm.at[block, :], g_buf.at[block, :], sems.at[step])

    for step in range(steps):
        g_copy(step).start()
    own_ref[:, :rank] = lax.dot_general(x_ref[...], pin_ref[...], NT, preferred_element_type=f32)

    @pl.loop(0, steps)
    def _(step):
        g_copy(step).wait()
        block = pl.ds(pl.multiple_of(step * rows, rows), rows)
        right = lax.dot_general(g_buf[block, :], pout_ref[...], NT, preferred_element_type=f32)
        both = jnp.concatenate([own_ref[block, :rank], right], axis=1)
        own_ref[block, :] = both
        sent_ref[block, :] = both.astype(bf16)


def project(x, g, pin, pout, rows):
    tokens, in_width = x.shape
    out_width = g.shape[1]
    rank = pin.shape[0]
    return pl.pallas_call(
        functools.partial(project_body, rows),
        out_shape=(
            jax.ShapeDtypeStruct((tokens, 2 * rank), f32),
            jax.ShapeDtypeStruct((tokens, 2 * rank), bf16),
        ),
        in_specs=[VMEM, ANY, VMEM, VMEM],
        out_specs=(VMEM, VMEM),
        scratch_shapes=[pltpu.VMEM(g.shape, bf16), pltpu.SemaphoreType.DMA((tokens // rows,))],
        compiler_params=pltpu.CompilerParams(vmem_limit_bytes=PROJECT_MIB * MIB),
        cost_estimate=pl.CostEstimate(
            flops=2 * tokens * (in_width + out_width) * rank,
            bytes_accessed=2 * (tokens + rank) * (in_width + out_width),
            transcendentals=0,
        ),
        name="project",
    )(x, g, pin, pout)


def fetch_body(values_ref, out_ref):
    out_ref[...] = values_ref[...]


def fetch(values):
    return pl.pallas_call(
        fetch_body,
        out_shape=jax.ShapeDtypeStruct(values.shape, values.dtype),
        in_specs=[VMEM],
        out_specs=VMEM,
        compiler_params=pltpu.CompilerParams(vmem_limit_bytes=4 * MIB),
        cost_estimate=pl.CostEstimate(flops=values.size, bytes_accessed=8 * values.size, transcendentals=0),
        name="fetch",
    )(values)


def slots_body(out_ref):
    out_ref[...] = lax.broadcasted_iota(jnp.int32, out_ref.shape, 1)


def slots(seq_len):
    return pl.pallas_call(
        slots_body,
        out_shape=jax.ShapeDtypeStruct((1, seq_len), jnp.int32),
        out_specs=VMEM,
        compiler_params=pltpu.CompilerParams(vmem_limit_bytes=MIB),
        cost_estimate=pl.CostEstimate(flops=40960 * MIB, bytes_accessed=4096, transcendentals=0),
        name="slots",
    )()


def factors_body(received, lengths_ref, positions_ref, mask_ref, own_ref, *refs):
    received_refs = refs[:received]
    factor_ref, rounded_ref, turned_ref = refs[received:]
    examples, seq_len = mask_ref.shape
    rank = factor_ref.shape[0]
    positions = positions_ref[...]
    total = None
    for example in range(examples):
        rows = pl.ds(example * seq_len, seq_len)
        summed = own_ref[rows, :]
        for ref in received_refs:
            summed = summed + ref[rows, :].astype(f32)
        rounded = summed.astype(bf16)
        rounded_ref[rows, :] = rounded
        live = (mask_ref[example : example + 1, :] > 0) & (positions < lengths_ref[example])
        turned = jnp.where(live, rounded.astype(f32).T, 0.0).astype(bf16)
        turned_ref[example] = turned
        products = jnp.dot(turned, rounded, preferred_element_type=f32)
        total = products if total is None else total + products
    lane = lax.broadcasted_iota(jnp.int32, (rank, 2 * rank), 1)
    factor_ref[...] = jnp.where(lane < rank, total[:rank, :], total[rank:, :])


def factors(lengths, positions, mask, own, received):
    tokens, width = own.shape
    examples, seq_len = mask.shape
    return pl.pallas_call(
        functools.partial(factors_body, len(received)),
        out_shape=(
            jax.ShapeDtypeStruct((width // 2, width), f32),
            jax.ShapeDtypeStruct((tokens, width), bf16),
            jax.ShapeDtypeStruct((examples, width, seq_len), bf16),
        ),
        in_specs=[SMEM, VMEM, VMEM, VMEM] + [VMEM] * len(received),
        out_specs=(VMEM, VMEM, VMEM),
        compiler_params=pltpu.CompilerParams(vmem_limit_bytes=4 * MIB),
        name="factors",
    )(lengths, positions, mask, own, *received)


def features_body(lengths_ref, rounded_ref, turned_ref, feats_ref):
    half, rank, _ = feats_ref.shape
    examples, _, seq_len = turned_ref.shape
    lane = lax.broadcasted_iota(jnp.int32, (rank, 2 * rank), 1)

    def features(example):
        products = jnp.dot(
            turned_ref[example, rank:, :], rounded_ref[pl.ds(example * seq_len, seq_len), :], preferred_element_type=f32
        )
        return products / lengths_ref[example].astype(f32)

    for pair in range(half):
        other = pltpu.roll(features(half + pair), rank, 1)
        feats_ref[pair] = jnp.where(lane < rank, features(pair), other).astype(bf16)


def features_of(lengths, rounded, turned):
    examples, width, seq_len = turned.shape
    return pl.pallas_call(
        features_body,
        out_shape=jax.ShapeDtypeStruct((examples // 2, width // 2, width), bf16),
        in_specs=[SMEM, VMEM, VMEM],
        out_specs=VMEM,
        compiler_params=pltpu.CompilerParams(vmem_limit_bytes=4 * MIB),
        cost_estimate=pl.CostEstimate(flops=2 * examples * seq_len * width * width, bytes_accessed=8 * MIB, transcendentals=0),
        name="features",
    )(lengths, rounded, turned)


def split(values):
    high = values.astype(bf16)
    return high, (values - high.astype(f32)).astype(bf16)


def invert(packed):
    rank, width = packed.shape
    run = 8
    blocks = [packed[run * r : run * (r + 1), :] for r in range(rank // run)]
    lane = lax.broadcasted_iota(jnp.int32, (run, width), 1)
    sub = lax.broadcasted_iota(jnp.int32, (run, width), 0)
    column = jnp.where(lane < rank, lane, lane - rank)
    base = jnp.where(lane < rank, 0, rank)

    def pick(values, at):
        return jnp.take_along_axis(values, base + at, axis=1)

    for p in range(len(blocks)):
        first = run * p
        rows = [jnp.broadcast_to(blocks[p][i : i + 1, :], (run, width)) for i in range(run)]
        entry = [[None] * run for _ in range(run)]
        for i in range(run):
            for j in range(i, run):
                entry[i][j] = entry[j][i] = pick(rows[i], first + j)
        columns = [[pick(block, first + j) for j in range(run)] for block in blocks]
        for j in range(0, run, 2):
            a, b, c = entry[j][j], entry[j][j + 1], entry[j + 1][j + 1]
            scale = 1.0 / (a * c - b * b)
            ia, ib, ic = c * scale, -(b * scale), a * scale
            at_first, at_second = column == first + j, column == first + j + 1
            low = jnp.where(at_first, ia, jnp.where(at_second, ib, ia * rows[j] + ib * rows[j + 1]))
            high = jnp.where(at_first, ib, jnp.where(at_second, ic, ib * rows[j] + ic * rows[j + 1]))
            later = range(j + 2, run)
            low_entry = {k: ia * entry[j][k] + ib * entry[j + 1][k] for k in later}
            high_entry = {k: ib * entry[j][k] + ic * entry[j + 1][k] for k in later}
            for i in range(run):
                if i in (j, j + 1):
                    continue
                from_low, from_high = entry[i][j], entry[i][j + 1]
                rows[i] = jnp.where(at_first | at_second, 0.0, rows[i]) - (from_low * low + from_high * high)
                for k in later:
                    if j + 1 < i and k < i:
                        entry[i][k] = entry[k][i]
                    else:
                        entry[i][k] = entry[i][k] - (from_low * low_entry[k] + from_high * high_entry[k])
            rows[j], rows[j + 1] = low, high
            for k in later:
                entry[j][k], entry[j + 1][k] = low_entry[k], high_entry[k]
        pivots = (column >= first) & (column < first + run)
        for r in range(len(blocks)):
            if r != p:
                terms = [columns[r][i] * rows[i] for i in range(run)]
                while len(terms) > 1:
                    terms = [terms[i] + terms[i + 1] for i in range(0, len(terms), 2)]
                blocks[r] = jnp.where(pivots, 0.0, blocks[r]) - terms[0]
        turned = rows[0]
        for i in range(1, run):
            turned = jnp.where(sub == i, rows[i], turned)
        blocks[p] = turned
    return jnp.concatenate(blocks, axis=0)


def inverses_body(total_tokens, factor_a_ref, factor_b_ref, grad_ref, in_ref):
    rank = factor_a_ref.shape[0]
    lane = lax.broadcasted_iota(jnp.int32, (rank, 2 * rank), 1)
    sub = lax.broadcasted_iota(jnp.int32, (rank, 2 * rank), 0)
    left = lane < rank
    column = jnp.where(left, lane, lane - rank)
    diagonal = column == sub
    packed = (factor_a_ref[...] + factor_b_ref[...]) / total_tokens
    on_diagonal = jnp.sum(jnp.where(diagonal, packed, 0.0), axis=0, keepdims=True)
    trace_in = jnp.sum(jnp.where(left[:1], on_diagonal, 0.0), axis=1, keepdims=True)
    trace_grad = jnp.sum(jnp.where(left[:1], 0.0, on_diagonal), axis=1, keepdims=True)
    damping = 0.1 * jnp.where(left[:1], trace_in, trace_grad) / rank + 1e-06
    packed = packed + jnp.where(diagonal, damping, 0.0)
    packed = invert(packed)
    twice = pltpu.roll(packed, rank, 1)
    grad_ref[0], grad_ref[1] = split(twice[:, :rank])
    in_ref[0, :rank, :], in_ref[1, :rank, :] = split(jnp.where(left, packed, 0.0))
    in_ref[0, rank:, :], in_ref[1, rank:, :] = split(jnp.where(left, 0.0, twice))


def inverses(total_tokens, factor_a, factor_b):
    rank, width = factor_a.shape
    return pl.pallas_call(
        functools.partial(inverses_body, total_tokens),
        out_shape=(
            jax.ShapeDtypeStruct((2, rank, rank), bf16),
            jax.ShapeDtypeStruct((2, width, width), bf16),
        ),
        in_specs=[VMEM, VMEM],
        out_specs=(VMEM, VMEM),
        compiler_params=pltpu.CompilerParams(vmem_limit_bytes=4 * MIB),
        cost_estimate=pl.CostEstimate(flops=16384 * MIB, bytes_accessed=0, transcendentals=0),
        name="inverses",
    )(factor_a, factor_b)


def pack_body(tests_ref, *out_refs):
    feat_count = len(out_refs)
    rows, width = tests_ref.shape
    fold, block = rows // feat_count, width // feat_count
    feat = lax.axis_index("feat")
    pieces = []
    for target in range(feat_count):
        columns = slice(target * block, (target + 1) * block)
        parts = [tests_ref[j * fold : (j + 1) * fold, columns] for j in range(feat_count)]
        pieces.append(jnp.concatenate(parts, axis=1))
    for mask, out_ref in enumerate(out_refs):
        piece = pieces[0]
        for target in range(1, feat_count):
            piece = jnp.where((feat ^ mask) == target, pieces[target], piece)
        out_ref[...] = piece


def pack(tests, flops):
    rows, width = tests.shape
    feat_count = lax.axis_size("feat")
    return pl.pallas_call(
        pack_body,
        out_shape=[jax.ShapeDtypeStruct((rows // feat_count, width), bf16)] * feat_count,
        in_specs=[VMEM],
        out_specs=[VMEM] * feat_count,
        compiler_params=pltpu.CompilerParams(vmem_limit_bytes=8 * MIB),
        cost_estimate=pl.CostEstimate(flops=flops, bytes_accessed=4 * MIB, transcendentals=0),
        name="pack",
    )(tests)


def scores_body(blocks, piece_counts, grad_ref, in_ref, *refs):
    feat_count = lax.axis_size("feat")
    feat = lax.axis_index("feat")
    counts, pieces = piece_counts, []
    for count in counts:
        rows = refs[0].shape[0] // count
        pieces += [refs[0].at[pl.ds(rows * i, rows), :] for i in range(count)]
        refs = refs[1:]
    feats_refs, out_refs, (solved_buf, line_buf) = refs[:blocks], refs[blocks : 2 * blocks], refs[2 * blocks :]
    rank = grad_ref.shape[1]
    pairs = [ref[i] for ref in feats_refs for i in range(ref.shape[0])]
    count = len(pairs)
    half = count // blocks
    fold, width = pieces[0].shape
    block = width // feat_count
    dot = functools.partial(jnp.dot, preferred_element_type=f32)
    both = dot(jnp.concatenate([grad_ref[0], grad_ref[1]], axis=0), jnp.concatenate(pairs, axis=1))
    solved = both[:rank, :] + both[rank:, :]
    rows = [solved[:, 2 * rank * at : 2 * rank * (at + 1)] for at in range(count)]
    high, low = split(jnp.concatenate(rows, axis=0))
    both = dot(high, jnp.concatenate([in_ref[0], in_ref[1]], axis=1))
    solved_buf[...] = both[:, : 2 * rank] + both[:, 2 * rank :] + dot(low, in_ref[0])
    lane = lax.broadcasted_iota(jnp.int32, (count, 2 * rank), 1)
    for g in range(0, rank, 2):
        low = solved_buf[pl.ds(g, count, stride=rank), :]
        high = solved_buf[pl.ds(g + 1, count, stride=rank), :]
        first = jnp.where(lane < rank, low, pltpu.roll(high, rank, 1))
        second = jnp.where(lane < rank, pltpu.roll(low, rank, 1), high)
        line = jnp.concatenate([first, second], axis=0).astype(bf16)
        step = min(fold, 2 * rank)
        for begin in range(0, 2 * rank, step):
            at = (g * rank + begin) // fold
            to = (g * rank + begin) % fold
            line_buf[at // feat_count, at % feat_count, :, to : to + step] = line[:, begin : begin + step]
    lines = []
    for mask in range(feat_count):
        owner = feat ^ mask
        lines.append(jnp.concatenate([line_buf[owner, j] for j in range(feat_count)], axis=0))
    is_first = lax.axis_index("test") == 0
    odd = lax.rem(lax.axis_index("dp"), 2)
    for dp_bit in range(2):
        parts = []
        for test_bit in range(2):
            at = (2 * dp_bit + test_bit) * feat_count
            total = dot(lines[0], pieces[at][...])
            for mask in range(1, feat_count):
                total = total + dot(lines[mask], pieces[at + mask][...])
            part = total[: 2 * count, :block]
            for j in range(1, feat_count):
                part = part + total[2 * count * j : 2 * count * (j + 1), block * j : block * (j + 1)]
            parts.append(part)
        both = jnp.concatenate(
            [jnp.where(is_first, parts[0], parts[1]), jnp.where(is_first, parts[1], parts[0])], axis=1
        )
        for at, out_ref in enumerate(out_refs):
            out_ref[odd ^ dp_bit, :half, :] = both[at * half : (at + 1) * half, :]
            out_ref[odd ^ dp_bit, half:, :] = both[count + at * half : count + (at + 1) * half, :]


def scores_of(grad, in_pair, pieces, piece_counts, feats):
    feat_count = lax.axis_size("feat")
    rank = grad.shape[1]
    fold, width = pieces[0].shape[0] // piece_counts[0], pieces[0].shape[1]
    half = feats[0].shape[0]
    count = half * len(feats)
    return pl.pallas_call(
        functools.partial(scores_body, len(feats), piece_counts),
        out_shape=[jax.ShapeDtypeStruct((2, 2 * half, 2 * width // feat_count), f32)] * len(feats),
        in_specs=[VMEM] * (2 + len(pieces) + len(feats)),
        out_specs=[VMEM] * len(feats),
        scratch_shapes=[
            pltpu.VMEM((count * rank, 2 * rank), f32),
            pltpu.VMEM((feat_count, feat_count, 2 * count, fold), bf16),
        ],
        compiler_params=pltpu.CompilerParams(vmem_limit_bytes=16 * MIB),
        name="scores",
    )(grad, in_pair, *pieces, *feats)


def finish_body(*refs):
    block_refs, out_ref = refs[:-1], refs[-1]
    count = len(block_refs)
    _, examples, width = block_refs[0].shape
    half = width // 2
    own = lax.div(lax.axis_index("dp"), 2)
    for place in range(count):
        for odd in range(2):
            block = block_refs[0][odd]
            for mask in range(1, count):
                block = jnp.where((own ^ mask) == place, block_refs[mask][odd], block)
            for test in range(2):
                rows = pl.ds(4 * place + 2 * odd + test, examples, stride=4 * count)
                out_ref[rows, :] = block[:, test * half : (test + 1) * half]


def finish(blocks):
    _, examples, width = blocks[0].shape
    queries = 4 * len(blocks)
    out = pl.pallas_call(
        finish_body,
        out_shape=jax.ShapeDtypeStruct((examples * queries, width // 2), f32),
        in_specs=[VMEM] * len(blocks),
        out_specs=VMEM,
        compiler_params=pltpu.CompilerParams(vmem_limit_bytes=4 * MIB),
        name="finish",
    )(*blocks)
    return out.reshape(examples, queries, width // 2)


def after(values, *others):
    return lax.optimization_barrier((values, *others))[0]


def on_device(train_inputs, train_grads, proj_in, proj_out, lengths, loss_mask, test_feats):
    examples, seq_len, in_width = train_inputs.shape
    out_width = train_grads.shape[2]
    tokens = examples * seq_len
    feat_count = lax.axis_size("feat")
    dp_count = lax.axis_size("dp")
    test_count = lax.axis_size("test")
    own_rows = test_feats.shape[1]
    x = train_inputs.reshape(tokens, in_width)
    g = train_grads.reshape(tokens, out_width)
    tests = test_feats.transpose(1, 2, 0).reshape(own_rows * test_feats.shape[2], test_feats.shape[0])
    positions = slots(seq_len)
    far_tests = xor_permute(tests, "dp", 1)
    own, sent = project(x, g, after(proj_in.T, positions), proj_out.T, tokens // 3)
    cut = pack(after(tests, sent), 4 * MIB)
    near = [cut[0]] + [xor_permute(cut[mask], "feat", mask) for mask in range(1, feat_count)]
    received = [xor_permute(sent, "feat", mask) for mask in range(1, feat_count)]
    cut = pack(after(far_tests, *(sent,)), 4 * MIB)
    far = [cut[0]] + [xor_permute(cut[mask], "feat", mask) for mask in range(1, feat_count)]
    factor, rounded, turned = factors(lengths, positions, loss_mask, own, received)
    feats = [features_of(lengths, rounded, turned)]
    even_masks = range(2, dp_count, 2)
    steps = [("test", 1)] + [("dp", m) for m in masks_of(dp_count)]
    sums = [factor]
    for axis, mask in steps:
        if len(sums) == len(steps):
            sums[-1] = after(sums[-1], feats[0])
        other = xor_permute(sums[-1], axis, mask)
        sums.append(sums[-1] + other)
    pieces, piece_counts = [], []
    pieces += near + [xor_permute(piece, "test", 1) for piece in after(tuple(near), *(sums[2],))]
    piece_counts += [1] * (2 * feat_count)
    pieces += far + [xor_permute(jnp.concatenate(after(tuple(far), *(other,)), axis=0), "test", 1)]
    piece_counts += [1] * feat_count + [feat_count]
    feats += [xor_permute(feats[0], "dp", mask) for mask in even_masks]
    total_tokens = float(tokens * dp_count * test_count)
    grad, in_pair = inverses(total_tokens, sums[-2], other)
    blocks = scores_of(grad, in_pair, pieces, piece_counts, feats)
    blocks = [blocks[0]] + [xor_permute(blocks[at + 1], "dp", mask) for at, mask in enumerate(even_masks)]
    return finish(blocks)


def solution(mesh):
    return jax.shard_map(
        on_device,
        mesh=mesh,
        in_specs=(
            P(("groups", "dp", "test"), None, "feat"),
            P(("groups", "dp", "test"), None, "feat"),
            P("feat", None),
            P("feat", None),
            P(("groups", "dp", "test")),
            P(("groups", "dp", "test"), None),
            P(("groups", "dp", "test"), "feat", None),
        ),
        out_specs=P(("groups", "dp", "test"), None, "feat"),
        check_vma=False,
    )
```

```python
import functools

import jax
import jax.numpy as jnp
from jax import lax
from jax.experimental import pallas as pl
from jax.experimental.pallas import tpu as pltpu
from jax.sharding import PartitionSpec as P

f32 = jnp.float32
bf16 = jnp.bfloat16
MIB = 1024 * 1024
NT = (((1,), (1,)), ((), ()))
VMEM = pl.BlockSpec(memory_space=pltpu.VMEM)
SMEM = pl.BlockSpec(memory_space=pltpu.SMEM)
ANY = pl.BlockSpec(memory_space=pl.ANY)
PROJECT_MIB = 48


def xor_permute(values, axis, mask):
    size = lax.axis_size(axis)
    return lax.ppermute(values, axis, [(i, i ^ mask) for i in range(size)])


def masks_of(size):
    masks, mask = [], 1
    while mask < size:
        masks.append(mask)
        mask *= 2
    return masks


def project_body(rows, x_ref, g_hbm, pin_ref, pout_ref, own_ref, sent_ref, g_buf, sems):
    steps = x_ref.shape[0] // rows
    rank = pin_ref.shape[0]

    def g_copy(step):
        begin = step * rows if isinstance(step, int) else pl.multiple_of(step * rows, rows)
        block = pl.ds(begin, rows)
        return pltpu.make_async_copy(g_hbm.at[block, :], g_buf.at[block, :], sems.at[step])

    for step in range(steps):
        g_copy(step).start()
    own_ref[:, :rank] = lax.dot_general(x_ref[...], pin_ref[...], NT, preferred_element_type=f32)

    @pl.loop(0, steps)
    def _(step):
        g_copy(step).wait()
        block = pl.ds(pl.multiple_of(step * rows, rows), rows)
        right = lax.dot_general(g_buf[block, :], pout_ref[...], NT, preferred_element_type=f32)
        both = jnp.concatenate([own_ref[block, :rank], right], axis=1)
        own_ref[block, :] = both
        sent_ref[block, :] = both.astype(bf16)


def project(x, g, pin, pout, rows):
    tokens, in_width = x.shape
    out_width = g.shape[1]
    rank = pin.shape[0]
    return pl.pallas_call(
        functools.partial(project_body, rows),
        out_shape=(
            jax.ShapeDtypeStruct((tokens, 2 * rank), f32),
            jax.ShapeDtypeStruct((tokens, 2 * rank), bf16),
        ),
        in_specs=[VMEM, ANY, VMEM, VMEM],
        out_specs=(VMEM, VMEM),
        scratch_shapes=[pltpu.VMEM(g.shape, bf16), pltpu.SemaphoreType.DMA((tokens // rows,))],
        compiler_params=pltpu.CompilerParams(vmem_limit_bytes=PROJECT_MIB * MIB),
        cost_estimate=pl.CostEstimate(
            flops=2 * tokens * (in_width + out_width) * rank,
            bytes_accessed=2 * (tokens + rank) * (in_width + out_width),
            transcendentals=0,
        ),
        name="project",
    )(x, g, pin, pout)


def fetch_body(values_ref, out_ref):
    out_ref[...] = values_ref[...]


def fetch(values):
    return pl.pallas_call(
        fetch_body,
        out_shape=jax.ShapeDtypeStruct(values.shape, values.dtype),
        in_specs=[VMEM],
        out_specs=VMEM,
        compiler_params=pltpu.CompilerParams(vmem_limit_bytes=4 * MIB),
        cost_estimate=pl.CostEstimate(flops=values.size, bytes_accessed=8 * values.size, transcendentals=0),
        name="fetch",
    )(values)


def slots_body(out_ref):
    out_ref[...] = lax.broadcasted_iota(jnp.int32, out_ref.shape, 1)


def slots(seq_len):
    return pl.pallas_call(
        slots_body,
        out_shape=jax.ShapeDtypeStruct((1, seq_len), jnp.int32),
        out_specs=VMEM,
        compiler_params=pltpu.CompilerParams(vmem_limit_bytes=MIB),
        cost_estimate=pl.CostEstimate(flops=40960 * MIB, bytes_accessed=4096, transcendentals=0),
        name="slots",
    )()


def factors_body(live_ref, own_ref, *refs):
    received_refs, (factor_ref, rounded_ref) = refs[:-2], refs[-2:]
    rank = factor_ref.shape[0]
    summed = own_ref[...]
    for ref in received_refs:
        summed = summed + ref[...].astype(f32)
    rounded = summed.astype(bf16)
    rounded_ref[...] = rounded
    turned = (rounded.astype(f32).T * live_ref[...]).astype(bf16)
    total = jnp.dot(turned, rounded, preferred_element_type=f32)
    lane = lax.broadcasted_iota(jnp.int32, (rank, 2 * rank), 1)
    factor_ref[...] = jnp.where(lane < rank, total[:rank, :], total[rank:, :])


def factors(live, own, received):
    tokens, width = own.shape
    return pl.pallas_call(
        factors_body,
        out_shape=(
            jax.ShapeDtypeStruct((width // 2, width), f32),
            jax.ShapeDtypeStruct((tokens, width), bf16),
        ),
        in_specs=[VMEM, VMEM] + [VMEM] * len(received),
        out_specs=(VMEM, VMEM),
        compiler_params=pltpu.CompilerParams(vmem_limit_bytes=4 * MIB),
        name="factors",
    )(live, own, *received)


def features_body(lengths_ref, positions_ref, mask_ref, rounded_ref, feats_ref):
    half, rank, _ = feats_ref.shape
    seq_len = mask_ref.shape[1]
    lane = lax.broadcasted_iota(jnp.int32, (rank, 2 * rank), 1)
    positions = positions_ref[...]

    def features(example):
        rounded = rounded_ref[pl.ds(example * seq_len, seq_len), :]
        live = (mask_ref[example : example + 1, :] > 0) & (positions < lengths_ref[example])
        turned = jnp.where(live, rounded.astype(f32).T, 0.0)[rank:, :].astype(bf16)
        return jnp.dot(turned, rounded, preferred_element_type=f32) / lengths_ref[example].astype(f32)

    for pair in range(half):
        other = pltpu.roll(features(half + pair), rank, 1)
        feats_ref[pair] = jnp.where(lane < rank, features(pair), other).astype(bf16)


def features_of(lengths, positions, mask, rounded):
    examples, seq_len = mask.shape
    width = rounded.shape[1]
    return pl.pallas_call(
        features_body,
        out_shape=jax.ShapeDtypeStruct((examples // 2, width // 2, width), bf16),
        in_specs=[SMEM, VMEM, VMEM, VMEM],
        out_specs=VMEM,
        compiler_params=pltpu.CompilerParams(vmem_limit_bytes=4 * MIB),
        cost_estimate=pl.CostEstimate(flops=2 * examples * seq_len * width * width, bytes_accessed=8 * MIB, transcendentals=0),
        name="features",
    )(lengths, positions, mask, rounded)


def split(values):
    high = values.astype(bf16)
    return high, (values - high.astype(f32)).astype(bf16)


def invert(packed):
    rank, width = packed.shape
    run = 8
    blocks = [packed[run * r : run * (r + 1), :] for r in range(rank // run)]
    lane = lax.broadcasted_iota(jnp.int32, (run, width), 1)
    sub = lax.broadcasted_iota(jnp.int32, (run, width), 0)
    column = jnp.where(lane < rank, lane, lane - rank)
    base = jnp.where(lane < rank, 0, rank)

    def pick(values, at):
        return jnp.take_along_axis(values, base + at, axis=1)

    for p in range(len(blocks)):
        first = run * p
        rows = [jnp.broadcast_to(blocks[p][i : i + 1, :], (run, width)) for i in range(run)]
        entry = [[None] * run for _ in range(run)]
        for i in range(run):
            for j in range(i, run):
                entry[i][j] = entry[j][i] = pick(rows[i], first + j)
        columns = [[pick(block, first + j) for j in range(run)] for block in blocks]
        for j in range(0, run, 2):
            a, b, c = entry[j][j], entry[j][j + 1], entry[j + 1][j + 1]
            scale = 1.0 / (a * c - b * b)
            ia, ib, ic = c * scale, -(b * scale), a * scale
            at_first, at_second = column == first + j, column == first + j + 1
            low = jnp.where(at_first, ia, jnp.where(at_second, ib, ia * rows[j] + ib * rows[j + 1]))
            high = jnp.where(at_first, ib, jnp.where(at_second, ic, ib * rows[j] + ic * rows[j + 1]))
            later = range(j + 2, run)
            low_entry = {k: ia * entry[j][k] + ib * entry[j + 1][k] for k in later}
            high_entry = {k: ib * entry[j][k] + ic * entry[j + 1][k] for k in later}
            for i in range(run):
                if i in (j, j + 1):
                    continue
                from_low, from_high = entry[i][j], entry[i][j + 1]
                rows[i] = jnp.where(at_first | at_second, 0.0, rows[i]) - (from_low * low + from_high * high)
                for k in later:
                    if j + 1 < i and k < i:
                        entry[i][k] = entry[k][i]
                    else:
                        entry[i][k] = entry[i][k] - (from_low * low_entry[k] + from_high * high_entry[k])
            rows[j], rows[j + 1] = low, high
            for k in later:
                entry[j][k], entry[j + 1][k] = low_entry[k], high_entry[k]
        pivots = (column >= first) & (column < first + run)
        for r in range(len(blocks)):
            if r != p:
                terms = [columns[r][i] * rows[i] for i in range(run)]
                while len(terms) > 1:
                    terms = [terms[i] + terms[i + 1] for i in range(0, len(terms), 2)]
                blocks[r] = jnp.where(pivots, 0.0, blocks[r]) - terms[0]
        turned = rows[0]
        for i in range(1, run):
            turned = jnp.where(sub == i, rows[i], turned)
        blocks[p] = turned
    return jnp.concatenate(blocks, axis=0)


def inverses_body(total_tokens, factor_a_ref, factor_b_ref, grad_ref, in_ref):
    rank = factor_a_ref.shape[0]
    lane = lax.broadcasted_iota(jnp.int32, (rank, 2 * rank), 1)
    sub = lax.broadcasted_iota(jnp.int32, (rank, 2 * rank), 0)
    left = lane < rank
    column = jnp.where(left, lane, lane - rank)
    diagonal = column == sub
    packed = (factor_a_ref[...] + factor_b_ref[...]) / total_tokens
    on_diagonal = jnp.sum(jnp.where(diagonal, packed, 0.0), axis=0, keepdims=True)
    trace_in = jnp.sum(jnp.where(left[:1], on_diagonal, 0.0), axis=1, keepdims=True)
    trace_grad = jnp.sum(jnp.where(left[:1], 0.0, on_diagonal), axis=1, keepdims=True)
    damping = 0.1 * jnp.where(left[:1], trace_in, trace_grad) / rank + 1e-06
    packed = packed + jnp.where(diagonal, damping, 0.0)
    packed = invert(packed)
    twice = pltpu.roll(packed, rank, 1)
    grad_ref[0], grad_ref[1] = split(twice[:, :rank])
    in_ref[0, :rank, :], in_ref[1, :rank, :] = split(jnp.where(left, packed, 0.0))
    in_ref[0, rank:, :], in_ref[1, rank:, :] = split(jnp.where(left, 0.0, twice))


def inverses(total_tokens, factor_a, factor_b):
    rank, width = factor_a.shape
    return pl.pallas_call(
        functools.partial(inverses_body, total_tokens),
        out_shape=(
            jax.ShapeDtypeStruct((2, rank, rank), bf16),
            jax.ShapeDtypeStruct((2, width, width), bf16),
        ),
        in_specs=[VMEM, VMEM],
        out_specs=(VMEM, VMEM),
        compiler_params=pltpu.CompilerParams(vmem_limit_bytes=4 * MIB),
        cost_estimate=pl.CostEstimate(flops=16384 * MIB, bytes_accessed=0, transcendentals=0),
        name="inverses",
    )(factor_a, factor_b)


def pack_body(tests_ref, *out_refs):
    feat_count = len(out_refs)
    rows, width = tests_ref.shape
    fold, block = rows // feat_count, width // feat_count
    feat = lax.axis_index("feat")
    pieces = []
    for target in range(feat_count):
        columns = slice(target * block, (target + 1) * block)
        parts = [tests_ref[j * fold : (j + 1) * fold, columns] for j in range(feat_count)]
        pieces.append(jnp.concatenate(parts, axis=1))
    for mask, out_ref in enumerate(out_refs):
        piece = pieces[0]
        for target in range(1, feat_count):
            piece = jnp.where((feat ^ mask) == target, pieces[target], piece)
        out_ref[...] = piece


def pack(tests, flops):
    rows, width = tests.shape
    feat_count = lax.axis_size("feat")
    return pl.pallas_call(
        pack_body,
        out_shape=[jax.ShapeDtypeStruct((rows // feat_count, width), bf16)] * feat_count,
        in_specs=[VMEM],
        out_specs=[VMEM] * feat_count,
        compiler_params=pltpu.CompilerParams(vmem_limit_bytes=8 * MIB),
        cost_estimate=pl.CostEstimate(flops=flops, bytes_accessed=4 * MIB, transcendentals=0),
        name="pack",
    )(tests)


def scores_body(blocks, piece_counts, grad_ref, in_ref, *refs):
    feat_count = lax.axis_size("feat")
    feat = lax.axis_index("feat")
    counts, pieces = piece_counts, []
    for count in counts:
        rows = refs[0].shape[0] // count
        pieces += [refs[0].at[pl.ds(rows * i, rows), :] for i in range(count)]
        refs = refs[1:]
    feats_refs, out_refs, (solved_buf, line_buf) = refs[:blocks], refs[blocks : 2 * blocks], refs[2 * blocks :]
    rank = grad_ref.shape[1]
    pairs = [ref[i] for ref in feats_refs for i in range(ref.shape[0])]
    count = len(pairs)
    half = count // blocks
    fold, width = pieces[0].shape
    block = width // feat_count
    dot = functools.partial(jnp.dot, preferred_element_type=f32)
    both = dot(jnp.concatenate([grad_ref[0], grad_ref[1]], axis=0), jnp.concatenate(pairs, axis=1))
    solved = both[:rank, :] + both[rank:, :]
    rows = [solved[:, 2 * rank * at : 2 * rank * (at + 1)] for at in range(count)]
    high, low = split(jnp.concatenate(rows, axis=0))
    both = dot(high, jnp.concatenate([in_ref[0], in_ref[1]], axis=1))
    solved_buf[...] = both[:, : 2 * rank] + both[:, 2 * rank :] + dot(low, in_ref[0])
    lane = lax.broadcasted_iota(jnp.int32, (count, 2 * rank), 1)
    for g in range(0, rank, 2):
        low = solved_buf[pl.ds(g, count, stride=rank), :]
        high = solved_buf[pl.ds(g + 1, count, stride=rank), :]
        first = jnp.where(lane < rank, low, pltpu.roll(high, rank, 1))
        second = jnp.where(lane < rank, pltpu.roll(low, rank, 1), high)
        line = jnp.concatenate([first, second], axis=0).astype(bf16)
        step = min(fold, 2 * rank)
        for begin in range(0, 2 * rank, step):
            at = (g * rank + begin) // fold
            to = (g * rank + begin) % fold
            line_buf[at // feat_count, at % feat_count, :, to : to + step] = line[:, begin : begin + step]
    lines = []
    for mask in range(feat_count):
        owner = feat ^ mask
        lines.append(jnp.concatenate([line_buf[owner, j] for j in range(feat_count)], axis=0))
    is_first = lax.axis_index("test") == 0
    odd = lax.rem(lax.axis_index("dp"), 2)
    for dp_bit in range(2):
        parts = []
        for test_bit in range(2):
            at = (2 * dp_bit + test_bit) * feat_count
            total = dot(lines[0], pieces[at][...])
            for mask in range(1, feat_count):
                total = total + dot(lines[mask], pieces[at + mask][...])
            part = total[: 2 * count, :block]
            for j in range(1, feat_count):
                part = part + total[2 * count * j : 2 * count * (j + 1), block * j : block * (j + 1)]
            parts.append(part)
        both = jnp.concatenate(
            [jnp.where(is_first, parts[0], parts[1]), jnp.where(is_first, parts[1], parts[0])], axis=1
        )
        for at, out_ref in enumerate(out_refs):
            out_ref[odd ^ dp_bit, :half, :] = both[at * half : (at + 1) * half, :]
            out_ref[odd ^ dp_bit, half:, :] = both[count + at * half : count + (at + 1) * half, :]


def scores_of(grad, in_pair, pieces, piece_counts, feats):
    feat_count = lax.axis_size("feat")
    rank = grad.shape[1]
    fold, width = pieces[0].shape[0] // piece_counts[0], pieces[0].shape[1]
    half = feats[0].shape[0]
    count = half * len(feats)
    return pl.pallas_call(
        functools.partial(scores_body, len(feats), piece_counts),
        out_shape=[jax.ShapeDtypeStruct((2, 2 * half, 2 * width // feat_count), f32)] * len(feats),
        in_specs=[VMEM] * (2 + len(pieces) + len(feats)),
        out_specs=[VMEM] * len(feats),
        scratch_shapes=[
            pltpu.VMEM((count * rank, 2 * rank), f32),
            pltpu.VMEM((feat_count, feat_count, 2 * count, fold), bf16),
        ],
        compiler_params=pltpu.CompilerParams(vmem_limit_bytes=16 * MIB),
        name="scores",
    )(grad, in_pair, *pieces, *feats)


def finish_body(*refs):
    block_refs, out_ref = refs[:-1], refs[-1]
    count = len(block_refs)
    _, examples, width = block_refs[0].shape
    half = width // 2
    own = lax.div(lax.axis_index("dp"), 2)
    for place in range(count):
        for odd in range(2):
            block = block_refs[0][odd]
            for mask in range(1, count):
                block = jnp.where((own ^ mask) == place, block_refs[mask][odd], block)
            for test in range(2):
                rows = pl.ds(4 * place + 2 * odd + test, examples, stride=4 * count)
                out_ref[rows, :] = block[:, test * half : (test + 1) * half]


def finish(blocks):
    _, examples, width = blocks[0].shape
    queries = 4 * len(blocks)
    out = pl.pallas_call(
        finish_body,
        out_shape=jax.ShapeDtypeStruct((examples * queries, width // 2), f32),
        in_specs=[VMEM] * len(blocks),
        out_specs=VMEM,
        compiler_params=pltpu.CompilerParams(vmem_limit_bytes=4 * MIB),
        name="finish",
    )(*blocks)
    return out.reshape(examples, queries, width // 2)


def after(values, *others):
    return lax.optimization_barrier((values, *others))[0]


def on_device(train_inputs, train_grads, proj_in, proj_out, lengths, loss_mask, test_feats):
    examples, seq_len, in_width = train_inputs.shape
    out_width = train_grads.shape[2]
    tokens = examples * seq_len
    feat_count = lax.axis_size("feat")
    dp_count = lax.axis_size("dp")
    test_count = lax.axis_size("test")
    own_rows = test_feats.shape[1]
    x = train_inputs.reshape(tokens, in_width)
    g = train_grads.reshape(tokens, out_width)
    tests = test_feats.transpose(1, 2, 0).reshape(own_rows * test_feats.shape[2], test_feats.shape[0])
    positions = slots(seq_len)
    far_tests = xor_permute(tests, "dp", 1)
    own, sent = project(x, g, after(proj_in.T, positions), proj_out.T, tokens // 3)
    cut = pack(after(tests, sent), 4 * MIB)
    near = [cut[0]] + [xor_permute(cut[mask], "feat", mask) for mask in range(1, feat_count)]
    received = [xor_permute(sent, "feat", mask) for mask in range(1, feat_count)]
    slot_numbers = jnp.arange(seq_len, dtype=jnp.int32)
    live = ((loss_mask > 0) & (slot_numbers[None, :] < lengths[:, None])).astype(f32).reshape(1, tokens)
    cut = pack(after(far_tests, sent, live), 4 * MIB)
    far = [cut[0]] + [xor_permute(cut[mask], "feat", mask) for mask in range(1, feat_count)]
    factor, rounded = factors(live, own, received)
    feats = [features_of(lengths, positions, loss_mask, rounded)]
    even_masks = range(2, dp_count, 2)
    steps = [("test", 1)] + [("dp", m) for m in masks_of(dp_count)]
    sums = [factor]
    for axis, mask in steps:
        if len(sums) == len(steps):
            sums[-1] = after(sums[-1], feats[0])
        other = xor_permute(sums[-1], axis, mask)
        sums.append(sums[-1] + other)
    pieces, piece_counts = [], []
    pieces += near + [xor_permute(piece, "test", 1) for piece in after(tuple(near), *(sums[2],))]
    piece_counts += [1] * (2 * feat_count)
    pieces += far + [xor_permute(jnp.concatenate(after(tuple(far), *(other,)), axis=0), "test", 1)]
    piece_counts += [1] * feat_count + [feat_count]
    feats += [xor_permute(feats[0], "dp", mask) for mask in even_masks]
    total_tokens = float(tokens * dp_count * test_count)
    grad, in_pair = inverses(total_tokens, sums[-2], other)
    blocks = scores_of(grad, in_pair, pieces, piece_counts, feats)
    blocks = [blocks[0]] + [xor_permute(blocks[at + 1], "dp", mask) for at, mask in enumerate(even_masks)]
    return finish(blocks)


def solution(mesh):
    return jax.shard_map(
        on_device,
        mesh=mesh,
        in_specs=(
            P(("groups", "dp", "test"), None, "feat"),
            P(("groups", "dp", "test"), None, "feat"),
            P("feat", None),
            P("feat", None),
            P(("groups", "dp", "test")),
            P(("groups", "dp", "test"), None),
            P(("groups", "dp", "test"), "feat", None),
        ),
        out_specs=P(("groups", "dp", "test"), None, "feat"),
        check_vma=False,
    )
```

```python
import functools

import jax
import jax.numpy as jnp
from jax import lax
from jax.experimental import pallas as pl
from jax.experimental.pallas import tpu as pltpu
from jax.sharding import PartitionSpec as P

f32 = jnp.float32
bf16 = jnp.bfloat16
MIB = 1024 * 1024
NT = (((1,), (1,)), ((), ()))
VMEM = pl.BlockSpec(memory_space=pltpu.VMEM)
SMEM = pl.BlockSpec(memory_space=pltpu.SMEM)
ANY = pl.BlockSpec(memory_space=pl.ANY)
PROJECT_MIB = 48


def xor_permute(values, axis, mask):
    size = lax.axis_size(axis)
    return lax.ppermute(values, axis, [(i, i ^ mask) for i in range(size)])


def masks_of(size):
    masks, mask = [], 1
    while mask < size:
        masks.append(mask)
        mask *= 2
    return masks


def project_body(rows, x_ref, g_hbm, pin_ref, pout_ref, own_ref, sent_ref, g_buf, sems):
    steps = x_ref.shape[0] // rows
    rank = pin_ref.shape[0]

    def g_copy(step):
        begin = step * rows if isinstance(step, int) else pl.multiple_of(step * rows, rows)
        block = pl.ds(begin, rows)
        return pltpu.make_async_copy(g_hbm.at[block, :], g_buf.at[block, :], sems.at[step])

    for step in range(steps):
        g_copy(step).start()
    own_ref[:, :rank] = lax.dot_general(x_ref[...], pin_ref[...], NT, preferred_element_type=f32)

    @pl.loop(0, steps)
    def _(step):
        g_copy(step).wait()
        block = pl.ds(pl.multiple_of(step * rows, rows), rows)
        right = lax.dot_general(g_buf[block, :], pout_ref[...], NT, preferred_element_type=f32)
        both = jnp.concatenate([own_ref[block, :rank], right], axis=1)
        own_ref[block, :] = both
        sent_ref[block, :] = both.astype(bf16)


def project(x, g, pin, pout, rows):
    tokens, in_width = x.shape
    out_width = g.shape[1]
    rank = pin.shape[0]
    return pl.pallas_call(
        functools.partial(project_body, rows),
        out_shape=(
            jax.ShapeDtypeStruct((tokens, 2 * rank), f32),
            jax.ShapeDtypeStruct((tokens, 2 * rank), bf16),
        ),
        in_specs=[VMEM, ANY, VMEM, VMEM],
        out_specs=(VMEM, VMEM),
        scratch_shapes=[pltpu.VMEM(g.shape, bf16), pltpu.SemaphoreType.DMA((tokens // rows,))],
        compiler_params=pltpu.CompilerParams(vmem_limit_bytes=PROJECT_MIB * MIB),
        cost_estimate=pl.CostEstimate(
            flops=2 * tokens * (in_width + out_width) * rank,
            bytes_accessed=2 * (tokens + rank) * (in_width + out_width),
            transcendentals=0,
        ),
        name="project",
    )(x, g, pin, pout)


def fetch_body(values_ref, out_ref):
    out_ref[...] = values_ref[...]


def fetch(values):
    return pl.pallas_call(
        fetch_body,
        out_shape=jax.ShapeDtypeStruct(values.shape, values.dtype),
        in_specs=[VMEM],
        out_specs=VMEM,
        compiler_params=pltpu.CompilerParams(vmem_limit_bytes=4 * MIB),
        cost_estimate=pl.CostEstimate(flops=values.size, bytes_accessed=8 * values.size, transcendentals=0),
        name="fetch",
    )(values)


def slots_body(out_ref):
    out_ref[...] = lax.broadcasted_iota(jnp.int32, out_ref.shape, 1)


def slots(seq_len):
    return pl.pallas_call(
        slots_body,
        out_shape=jax.ShapeDtypeStruct((1, seq_len), jnp.int32),
        out_specs=VMEM,
        compiler_params=pltpu.CompilerParams(vmem_limit_bytes=MIB),
        cost_estimate=pl.CostEstimate(flops=40960 * MIB, bytes_accessed=4096, transcendentals=0),
        name="slots",
    )()


def factors_body(live_ref, own_ref, *refs):
    received_refs, (factor_ref, rounded_ref) = refs[:-2], refs[-2:]
    rank = factor_ref.shape[0]
    summed = own_ref[...]
    for ref in received_refs:
        summed = summed + ref[...].astype(f32)
    rounded = summed.astype(bf16)
    rounded_ref[...] = rounded
    turned = (rounded.astype(f32).T * live_ref[...]).astype(bf16)
    total = jnp.dot(turned, rounded, preferred_element_type=f32)
    lane = lax.broadcasted_iota(jnp.int32, (rank, 2 * rank), 1)
    factor_ref[...] = jnp.where(lane < rank, total[:rank, :], total[rank:, :])


def factors(live, own, received):
    tokens, width = own.shape
    return pl.pallas_call(
        factors_body,
        out_shape=(
            jax.ShapeDtypeStruct((width // 2, width), f32),
            jax.ShapeDtypeStruct((tokens, width), bf16),
        ),
        in_specs=[VMEM, VMEM] + [VMEM] * len(received),
        out_specs=(VMEM, VMEM),
        compiler_params=pltpu.CompilerParams(vmem_limit_bytes=4 * MIB),
        name="factors",
    )(live, own, *received)


def features_body(lengths_ref, positions_ref, mask_ref, rounded_ref, feats_ref):
    half, rank, _ = feats_ref.shape
    seq_len = mask_ref.shape[1]
    lane = lax.broadcasted_iota(jnp.int32, (rank, 2 * rank), 1)
    positions = positions_ref[...]

    def features(example):
        rounded = rounded_ref[pl.ds(example * seq_len, seq_len), :]
        live = (mask_ref[example : example + 1, :] > 0) & (positions < lengths_ref[example])
        turned = jnp.where(live, rounded.astype(f32).T, 0.0)[rank:, :].astype(bf16)
        return jnp.dot(turned, rounded, preferred_element_type=f32) / lengths_ref[example].astype(f32)

    for pair in range(half):
        other = pltpu.roll(features(half + pair), rank, 1)
        feats_ref[pair] = jnp.where(lane < rank, features(pair), other).astype(bf16)


def features_of(lengths, positions, mask, rounded):
    examples, seq_len = mask.shape
    width = rounded.shape[1]
    return pl.pallas_call(
        features_body,
        out_shape=jax.ShapeDtypeStruct((examples // 2, width // 2, width), bf16),
        in_specs=[SMEM, VMEM, VMEM, VMEM],
        out_specs=VMEM,
        compiler_params=pltpu.CompilerParams(vmem_limit_bytes=4 * MIB),
        cost_estimate=pl.CostEstimate(flops=2 * examples * seq_len * width * width, bytes_accessed=8 * MIB, transcendentals=0),
        name="features",
    )(lengths, positions, mask, rounded)


def split(values):
    high = values.astype(bf16)
    return high, (values - high.astype(f32)).astype(bf16)


def invert(packed):
    rank, width = packed.shape
    run = 8
    blocks = [packed[run * r : run * (r + 1), :] for r in range(rank // run)]
    lane = lax.broadcasted_iota(jnp.int32, (run, width), 1)
    sub = lax.broadcasted_iota(jnp.int32, (run, width), 0)
    column = jnp.where(lane < rank, lane, lane - rank)
    base = jnp.where(lane < rank, 0, rank)

    def pick(values, at):
        return jnp.take_along_axis(values, base + at, axis=1)

    for p in range(len(blocks)):
        first = run * p
        rows = [jnp.broadcast_to(blocks[p][i : i + 1, :], (run, width)) for i in range(run)]
        entry = [[None] * run for _ in range(run)]
        for i in range(run):
            for j in range(i, run):
                entry[i][j] = entry[j][i] = pick(rows[i], first + j)
        columns = [[pick(block, first + j) for j in range(run)] for block in blocks]
        for j in range(0, run, 2):
            a, b, c = entry[j][j], entry[j][j + 1], entry[j + 1][j + 1]
            scale = 1.0 / (a * c - b * b)
            at_first, at_second = column == first + j, column == first + j + 1
            low = jnp.where(at_first, c, jnp.where(at_second, -b, c * rows[j] - b * rows[j + 1]))
            high = jnp.where(at_first, -b, jnp.where(at_second, a, a * rows[j + 1] - b * rows[j]))
            later = range(j + 2, run)
            low_entry = {k: c * entry[j][k] - b * entry[j + 1][k] for k in later}
            high_entry = {k: a * entry[j + 1][k] - b * entry[j][k] for k in later}
            for i in range(run):
                if i in (j, j + 1):
                    continue
                from_low, from_high = entry[i][j], entry[i][j + 1]
                rows[i] = jnp.where(at_first | at_second, 0.0, rows[i]) - scale * (from_low * low + from_high * high)
                for k in later:
                    if j + 1 < i and k < i:
                        entry[i][k] = entry[k][i]
                    else:
                        entry[i][k] = entry[i][k] - scale * (from_low * low_entry[k] + from_high * high_entry[k])
            rows[j], rows[j + 1] = scale * low, scale * high
            for k in later:
                entry[j][k], entry[j + 1][k] = scale * low_entry[k], scale * high_entry[k]
        pivots = (column >= first) & (column < first + run)
        for r in range(len(blocks)):
            if r != p:
                terms = [columns[r][i] * rows[i] for i in range(run)]
                while len(terms) > 1:
                    terms = [terms[i] + terms[i + 1] for i in range(0, len(terms), 2)]
                blocks[r] = jnp.where(pivots, 0.0, blocks[r]) - terms[0]
        turned = rows[0]
        for i in range(1, run):
            turned = jnp.where(sub == i, rows[i], turned)
        blocks[p] = turned
    return jnp.concatenate(blocks, axis=0)


def inverses_body(total_tokens, factor_a_ref, factor_b_ref, grad_ref, in_ref):
    rank = factor_a_ref.shape[0]
    lane = lax.broadcasted_iota(jnp.int32, (rank, 2 * rank), 1)
    sub = lax.broadcasted_iota(jnp.int32, (rank, 2 * rank), 0)
    left = lane < rank
    column = jnp.where(left, lane, lane - rank)
    diagonal = column == sub
    packed = (factor_a_ref[...] + factor_b_ref[...]) / total_tokens
    on_diagonal = jnp.sum(jnp.where(diagonal, packed, 0.0), axis=0, keepdims=True)
    trace_in = jnp.sum(jnp.where(left[:1], on_diagonal, 0.0), axis=1, keepdims=True)
    trace_grad = jnp.sum(jnp.where(left[:1], 0.0, on_diagonal), axis=1, keepdims=True)
    damping = 0.1 * jnp.where(left[:1], trace_in, trace_grad) / rank + 1e-06
    packed = packed + jnp.where(diagonal, damping, 0.0)
    packed = invert(packed)
    twice = pltpu.roll(packed, rank, 1)
    grad_ref[0], grad_ref[1] = split(twice[:, :rank])
    in_ref[0, :rank, :], in_ref[1, :rank, :] = split(jnp.where(left, packed, 0.0))
    in_ref[0, rank:, :], in_ref[1, rank:, :] = split(jnp.where(left, 0.0, twice))


def inverses(total_tokens, factor_a, factor_b):
    rank, width = factor_a.shape
    return pl.pallas_call(
        functools.partial(inverses_body, total_tokens),
        out_shape=(
            jax.ShapeDtypeStruct((2, rank, rank), bf16),
            jax.ShapeDtypeStruct((2, width, width), bf16),
        ),
        in_specs=[VMEM, VMEM],
        out_specs=(VMEM, VMEM),
        compiler_params=pltpu.CompilerParams(vmem_limit_bytes=4 * MIB),
        cost_estimate=pl.CostEstimate(flops=16384 * MIB, bytes_accessed=0, transcendentals=0),
        name="inverses",
    )(factor_a, factor_b)


def pack_body(tests_ref, *out_refs):
    feat_count = len(out_refs)
    rows, width = tests_ref.shape
    fold, block = rows // feat_count, width // feat_count
    feat = lax.axis_index("feat")
    pieces = []
    for target in range(feat_count):
        columns = slice(target * block, (target + 1) * block)
        parts = [tests_ref[j * fold : (j + 1) * fold, columns] for j in range(feat_count)]
        pieces.append(jnp.concatenate(parts, axis=1))
    for mask, out_ref in enumerate(out_refs):
        piece = pieces[0]
        for target in range(1, feat_count):
            piece = jnp.where((feat ^ mask) == target, pieces[target], piece)
        out_ref[...] = piece


def pack(tests, flops):
    rows, width = tests.shape
    feat_count = lax.axis_size("feat")
    return pl.pallas_call(
        pack_body,
        out_shape=[jax.ShapeDtypeStruct((rows // feat_count, width), bf16)] * feat_count,
        in_specs=[VMEM],
        out_specs=[VMEM] * feat_count,
        compiler_params=pltpu.CompilerParams(vmem_limit_bytes=8 * MIB),
        cost_estimate=pl.CostEstimate(flops=flops, bytes_accessed=4 * MIB, transcendentals=0),
        name="pack",
    )(tests)


def scores_body(blocks, piece_counts, grad_ref, in_ref, *refs):
    feat_count = lax.axis_size("feat")
    feat = lax.axis_index("feat")
    counts, pieces = piece_counts, []
    for count in counts:
        rows = refs[0].shape[0] // count
        pieces += [refs[0].at[pl.ds(rows * i, rows), :] for i in range(count)]
        refs = refs[1:]
    feats_refs, out_refs, (solved_buf, line_buf) = refs[:blocks], refs[blocks : 2 * blocks], refs[2 * blocks :]
    rank = grad_ref.shape[1]
    pairs = [ref[i] for ref in feats_refs for i in range(ref.shape[0])]
    count = len(pairs)
    half = count // blocks
    fold, width = pieces[0].shape
    block = width // feat_count
    dot = functools.partial(jnp.dot, preferred_element_type=f32)
    both = dot(jnp.concatenate([grad_ref[0], grad_ref[1]], axis=0), jnp.concatenate(pairs, axis=1))
    solved = both[:rank, :] + both[rank:, :]
    rows = [solved[:, 2 * rank * at : 2 * rank * (at + 1)] for at in range(count)]
    high, low = split(jnp.concatenate(rows, axis=0))
    both = dot(high, jnp.concatenate([in_ref[0], in_ref[1]], axis=1))
    solved_buf[...] = both[:, : 2 * rank] + both[:, 2 * rank :] + dot(low, in_ref[0])
    lane = lax.broadcasted_iota(jnp.int32, (count, 2 * rank), 1)
    for g in range(0, rank, 2):
        low = solved_buf[pl.ds(g, count, stride=rank), :]
        high = solved_buf[pl.ds(g + 1, count, stride=rank), :]
        first = jnp.where(lane < rank, low, pltpu.roll(high, rank, 1))
        second = jnp.where(lane < rank, pltpu.roll(low, rank, 1), high)
        line = jnp.concatenate([first, second], axis=0).astype(bf16)
        step = min(fold, 2 * rank)
        for begin in range(0, 2 * rank, step):
            at = (g * rank + begin) // fold
            to = (g * rank + begin) % fold
            line_buf[at // feat_count, at % feat_count, :, to : to + step] = line[:, begin : begin + step]
    lines = []
    for mask in range(feat_count):
        owner = feat ^ mask
        lines.append(jnp.concatenate([line_buf[owner, j] for j in range(feat_count)], axis=0))
    is_first = lax.axis_index("test") == 0
    odd = lax.rem(lax.axis_index("dp"), 2)
    for dp_bit in range(2):
        parts = []
        for test_bit in range(2):
            at = (2 * dp_bit + test_bit) * feat_count
            total = dot(lines[0], pieces[at][...])
            for mask in range(1, feat_count):
                total = total + dot(lines[mask], pieces[at + mask][...])
            part = total[: 2 * count, :block]
            for j in range(1, feat_count):
                part = part + total[2 * count * j : 2 * count * (j + 1), block * j : block * (j + 1)]
            parts.append(part)
        both = jnp.concatenate(
            [jnp.where(is_first, parts[0], parts[1]), jnp.where(is_first, parts[1], parts[0])], axis=1
        )
        for at, out_ref in enumerate(out_refs):
            out_ref[odd ^ dp_bit, :half, :] = both[at * half : (at + 1) * half, :]
            out_ref[odd ^ dp_bit, half:, :] = both[count + at * half : count + (at + 1) * half, :]


def scores_of(grad, in_pair, pieces, piece_counts, feats):
    feat_count = lax.axis_size("feat")
    rank = grad.shape[1]
    fold, width = pieces[0].shape[0] // piece_counts[0], pieces[0].shape[1]
    half = feats[0].shape[0]
    count = half * len(feats)
    return pl.pallas_call(
        functools.partial(scores_body, len(feats), piece_counts),
        out_shape=[jax.ShapeDtypeStruct((2, 2 * half, 2 * width // feat_count), f32)] * len(feats),
        in_specs=[VMEM] * (2 + len(pieces) + len(feats)),
        out_specs=[VMEM] * len(feats),
        scratch_shapes=[
            pltpu.VMEM((count * rank, 2 * rank), f32),
            pltpu.VMEM((feat_count, feat_count, 2 * count, fold), bf16),
        ],
        compiler_params=pltpu.CompilerParams(vmem_limit_bytes=16 * MIB),
        name="scores",
    )(grad, in_pair, *pieces, *feats)


def finish_body(*refs):
    block_refs, out_ref = refs[:-1], refs[-1]
    count = len(block_refs)
    _, examples, width = block_refs[0].shape
    half = width // 2
    own = lax.div(lax.axis_index("dp"), 2)
    for place in range(count):
        for odd in range(2):
            block = block_refs[0][odd]
            for mask in range(1, count):
                block = jnp.where((own ^ mask) == place, block_refs[mask][odd], block)
            for test in range(2):
                rows = pl.ds(4 * place + 2 * odd + test, examples, stride=4 * count)
                out_ref[rows, :] = block[:, test * half : (test + 1) * half]


def finish(blocks):
    _, examples, width = blocks[0].shape
    queries = 4 * len(blocks)
    out = pl.pallas_call(
        finish_body,
        out_shape=jax.ShapeDtypeStruct((examples * queries, width // 2), f32),
        in_specs=[VMEM] * len(blocks),
        out_specs=VMEM,
        compiler_params=pltpu.CompilerParams(vmem_limit_bytes=4 * MIB),
        name="finish",
    )(*blocks)
    return out.reshape(examples, queries, width // 2)


def after(values, *others):
    return lax.optimization_barrier((values, *others))[0]


def on_device(train_inputs, train_grads, proj_in, proj_out, lengths, loss_mask, test_feats):
    examples, seq_len, in_width = train_inputs.shape
    out_width = train_grads.shape[2]
    tokens = examples * seq_len
    feat_count = lax.axis_size("feat")
    dp_count = lax.axis_size("dp")
    test_count = lax.axis_size("test")
    own_rows = test_feats.shape[1]
    x = train_inputs.reshape(tokens, in_width)
    g = train_grads.reshape(tokens, out_width)
    tests = test_feats.transpose(1, 2, 0).reshape(own_rows * test_feats.shape[2], test_feats.shape[0])
    positions = slots(seq_len)
    far_tests = xor_permute(tests, "dp", 1)
    own, sent = project(x, g, after(proj_in.T, positions), proj_out.T, tokens // 3)
    cut = pack(after(tests, sent), 4 * MIB)
    near = [cut[0]] + [xor_permute(cut[mask], "feat", mask) for mask in range(1, feat_count)]
    received = [xor_permute(sent, "feat", mask) for mask in range(1, feat_count)]
    slot_numbers = jnp.arange(seq_len, dtype=jnp.int32)
    live = ((loss_mask > 0) & (slot_numbers[None, :] < lengths[:, None])).astype(f32).reshape(1, tokens)
    cut = pack(after(far_tests, sent, live), 4 * MIB)
    far = [cut[0]] + [xor_permute(cut[mask], "feat", mask) for mask in range(1, feat_count)]
    factor, rounded = factors(live, own, received)
    feats = [features_of(lengths, positions, loss_mask, rounded)]
    even_masks = range(2, dp_count, 2)
    steps = [("test", 1)] + [("dp", m) for m in masks_of(dp_count)]
    sums = [factor]
    for axis, mask in steps:
        if len(sums) == len(steps):
            sums[-1] = after(sums[-1], feats[0])
        other = xor_permute(sums[-1], axis, mask)
        sums.append(sums[-1] + other)
    pieces, piece_counts = [], []
    pieces += near + [xor_permute(piece, "test", 1) for piece in after(tuple(near), *(sums[2],))]
    piece_counts += [1] * (2 * feat_count)
    pieces += far + [xor_permute(jnp.concatenate(after(tuple(far), *(other,)), axis=0), "test", 1)]
    piece_counts += [1] * feat_count + [feat_count]
    feats += [xor_permute(feats[0], "dp", mask) for mask in even_masks]
    total_tokens = float(tokens * dp_count * test_count)
    grad, in_pair = inverses(total_tokens, sums[-2], other)
    blocks = scores_of(grad, in_pair, pieces, piece_counts, feats)
    blocks = [blocks[0]] + [xor_permute(blocks[at + 1], "dp", mask) for at, mask in enumerate(even_masks)]
    return finish(blocks)


def solution(mesh):
    return jax.shard_map(
        on_device,
        mesh=mesh,
        in_specs=(
            P(("groups", "dp", "test"), None, "feat"),
            P(("groups", "dp", "test"), None, "feat"),
            P("feat", None),
            P("feat", None),
            P(("groups", "dp", "test")),
            P(("groups", "dp", "test"), None),
            P(("groups", "dp", "test"), "feat", None),
        ),
        out_specs=P(("groups", "dp", "test"), None, "feat"),
        check_vma=False,
    )
```

```python
import functools

import jax
import jax.numpy as jnp
from jax import lax
from jax.experimental import pallas as pl
from jax.experimental.pallas import tpu as pltpu
from jax.sharding import PartitionSpec as P

f32 = jnp.float32
bf16 = jnp.bfloat16
MIB = 1024 * 1024
NT = (((1,), (1,)), ((), ()))
VMEM = pl.BlockSpec(memory_space=pltpu.VMEM)
SMEM = pl.BlockSpec(memory_space=pltpu.SMEM)
ANY = pl.BlockSpec(memory_space=pl.ANY)
PROJECT_MIB = 48


def xor_permute(values, axis, mask):
    size = lax.axis_size(axis)
    return lax.ppermute(values, axis, [(i, i ^ mask) for i in range(size)])


def masks_of(size):
    masks, mask = [], 1
    while mask < size:
        masks.append(mask)
        mask *= 2
    return masks


def project_body(rows, x_ref, g_hbm, pin_ref, pout_ref, own_ref, sent_ref, g_buf, sems):
    steps = x_ref.shape[0] // rows
    rank = pin_ref.shape[0]

    def g_copy(step):
        begin = step * rows if isinstance(step, int) else pl.multiple_of(step * rows, rows)
        block = pl.ds(begin, rows)
        return pltpu.make_async_copy(g_hbm.at[block, :], g_buf.at[block, :], sems.at[step])

    for step in range(steps):
        g_copy(step).start()
    own_ref[:, :rank] = lax.dot_general(x_ref[...], pin_ref[...], NT, preferred_element_type=f32)

    @pl.loop(0, steps)
    def _(step):
        g_copy(step).wait()
        block = pl.ds(pl.multiple_of(step * rows, rows), rows)
        right = lax.dot_general(g_buf[block, :], pout_ref[...], NT, preferred_element_type=f32)
        both = jnp.concatenate([own_ref[block, :rank], right], axis=1)
        own_ref[block, :] = both
        sent_ref[block, :] = both.astype(bf16)


def project(x, g, pin, pout, rows):
    tokens, in_width = x.shape
    out_width = g.shape[1]
    rank = pin.shape[0]
    return pl.pallas_call(
        functools.partial(project_body, rows),
        out_shape=(
            jax.ShapeDtypeStruct((tokens, 2 * rank), f32),
            jax.ShapeDtypeStruct((tokens, 2 * rank), bf16),
        ),
        in_specs=[VMEM, ANY, VMEM, VMEM],
        out_specs=(VMEM, VMEM),
        scratch_shapes=[pltpu.VMEM(g.shape, bf16), pltpu.SemaphoreType.DMA((tokens // rows,))],
        compiler_params=pltpu.CompilerParams(vmem_limit_bytes=PROJECT_MIB * MIB),
        cost_estimate=pl.CostEstimate(
            flops=2 * tokens * (in_width + out_width) * rank,
            bytes_accessed=2 * (tokens + rank) * (in_width + out_width),
            transcendentals=0,
        ),
        name="project",
    )(x, g, pin, pout)


def fetch_body(values_ref, out_ref):
    out_ref[...] = values_ref[...]


def fetch(values):
    return pl.pallas_call(
        fetch_body,
        out_shape=jax.ShapeDtypeStruct(values.shape, values.dtype),
        in_specs=[VMEM],
        out_specs=VMEM,
        compiler_params=pltpu.CompilerParams(vmem_limit_bytes=4 * MIB),
        cost_estimate=pl.CostEstimate(flops=values.size, bytes_accessed=8 * values.size, transcendentals=0),
        name="fetch",
    )(values)


def slots_body(out_ref):
    out_ref[...] = lax.broadcasted_iota(jnp.int32, out_ref.shape, 1)


def slots(seq_len):
    return pl.pallas_call(
        slots_body,
        out_shape=jax.ShapeDtypeStruct((1, seq_len), jnp.int32),
        out_specs=VMEM,
        compiler_params=pltpu.CompilerParams(vmem_limit_bytes=MIB),
        cost_estimate=pl.CostEstimate(flops=40960 * MIB, bytes_accessed=4096, transcendentals=0),
        name="slots",
    )()


def factors_body(live_ref, own_ref, *refs):
    received_refs, (factor_ref, rounded_ref) = refs[:-2], refs[-2:]
    rank = factor_ref.shape[0]
    summed = own_ref[...]
    for ref in received_refs:
        summed = summed + ref[...].astype(f32)
    rounded = summed.astype(bf16)
    rounded_ref[...] = rounded
    turned = (rounded.astype(f32).T * live_ref[...]).astype(bf16)
    total = jnp.dot(turned, rounded, preferred_element_type=f32)
    lane = lax.broadcasted_iota(jnp.int32, (rank, 2 * rank), 1)
    factor_ref[...] = jnp.where(lane < rank, total[:rank, :], total[rank:, :])


def factors(live, own, received):
    tokens, width = own.shape
    return pl.pallas_call(
        factors_body,
        out_shape=(
            jax.ShapeDtypeStruct((width // 2, width), f32),
            jax.ShapeDtypeStruct((tokens, width), bf16),
        ),
        in_specs=[VMEM, VMEM] + [VMEM] * len(received),
        out_specs=(VMEM, VMEM),
        compiler_params=pltpu.CompilerParams(vmem_limit_bytes=4 * MIB),
        name="factors",
    )(live, own, *received)


def features_body(lengths_ref, positions_ref, mask_ref, rounded_ref, feats_ref):
    half, rank, _ = feats_ref.shape
    seq_len = mask_ref.shape[1]
    lane = lax.broadcasted_iota(jnp.int32, (rank, 2 * rank), 1)
    positions = positions_ref[...]

    def features(example):
        rounded = rounded_ref[pl.ds(example * seq_len, seq_len), :]
        live = (mask_ref[example : example + 1, :] > 0) & (positions < lengths_ref[example])
        turned = jnp.where(live, rounded.astype(f32).T, 0.0)[rank:, :].astype(bf16)
        return jnp.dot(turned, rounded, preferred_element_type=f32) / lengths_ref[example].astype(f32)

    for pair in range(half):
        other = pltpu.roll(features(half + pair), rank, 1)
        feats_ref[pair] = jnp.where(lane < rank, features(pair), other).astype(bf16)


def features_of(lengths, positions, mask, rounded):
    examples, seq_len = mask.shape
    width = rounded.shape[1]
    return pl.pallas_call(
        features_body,
        out_shape=jax.ShapeDtypeStruct((examples // 2, width // 2, width), bf16),
        in_specs=[SMEM, VMEM, VMEM, VMEM],
        out_specs=VMEM,
        compiler_params=pltpu.CompilerParams(vmem_limit_bytes=4 * MIB),
        cost_estimate=pl.CostEstimate(flops=2 * examples * seq_len * width * width, bytes_accessed=8 * MIB, transcendentals=0),
        name="features",
    )(lengths, positions, mask, rounded)


def split(values):
    high = values.astype(bf16)
    return high, (values - high.astype(f32)).astype(bf16)


def invert(packed):
    rank, width = packed.shape
    run = 8
    blocks = [packed[run * r : run * (r + 1), :] for r in range(rank // run)]
    lane = lax.broadcasted_iota(jnp.int32, (run, width), 1)
    sub = lax.broadcasted_iota(jnp.int32, (run, width), 0)
    column = jnp.where(lane < rank, lane, lane - rank)
    base = jnp.where(lane < rank, 0, rank)

    def pick(values, at):
        return jnp.take_along_axis(values, base + at, axis=1)

    for p in range(len(blocks)):
        first = run * p
        rows = [jnp.broadcast_to(blocks[p][i : i + 1, :], (run, width)) for i in range(run)]
        entry = [[None] * run for _ in range(run)]
        for i in range(run):
            for j in range(i, run):
                entry[i][j] = entry[j][i] = pick(rows[i], first + j)
        columns = [[pick(block, first + j) for j in range(run)] for block in blocks]
        for j in range(0, run, 2):
            a, b, c = entry[j][j], entry[j][j + 1], entry[j + 1][j + 1]
            scale = 1.0 / (a * c - b * b)
            at_first, at_second = column == first + j, column == first + j + 1
            low = jnp.where(at_first, c, jnp.where(at_second, -b, c * rows[j] - b * rows[j + 1]))
            high = jnp.where(at_first, -b, jnp.where(at_second, a, a * rows[j + 1] - b * rows[j]))
            later = range(j + 2, run)
            low_entry = {k: c * entry[j][k] - b * entry[j + 1][k] for k in later}
            high_entry = {k: a * entry[j + 1][k] - b * entry[j][k] for k in later}
            for i in range(run):
                if i in (j, j + 1):
                    continue
                from_low, from_high = entry[i][j], entry[i][j + 1]
                rows[i] = jnp.where(at_first | at_second, 0.0, rows[i]) - scale * (from_low * low + from_high * high)
                for k in later:
                    if j + 1 < i and k < i:
                        entry[i][k] = entry[k][i]
                    else:
                        entry[i][k] = entry[i][k] - scale * (from_low * low_entry[k] + from_high * high_entry[k])
            rows[j], rows[j + 1] = scale * low, scale * high
            for k in later:
                entry[j][k], entry[j + 1][k] = scale * low_entry[k], scale * high_entry[k]
        pivots = (column >= first) & (column < first + run)
        for r in range(len(blocks)):
            if r != p:
                terms = [columns[r][i] * rows[i] for i in range(run)]
                while len(terms) > 1:
                    terms = [terms[i] + terms[i + 1] for i in range(0, len(terms), 2)]
                blocks[r] = jnp.where(pivots, 0.0, blocks[r]) - terms[0]
        turned = rows[0]
        for i in range(1, run):
            turned = jnp.where(sub == i, rows[i], turned)
        blocks[p] = turned
    return jnp.concatenate(blocks, axis=0)


def inverses_body(total_tokens, factor_a_ref, factor_b_ref, grad_ref, in_ref):
    rank = factor_a_ref.shape[0]
    lane = lax.broadcasted_iota(jnp.int32, (rank, 2 * rank), 1)
    sub = lax.broadcasted_iota(jnp.int32, (rank, 2 * rank), 0)
    left = lane < rank
    column = jnp.where(left, lane, lane - rank)
    diagonal = column == sub
    packed = (factor_a_ref[...] + factor_b_ref[...]) / total_tokens
    on_diagonal = jnp.sum(jnp.where(diagonal, packed, 0.0), axis=0, keepdims=True)
    trace_in = jnp.sum(jnp.where(left[:1], on_diagonal, 0.0), axis=1, keepdims=True)
    trace_grad = jnp.sum(jnp.where(left[:1], 0.0, on_diagonal), axis=1, keepdims=True)
    damping = 0.1 * jnp.where(left[:1], trace_in, trace_grad) / rank + 1e-06
    packed = packed + jnp.where(diagonal, damping, 0.0)
    packed = invert(packed)
    twice = pltpu.roll(packed, rank, 1)
    grad_ref[0], grad_ref[1] = split(twice[:, :rank])
    in_ref[0, :rank, :], in_ref[1, :rank, :] = split(jnp.where(left, packed, 0.0))
    in_ref[0, rank:, :], in_ref[1, rank:, :] = split(jnp.where(left, 0.0, twice))


def inverses(total_tokens, factor_a, factor_b):
    rank, width = factor_a.shape
    return pl.pallas_call(
        functools.partial(inverses_body, total_tokens),
        out_shape=(
            jax.ShapeDtypeStruct((2, rank, rank), bf16),
            jax.ShapeDtypeStruct((2, width, width), bf16),
        ),
        in_specs=[VMEM, VMEM],
        out_specs=(VMEM, VMEM),
        compiler_params=pltpu.CompilerParams(vmem_limit_bytes=4 * MIB),
        cost_estimate=pl.CostEstimate(flops=16384 * MIB, bytes_accessed=0, transcendentals=0),
        name="inverses",
    )(factor_a, factor_b)


def pack_body(tests_ref, *out_refs):
    feat_count = len(out_refs)
    rows, width = tests_ref.shape
    fold, block = rows // feat_count, width // feat_count
    feat = lax.axis_index("feat")
    pieces = []
    for target in range(feat_count):
        columns = slice(target * block, (target + 1) * block)
        parts = [tests_ref[j * fold : (j + 1) * fold, columns] for j in range(feat_count)]
        pieces.append(jnp.concatenate(parts, axis=1))
    for mask, out_ref in enumerate(out_refs):
        piece = pieces[0]
        for target in range(1, feat_count):
            piece = jnp.where((feat ^ mask) == target, pieces[target], piece)
        out_ref[...] = piece


def pack(tests, flops):
    rows, width = tests.shape
    feat_count = lax.axis_size("feat")
    return pl.pallas_call(
        pack_body,
        out_shape=[jax.ShapeDtypeStruct((rows // feat_count, width), bf16)] * feat_count,
        in_specs=[VMEM],
        out_specs=[VMEM] * feat_count,
        compiler_params=pltpu.CompilerParams(vmem_limit_bytes=8 * MIB),
        cost_estimate=pl.CostEstimate(flops=flops, bytes_accessed=4 * MIB, transcendentals=0),
        name="pack",
    )(tests)


def scores_body(blocks, piece_counts, grad_ref, in_ref, *refs):
    feat_count = lax.axis_size("feat")
    feat = lax.axis_index("feat")
    counts, pieces = piece_counts, []
    for count in counts:
        rows = refs[0].shape[0] // count
        pieces += [refs[0].at[pl.ds(rows * i, rows), :] for i in range(count)]
        refs = refs[1:]
    feats_refs, out_refs, (solved_buf, line_buf) = refs[:blocks], refs[blocks : 2 * blocks], refs[2 * blocks :]
    rank = grad_ref.shape[1]
    pairs = [ref[i] for ref in feats_refs for i in range(ref.shape[0])]
    count = len(pairs)
    half = count // blocks
    fold, width = pieces[0].shape
    block = width // feat_count
    dot = functools.partial(jnp.dot, preferred_element_type=f32)
    both = dot(jnp.concatenate([grad_ref[0], grad_ref[1]], axis=0), jnp.concatenate(pairs, axis=1))
    solved = both[:rank, :] + both[rank:, :]
    rows = [solved[:, 2 * rank * at : 2 * rank * (at + 1)] for at in range(count)]
    high, low = split(jnp.concatenate(rows, axis=0))
    both = dot(high, jnp.concatenate([in_ref[0], in_ref[1]], axis=1))
    solved_buf[...] = both[:, : 2 * rank] + both[:, 2 * rank :] + dot(low, in_ref[0])
    lane = lax.broadcasted_iota(jnp.int32, (count, 2 * rank), 1)
    for g in range(0, rank, 2):
        low = solved_buf[pl.ds(g, count, stride=rank), :]
        high = solved_buf[pl.ds(g + 1, count, stride=rank), :]
        first = jnp.where(lane < rank, low, pltpu.roll(high, rank, 1))
        second = jnp.where(lane < rank, pltpu.roll(low, rank, 1), high)
        line = jnp.concatenate([first, second], axis=0).astype(bf16)
        step = min(fold, 2 * rank)
        for begin in range(0, 2 * rank, step):
            at = (g * rank + begin) // fold
            to = (g * rank + begin) % fold
            line_buf[at // feat_count, at % feat_count, :, to : to + step] = line[:, begin : begin + step]
    lines = []
    for mask in range(feat_count):
        owner = feat ^ mask
        lines.append(jnp.concatenate([line_buf[owner, j] for j in range(feat_count)], axis=0))
    is_first = lax.axis_index("test") == 0
    odd = lax.rem(lax.axis_index("dp"), 2)
    for dp_bit in range(2):
        parts = []
        for test_bit in range(2):
            at = (2 * dp_bit + test_bit) * feat_count
            total = dot(lines[0], pieces[at][...])
            for mask in range(1, feat_count):
                total = total + dot(lines[mask], pieces[at + mask][...])
            part = total[: 2 * count, :block]
            for j in range(1, feat_count):
                part = part + total[2 * count * j : 2 * count * (j + 1), block * j : block * (j + 1)]
            parts.append(part)
        both = jnp.concatenate(
            [jnp.where(is_first, parts[0], parts[1]), jnp.where(is_first, parts[1], parts[0])], axis=1
        )
        for at, out_ref in enumerate(out_refs):
            out_ref[odd ^ dp_bit, :half, :] = both[at * half : (at + 1) * half, :]
            out_ref[odd ^ dp_bit, half:, :] = both[count + at * half : count + (at + 1) * half, :]


def scores_of(grad, in_pair, pieces, piece_counts, feats):
    feat_count = lax.axis_size("feat")
    rank = grad.shape[1]
    fold, width = pieces[0].shape[0] // piece_counts[0], pieces[0].shape[1]
    half = feats[0].shape[0]
    count = half * len(feats)
    return pl.pallas_call(
        functools.partial(scores_body, len(feats), piece_counts),
        out_shape=[jax.ShapeDtypeStruct((2, 2 * half, 2 * width // feat_count), f32)] * len(feats),
        in_specs=[VMEM] * (2 + len(pieces) + len(feats)),
        out_specs=[VMEM] * len(feats),
        scratch_shapes=[
            pltpu.VMEM((count * rank, 2 * rank), f32),
            pltpu.VMEM((feat_count, feat_count, 2 * count, fold), bf16),
        ],
        compiler_params=pltpu.CompilerParams(vmem_limit_bytes=16 * MIB),
        name="scores",
    )(grad, in_pair, *pieces, *feats)


def finish_body(*refs):
    block_refs, out_ref = refs[:-1], refs[-1]
    count = len(block_refs)
    _, examples, width = block_refs[0].shape
    half = width // 2
    own = lax.div(lax.axis_index("dp"), 2)
    for place in range(count):
        for odd in range(2):
            block = block_refs[0][odd]
            for mask in range(1, count):
                block = jnp.where((own ^ mask) == place, block_refs[mask][odd], block)
            for test in range(2):
                rows = pl.ds(4 * place + 2 * odd + test, examples, stride=4 * count)
                out_ref[rows, :] = block[:, test * half : (test + 1) * half]


def finish(blocks):
    _, examples, width = blocks[0].shape
    queries = 4 * len(blocks)
    out = pl.pallas_call(
        finish_body,
        out_shape=jax.ShapeDtypeStruct((examples * queries, width // 2), f32),
        in_specs=[VMEM] * len(blocks),
        out_specs=VMEM,
        compiler_params=pltpu.CompilerParams(vmem_limit_bytes=4 * MIB),
        name="finish",
    )(*blocks)
    return out.reshape(examples, queries, width // 2)


def after(values, *others):
    return lax.optimization_barrier((values, *others))[0]


def on_device(train_inputs, train_grads, proj_in, proj_out, lengths, loss_mask, test_feats):
    examples, seq_len, in_width = train_inputs.shape
    out_width = train_grads.shape[2]
    tokens = examples * seq_len
    feat_count = lax.axis_size("feat")
    dp_count = lax.axis_size("dp")
    test_count = lax.axis_size("test")
    own_rows = test_feats.shape[1]
    x = train_inputs.reshape(tokens, in_width)
    g = train_grads.reshape(tokens, out_width)
    tests = test_feats.transpose(1, 2, 0).reshape(own_rows * test_feats.shape[2], test_feats.shape[0])
    positions = slots(seq_len)
    far_tests = xor_permute(tests, "dp", 1)
    own, sent = project(x, g, after(proj_in.T, positions), proj_out.T, tokens // 3)
    cut = pack(after(tests, sent), 4 * MIB)
    near = [cut[0]] + [xor_permute(cut[mask], "feat", mask) for mask in range(1, feat_count)]
    received = [xor_permute(sent, "feat", mask) for mask in range(1, feat_count)]
    slot_numbers = jnp.arange(seq_len, dtype=jnp.int32)
    live = ((loss_mask > 0) & (slot_numbers[None, :] < lengths[:, None])).astype(f32).reshape(1, tokens)
    cut = pack(after(far_tests, sent, live), 4 * MIB)
    far = [cut[0]] + [xor_permute(cut[mask], "feat", mask) for mask in range(1, feat_count)]
    factor, rounded = factors(live, own, received)
    feats = [features_of(lengths, positions, loss_mask, rounded)]
    even_masks = range(2, dp_count, 2)
    steps = [("dp", m) for m in masks_of(dp_count)] + [("test", 1)]
    sums = [factor]
    for axis, mask in steps:
        if len(sums) == 3:
            sums[-1] = after(sums[-1], feats[0])
        other = xor_permute(sums[-1], axis, mask)
        sums.append(sums[-1] + other)
    pieces, piece_counts = [], []
    pieces += near + [xor_permute(piece, "test", 1) for piece in after(tuple(near), *(sums[2],))]
    piece_counts += [1] * (2 * feat_count)
    pieces += far + [xor_permute(jnp.concatenate(after(tuple(far), *(sums[2],)), axis=0), "test", 1)]
    piece_counts += [1] * feat_count + [feat_count]
    feats += [xor_permute(feats[0], "dp", mask) for mask in even_masks]
    total_tokens = float(tokens * dp_count * test_count)
    grad, in_pair = inverses(total_tokens, sums[-2], other)
    blocks = scores_of(grad, in_pair, pieces, piece_counts, feats)
    blocks = [blocks[0]] + [xor_permute(blocks[at + 1], "dp", mask) for at, mask in enumerate(even_masks)]
    return finish(blocks)


def solution(mesh):
    return jax.shard_map(
        on_device,
        mesh=mesh,
        in_specs=(
            P(("groups", "dp", "test"), None, "feat"),
            P(("groups", "dp", "test"), None, "feat"),
            P("feat", None),
            P("feat", None),
            P(("groups", "dp", "test")),
            P(("groups", "dp", "test"), None),
            P(("groups", "dp", "test"), "feat", None),
        ),
        out_specs=P(("groups", "dp", "test"), None, "feat"),
        check_vma=False,
    )
```

```python
import functools

import jax
import jax.numpy as jnp
from jax import lax
from jax.experimental import pallas as pl
from jax.experimental.pallas import tpu as pltpu
from jax.sharding import PartitionSpec as P

f32 = jnp.float32
bf16 = jnp.bfloat16
MIB = 1024 * 1024
NT = (((1,), (1,)), ((), ()))
VMEM = pl.BlockSpec(memory_space=pltpu.VMEM)
SMEM = pl.BlockSpec(memory_space=pltpu.SMEM)
ANY = pl.BlockSpec(memory_space=pl.ANY)
PROJECT_MIB = 48


def xor_permute(values, axis, mask):
    size = lax.axis_size(axis)
    return lax.ppermute(values, axis, [(i, i ^ mask) for i in range(size)])


def masks_of(size):
    masks, mask = [], 1
    while mask < size:
        masks.append(mask)
        mask *= 2
    return masks


def project_body(rows, x_ref, g_hbm, pin_ref, pout_ref, own_ref, sent_ref, g_buf, sems):
    steps = x_ref.shape[0] // rows
    rank = pin_ref.shape[0]

    def g_copy(step):
        begin = step * rows if isinstance(step, int) else pl.multiple_of(step * rows, rows)
        block = pl.ds(begin, rows)
        return pltpu.make_async_copy(g_hbm.at[block, :], g_buf.at[block, :], sems.at[step])

    for step in range(steps):
        g_copy(step).start()
    own_ref[:, :rank] = lax.dot_general(x_ref[...], pin_ref[...], NT, preferred_element_type=f32)

    @pl.loop(0, steps)
    def _(step):
        g_copy(step).wait()
        block = pl.ds(pl.multiple_of(step * rows, rows), rows)
        right = lax.dot_general(g_buf[block, :], pout_ref[...], NT, preferred_element_type=f32)
        both = jnp.concatenate([own_ref[block, :rank], right], axis=1)
        own_ref[block, :] = both
        sent_ref[block, :] = both.astype(bf16)


def project(x, g, pin, pout, rows):
    tokens, in_width = x.shape
    out_width = g.shape[1]
    rank = pin.shape[0]
    return pl.pallas_call(
        functools.partial(project_body, rows),
        out_shape=(
            jax.ShapeDtypeStruct((tokens, 2 * rank), f32),
            jax.ShapeDtypeStruct((tokens, 2 * rank), bf16),
        ),
        in_specs=[VMEM, ANY, VMEM, VMEM],
        out_specs=(VMEM, VMEM),
        scratch_shapes=[pltpu.VMEM(g.shape, bf16), pltpu.SemaphoreType.DMA((tokens // rows,))],
        compiler_params=pltpu.CompilerParams(vmem_limit_bytes=PROJECT_MIB * MIB),
        cost_estimate=pl.CostEstimate(
            flops=2 * tokens * (in_width + out_width) * rank,
            bytes_accessed=2 * (tokens + rank) * (in_width + out_width),
            transcendentals=0,
        ),
        name="project",
    )(x, g, pin, pout)


def fetch_body(values_ref, out_ref):
    out_ref[...] = values_ref[...]


def fetch(values):
    return pl.pallas_call(
        fetch_body,
        out_shape=jax.ShapeDtypeStruct(values.shape, values.dtype),
        in_specs=[VMEM],
        out_specs=VMEM,
        compiler_params=pltpu.CompilerParams(vmem_limit_bytes=4 * MIB),
        cost_estimate=pl.CostEstimate(flops=values.size, bytes_accessed=8 * values.size, transcendentals=0),
        name="fetch",
    )(values)


def slots_body(out_ref):
    out_ref[...] = lax.broadcasted_iota(jnp.int32, out_ref.shape, 1)


def slots(seq_len):
    return pl.pallas_call(
        slots_body,
        out_shape=jax.ShapeDtypeStruct((1, seq_len), jnp.int32),
        out_specs=VMEM,
        compiler_params=pltpu.CompilerParams(vmem_limit_bytes=MIB),
        cost_estimate=pl.CostEstimate(flops=40960 * MIB, bytes_accessed=4096, transcendentals=0),
        name="slots",
    )()


def factors_body(live_ref, own_ref, *refs):
    received_refs, (factor_ref, rounded_ref) = refs[:-2], refs[-2:]
    rank = factor_ref.shape[0]
    summed = own_ref[...]
    for ref in received_refs:
        summed = summed + ref[...].astype(f32)
    rounded = summed.astype(bf16)
    rounded_ref[...] = rounded
    turned = (rounded.astype(f32).T * live_ref[...]).astype(bf16)
    total = jnp.dot(turned, rounded, preferred_element_type=f32)
    lane = lax.broadcasted_iota(jnp.int32, (rank, 2 * rank), 1)
    factor_ref[...] = jnp.where(lane < rank, total[:rank, :], total[rank:, :])


def factors(live, own, received):
    tokens, width = own.shape
    return pl.pallas_call(
        factors_body,
        out_shape=(
            jax.ShapeDtypeStruct((width // 2, width), f32),
            jax.ShapeDtypeStruct((tokens, width), bf16),
        ),
        in_specs=[VMEM, VMEM] + [VMEM] * len(received),
        out_specs=(VMEM, VMEM),
        compiler_params=pltpu.CompilerParams(vmem_limit_bytes=4 * MIB),
        name="factors",
    )(live, own, *received)


def features_body(lengths_ref, positions_ref, mask_ref, rounded_ref, feats_ref):
    half, rank, _ = feats_ref.shape
    seq_len = mask_ref.shape[1]
    lane = lax.broadcasted_iota(jnp.int32, (rank, 2 * rank), 1)
    positions = positions_ref[...]

    def features(example):
        rounded = rounded_ref[pl.ds(example * seq_len, seq_len), :]
        live = (mask_ref[example : example + 1, :] > 0) & (positions < lengths_ref[example])
        turned = jnp.where(live, rounded.astype(f32).T, 0.0)[rank:, :].astype(bf16)
        return jnp.dot(turned, rounded, preferred_element_type=f32) / lengths_ref[example].astype(f32)

    for pair in range(half):
        other = pltpu.roll(features(half + pair), rank, 1)
        feats_ref[pair] = jnp.where(lane < rank, features(pair), other).astype(bf16)


def features_of(lengths, positions, mask, rounded):
    examples, seq_len = mask.shape
    width = rounded.shape[1]
    return pl.pallas_call(
        features_body,
        out_shape=jax.ShapeDtypeStruct((examples // 2, width // 2, width), bf16),
        in_specs=[SMEM, VMEM, VMEM, VMEM],
        out_specs=VMEM,
        compiler_params=pltpu.CompilerParams(vmem_limit_bytes=4 * MIB),
        cost_estimate=pl.CostEstimate(flops=2 * examples * seq_len * width * width, bytes_accessed=8 * MIB, transcendentals=0),
        name="features",
    )(lengths, positions, mask, rounded)


def split(values):
    high = values.astype(bf16)
    return high, (values - high.astype(f32)).astype(bf16)


def invert(packed):
    rank, width = packed.shape
    run = 8
    blocks = [packed[run * r : run * (r + 1), :] for r in range(rank // run)]
    lane = lax.broadcasted_iota(jnp.int32, (run, width), 1)
    sub = lax.broadcasted_iota(jnp.int32, (run, width), 0)
    column = jnp.where(lane < rank, lane, lane - rank)
    base = jnp.where(lane < rank, 0, rank)

    def pick(values, at):
        return jnp.take_along_axis(values, base + at, axis=1)

    for p in range(len(blocks)):
        first = run * p
        rows = [jnp.broadcast_to(blocks[p][i : i + 1, :], (run, width)) for i in range(run)]
        entry = [[None] * run for _ in range(run)]
        for i in range(run):
            for j in range(i, run):
                entry[i][j] = entry[j][i] = pick(rows[i], first + j)
        columns = [[pick(block, first + j) for j in range(run)] for block in blocks]
        for j in range(0, run, 2):
            a, b, c = entry[j][j], entry[j][j + 1], entry[j + 1][j + 1]
            scale = 1.0 / (a * c - b * b)
            at_first, at_second = column == first + j, column == first + j + 1
            low = jnp.where(at_first, c, jnp.where(at_second, -b, c * rows[j] - b * rows[j + 1]))
            high = jnp.where(at_first, -b, jnp.where(at_second, a, a * rows[j + 1] - b * rows[j]))
            later = range(j + 2, run)
            low_entry = {k: c * entry[j][k] - b * entry[j + 1][k] for k in later}
            high_entry = {k: a * entry[j + 1][k] - b * entry[j][k] for k in later}
            for i in range(run):
                if i in (j, j + 1):
                    continue
                from_low, from_high = entry[i][j], entry[i][j + 1]
                rows[i] = jnp.where(at_first | at_second, 0.0, rows[i]) - scale * (from_low * low + from_high * high)
                for k in later:
                    if j + 1 < i and k < i:
                        entry[i][k] = entry[k][i]
                    else:
                        entry[i][k] = entry[i][k] - scale * (from_low * low_entry[k] + from_high * high_entry[k])
            rows[j], rows[j + 1] = scale * low, scale * high
            for k in later:
                entry[j][k], entry[j + 1][k] = scale * low_entry[k], scale * high_entry[k]
        pivots = (column >= first) & (column < first + run)
        for r in range(len(blocks)):
            if r != p:
                terms = [columns[r][i] * rows[i] for i in range(run)]
                while len(terms) > 1:
                    terms = [terms[i] + terms[i + 1] for i in range(0, len(terms), 2)]
                blocks[r] = jnp.where(pivots, 0.0, blocks[r]) - terms[0]
        turned = rows[0]
        for i in range(1, run):
            turned = jnp.where(sub == i, rows[i], turned)
        blocks[p] = turned
    return jnp.concatenate(blocks, axis=0)


def inverses_body(total_tokens, factor_a_ref, factor_b_ref, grad_ref, in_ref):
    rank = factor_a_ref.shape[0]
    lane = lax.broadcasted_iota(jnp.int32, (rank, 2 * rank), 1)
    sub = lax.broadcasted_iota(jnp.int32, (rank, 2 * rank), 0)
    left = lane < rank
    column = jnp.where(left, lane, lane - rank)
    diagonal = column == sub
    packed = (factor_a_ref[...] + factor_b_ref[...]) / total_tokens
    on_diagonal = jnp.sum(jnp.where(diagonal, packed, 0.0), axis=0, keepdims=True)
    trace_in = jnp.sum(jnp.where(left[:1], on_diagonal, 0.0), axis=1, keepdims=True)
    trace_grad = jnp.sum(jnp.where(left[:1], 0.0, on_diagonal), axis=1, keepdims=True)
    damping = 0.1 * jnp.where(left[:1], trace_in, trace_grad) / rank + 1e-06
    packed = packed + jnp.where(diagonal, damping, 0.0)
    packed = invert(packed)
    twice = pltpu.roll(packed, rank, 1)
    grad_ref[0], grad_ref[1] = split(twice[:, :rank])
    in_ref[0, :rank, :], in_ref[1, :rank, :] = split(jnp.where(left, packed, 0.0))
    in_ref[0, rank:, :], in_ref[1, rank:, :] = split(jnp.where(left, 0.0, twice))


def inverses(total_tokens, factor_a, factor_b):
    rank, width = factor_a.shape
    return pl.pallas_call(
        functools.partial(inverses_body, total_tokens),
        out_shape=(
            jax.ShapeDtypeStruct((2, rank, rank), bf16),
            jax.ShapeDtypeStruct((2, width, width), bf16),
        ),
        in_specs=[VMEM, VMEM],
        out_specs=(VMEM, VMEM),
        compiler_params=pltpu.CompilerParams(vmem_limit_bytes=4 * MIB),
        cost_estimate=pl.CostEstimate(flops=16384 * MIB, bytes_accessed=0, transcendentals=0),
        name="inverses",
    )(factor_a, factor_b)


def pack_body(tests_ref, *out_refs):
    feat_count = len(out_refs)
    rows, width = tests_ref.shape
    fold, block = rows // feat_count, width // feat_count
    feat = lax.axis_index("feat")
    pieces = []
    for target in range(feat_count):
        columns = slice(target * block, (target + 1) * block)
        parts = [tests_ref[j * fold : (j + 1) * fold, columns] for j in range(feat_count)]
        pieces.append(jnp.concatenate(parts, axis=1))
    for mask, out_ref in enumerate(out_refs):
        piece = pieces[0]
        for target in range(1, feat_count):
            piece = jnp.where((feat ^ mask) == target, pieces[target], piece)
        out_ref[...] = piece


def pack(tests, flops):
    rows, width = tests.shape
    feat_count = lax.axis_size("feat")
    return pl.pallas_call(
        pack_body,
        out_shape=[jax.ShapeDtypeStruct((rows // feat_count, width), bf16)] * feat_count,
        in_specs=[VMEM],
        out_specs=[VMEM] * feat_count,
        compiler_params=pltpu.CompilerParams(vmem_limit_bytes=8 * MIB),
        cost_estimate=pl.CostEstimate(flops=flops, bytes_accessed=4 * MIB, transcendentals=0),
        name="pack",
    )(tests)


def scores_body(blocks, piece_counts, grad_ref, in_ref, *refs):
    feat_count = lax.axis_size("feat")
    feat = lax.axis_index("feat")
    counts, pieces = piece_counts, []
    for count in counts:
        rows = refs[0].shape[0] // count
        pieces += [refs[0].at[pl.ds(rows * i, rows), :] for i in range(count)]
        refs = refs[1:]
    feats_refs, out_refs, (solved_buf, line_buf) = refs[:blocks], refs[blocks : 2 * blocks], refs[2 * blocks :]
    rank = grad_ref.shape[1]
    pairs = [ref[i] for ref in feats_refs for i in range(ref.shape[0])]
    count = len(pairs)
    half = count // blocks
    fold, width = pieces[0].shape
    block = width // feat_count
    dot = functools.partial(jnp.dot, preferred_element_type=f32)
    both = dot(jnp.concatenate([grad_ref[0], grad_ref[1]], axis=0), jnp.concatenate(pairs, axis=1))
    solved = both[:rank, :] + both[rank:, :]
    rows = [solved[:, 2 * rank * at : 2 * rank * (at + 1)] for at in range(count)]
    high, low = split(jnp.concatenate(rows, axis=0))
    both = dot(high, jnp.concatenate([in_ref[0], in_ref[1]], axis=1))
    solved_buf[...] = both[:, : 2 * rank] + both[:, 2 * rank :] + dot(low, in_ref[0])
    lane = lax.broadcasted_iota(jnp.int32, (count, 2 * rank), 1)
    for g in range(0, rank, 2):
        low = solved_buf[pl.ds(g, count, stride=rank), :]
        high = solved_buf[pl.ds(g + 1, count, stride=rank), :]
        first = jnp.where(lane < rank, low, pltpu.roll(high, rank, 1))
        second = jnp.where(lane < rank, pltpu.roll(low, rank, 1), high)
        line = jnp.concatenate([first, second], axis=0)
        step = min(fold, 2 * rank)
        for begin in range(0, 2 * rank, step):
            at = (g * rank + begin) // fold
            to = (g * rank + begin) % fold
            line_buf[at // feat_count, at % feat_count, :, to : to + step] = line[:, begin : begin + step]
    lines = []
    for mask in range(feat_count):
        owner = feat ^ mask
        lines.append(jnp.concatenate([line_buf[owner, j] for j in range(feat_count)], axis=0).astype(bf16))
    is_first = lax.axis_index("test") == 0
    odd = lax.rem(lax.axis_index("dp"), 2)
    for dp_bit in range(2):
        parts = []
        for test_bit in range(2):
            at = (2 * dp_bit + test_bit) * feat_count
            total = dot(lines[0], pieces[at][...])
            for mask in range(1, feat_count):
                total = total + dot(lines[mask], pieces[at + mask][...])
            part = total[: 2 * count, :block]
            for j in range(1, feat_count):
                part = part + total[2 * count * j : 2 * count * (j + 1), block * j : block * (j + 1)]
            parts.append(part)
        both = jnp.concatenate(
            [jnp.where(is_first, parts[0], parts[1]), jnp.where(is_first, parts[1], parts[0])], axis=1
        )
        for at, out_ref in enumerate(out_refs):
            out_ref[odd ^ dp_bit, :half, :] = both[at * half : (at + 1) * half, :]
            out_ref[odd ^ dp_bit, half:, :] = both[count + at * half : count + (at + 1) * half, :]


def scores_of(grad, in_pair, pieces, piece_counts, feats):
    feat_count = lax.axis_size("feat")
    rank = grad.shape[1]
    fold, width = pieces[0].shape[0] // piece_counts[0], pieces[0].shape[1]
    half = feats[0].shape[0]
    count = half * len(feats)
    return pl.pallas_call(
        functools.partial(scores_body, len(feats), piece_counts),
        out_shape=[jax.ShapeDtypeStruct((2, 2 * half, 2 * width // feat_count), f32)] * len(feats),
        in_specs=[VMEM] * (2 + len(pieces) + len(feats)),
        out_specs=[VMEM] * len(feats),
        scratch_shapes=[
            pltpu.VMEM((count * rank, 2 * rank), f32),
            pltpu.VMEM((feat_count, feat_count, 2 * count, fold), f32),
        ],
        compiler_params=pltpu.CompilerParams(vmem_limit_bytes=16 * MIB),
        name="scores",
    )(grad, in_pair, *pieces, *feats)


def finish_body(*refs):
    block_refs, out_ref = refs[:-1], refs[-1]
    count = len(block_refs)
    _, examples, width = block_refs[0].shape
    half = width // 2
    own = lax.div(lax.axis_index("dp"), 2)
    for place in range(count):
        for odd in range(2):
            block = block_refs[0][odd]
            for mask in range(1, count):
                block = jnp.where((own ^ mask) == place, block_refs[mask][odd], block)
            for test in range(2):
                rows = pl.ds(4 * place + 2 * odd + test, examples, stride=4 * count)
                out_ref[rows, :] = block[:, test * half : (test + 1) * half]


def finish(blocks):
    _, examples, width = blocks[0].shape
    queries = 4 * len(blocks)
    out = pl.pallas_call(
        finish_body,
        out_shape=jax.ShapeDtypeStruct((examples * queries, width // 2), f32),
        in_specs=[VMEM] * len(blocks),
        out_specs=VMEM,
        compiler_params=pltpu.CompilerParams(vmem_limit_bytes=4 * MIB),
        name="finish",
    )(*blocks)
    return out.reshape(examples, queries, width // 2)


def after(values, *others):
    return lax.optimization_barrier((values, *others))[0]


def on_device(train_inputs, train_grads, proj_in, proj_out, lengths, loss_mask, test_feats):
    examples, seq_len, in_width = train_inputs.shape
    out_width = train_grads.shape[2]
    tokens = examples * seq_len
    feat_count = lax.axis_size("feat")
    dp_count = lax.axis_size("dp")
    test_count = lax.axis_size("test")
    own_rows = test_feats.shape[1]
    x = train_inputs.reshape(tokens, in_width)
    g = train_grads.reshape(tokens, out_width)
    tests = test_feats.transpose(1, 2, 0).reshape(own_rows * test_feats.shape[2], test_feats.shape[0])
    positions = slots(seq_len)
    far_tests = xor_permute(tests, "dp", 1)
    own, sent = project(x, g, after(proj_in.T, positions), proj_out.T, tokens // 3)
    cut = pack(after(tests, sent), 4 * MIB)
    near = [cut[0]] + [xor_permute(cut[mask], "feat", mask) for mask in range(1, feat_count)]
    received = [xor_permute(sent, "feat", mask) for mask in range(1, feat_count)]
    slot_numbers = jnp.arange(seq_len, dtype=jnp.int32)
    live = ((loss_mask > 0) & (slot_numbers[None, :] < lengths[:, None])).astype(f32).reshape(1, tokens)
    cut = pack(after(far_tests, sent, live), 4 * MIB)
    far = [cut[0]] + [xor_permute(cut[mask], "feat", mask) for mask in range(1, feat_count)]
    factor, rounded = factors(live, own, received)
    feats = [features_of(lengths, positions, loss_mask, rounded)]
    even_masks = range(2, dp_count, 2)
    steps = [("dp", m) for m in masks_of(dp_count)] + [("test", 1)]
    sums = [factor]
    for axis, mask in steps:
        if len(sums) == 3:
            sums[-1] = after(sums[-1], feats[0])
        other = xor_permute(sums[-1], axis, mask)
        sums.append(sums[-1] + other)
    pieces, piece_counts = [], []
    pieces += near + [xor_permute(piece, "test", 1) for piece in after(tuple(near), *(sums[2],))]
    piece_counts += [1] * (2 * feat_count)
    pieces += far + [xor_permute(jnp.concatenate(after(tuple(far), *(sums[2],)), axis=0), "test", 1)]
    piece_counts += [1] * feat_count + [feat_count]
    feats += [xor_permute(feats[0], "dp", mask) for mask in even_masks]
    total_tokens = float(tokens * dp_count * test_count)
    grad, in_pair = inverses(total_tokens, sums[-2], other)
    blocks = scores_of(grad, in_pair, pieces, piece_counts, feats[1:])
    blocks = [xor_permute(block, "dp", mask) for block, mask in zip(blocks, even_masks)]
    blocks = [*scores_of(grad, in_pair, pieces, piece_counts, feats[:1]), *blocks]
    return finish(blocks)


def solution(mesh):
    return jax.shard_map(
        on_device,
        mesh=mesh,
        in_specs=(
            P(("groups", "dp", "test"), None, "feat"),
            P(("groups", "dp", "test"), None, "feat"),
            P("feat", None),
            P("feat", None),
            P(("groups", "dp", "test")),
            P(("groups", "dp", "test"), None),
            P(("groups", "dp", "test"), "feat", None),
        ),
        out_specs=P(("groups", "dp", "test"), None, "feat"),
        check_vma=False,
    )
```
